32 devices in a mesh: ctx: 8 (over z, x), fsdp: 4 (over y, core).
Axes of the slice: x: 2, y: 2, z: 4, core: 2. Of those that a mesh axis runs over, the one named last changes fastest.
Arguments:
- tokens: bfloat16 [4, 1024, 2048], P('fsdp', 'ctx'), may hold values from -6 to 6
- cotangent: bfloat16 [4, 1024, 2048], P('fsdp', 'ctx'), may hold values from -6 to 6
- lengths: int32 [4, 3], P('fsdp'), may hold values from 1 to 512, 1024 in all within a row
- deal: int32 [4, 8, 8], P('fsdp'), may hold values from 0 to 7, each once within a row
- norm1_gain: float32 [2048], P('fsdp'), may hold values from 0.1 to 1.9
- w_qkv: float32 [2048, 6144], P('fsdp'), may hold values from -0.125 to 0.125
- w_out: float32 [2048, 2048], P('fsdp'), may hold values from -2 to 2
- norm2_gain: float32 [2048], P('fsdp'), may hold values from 0.1 to 1.9
- w_gate_up: float32 [2048, 11008], P('fsdp'), may hold values from -0.125 to 0.125
- w_down: float32 [5504, 2048], P('fsdp'), may hold values from -0.078125 to 0.078125
Outputs:
- block_out: bfloat16 [4, 1024, 2048], P('fsdp', 'ctx')
- grad_tokens: bfloat16 [4, 1024, 2048], P('fsdp', 'ctx')
- grad_norm1: float32 [2048], P('fsdp')
- grad_qkv: float32 [2048, 6144], P('fsdp')
- grad_out: float32 [2048, 2048], P('fsdp')
- grad_norm2: float32 [2048], P('fsdp')
- grad_gate_up: float32 [2048, 11008], P('fsdp')
- grad_down: float32 [5504, 2048], P('fsdp')
The draws below stay inside these ranges and needn't reach their ends.
Inputs may be any that keep to these rules, and one draw needn't show every extreme that they name: `lengths`: the 3 documents of a group fill its 1024 tokens in order; the longest has exactly 512. deal[f, d] lists, for the 16-token pieces of ctx device d of group f in order, the ctx device each piece goes to; each row names every device once.
All inputs are finite; a program needn't handle non-finite values.
Results may differ from the reference program's by a relative error of at most 0.019.
The reference program's roundings to bfloat16 on the way count: a program that leaves them out, or rounds other values in their place, can miss the bound.
Values may be sent and summed in bfloat16 or wider, within the bound.
A program may use at most 512 MiB of HBM per device.

```python
import math
import jax
import jax.numpy as jnp
import numpy as np
from jax import lax

D = 2048
H = 16
HD = 128
FF = 5504
TOK_DEV = 128
NSEQ = 3
PIECE = 16
GROUP = 1024
GROUPS = 4
MOST = 512
N_CTX = 8


def shard_levels(stream_key, extent, cuts, smallest, high):
    def one(axis_at, blocks):
        steps = jax.random.uniform(jax.random.fold_in(jax.random.fold_in(stream_key, 6), axis_at), (blocks,), jnp.float32, smallest / len(cuts), high / len(cuts))
        return jnp.repeat(jnp.exp(steps), extent[axis_at] // blocks).reshape((-1,) + (1,) * (len(extent) - axis_at - 1))

    factor_of = one(*cuts[0])
    for cut in cuts[1:]:
        factor_of = factor_of * one(*cut)
    return factor_of


def profile(count, total, reach, slope):
    weights = [(1 << 20) // math.isqrt(grade ** slope) + 1 for grade in range(2, count + 1)]
    rest, counts = total - reach - (count - 1), [1] * (count - 1)
    while rest > 0:
        candidates = [i for i in range(count - 1) if counts[i] < reach]
        pool, remaining = sum([weights[i] for i in candidates]), rest
        for i in candidates:
            extra = min(reach - counts[i], max(1, remaining * weights[i] // pool), rest)
            counts[i] = counts[i] + extra
            rest = rest - extra
    return np.array([reach] + counts)


def ragged(key, number_of, total, limit, skew):
    if number_of == 2:
        one = jax.random.randint(key, (), max(1, total - limit), min(limit, total - 1) + 1)
        return jnp.stack([one, total - one])
    sizes = jnp.asarray(profile(number_of, total, limit, skew), jnp.int32)
    couples = (number_of - 1) // 2
    source_of, sink = sizes[1:1 + 2 * couples:2], sizes[2:2 + 2 * couples:2]
    margin = jnp.minimum(source_of - 1, limit - sink)
    moved = jax.random.randint(jax.random.fold_in(key, 1), (couples,), 0, 1 << 20) % (margin + 1)
    sizes = sizes.at[1:1 + 2 * couples:2].set(source_of - moved).at[2:2 + 2 * couples:2].set(sink + moved)
    return sizes[jax.random.permutation(jax.random.fold_in(key, 2), number_of)]


def bell_draw(key, extent, spread, reach, pieces=(), kind=jnp.bfloat16):
    loudness = shard_levels(key, extent, pieces, -0.22, 0.18) if pieces else 1.0
    values = jax.random.normal(key, extent, jnp.float32) * spread * loudness
    return jnp.minimum(jnp.maximum(values, -reach), reach).astype(kind)


def setup_inputs(seed: int = 0) -> dict:
    arg_keys = jax.random.split(jax.random.key(seed), 11)
    return {
        "tokens": bell_draw(arg_keys[0], (GROUPS, GROUP, D), 1.0, 6.0, ((0, 4), (1, 8))),
        "cotangent": bell_draw(arg_keys[1], (GROUPS, GROUP, D), 1.0, 6.0, ((0, 4), (1, 8))),
        "lengths": jax.vmap(lambda own: ragged(own, NSEQ, GROUP, MOST, 2))(jax.random.split(arg_keys[2], GROUPS)).reshape((GROUPS, NSEQ)).astype(jnp.int32),
        "deal": jax.vmap(lambda own: jax.random.permutation(own, N_CTX))(jax.random.split(arg_keys[3], GROUPS * N_CTX)).reshape((GROUPS, N_CTX, N_CTX)).astype(jnp.int32),
        "norm1_gain": jnp.clip(1.0 + 0.18 * jax.random.normal(arg_keys[4], (D,), jnp.float32), 0.1, 1.9),
        "w_qkv": bell_draw(arg_keys[5], (D, 3 * D), D ** -0.5, 0.125, ((0, 4),), jnp.float32),
        "w_out": bell_draw(arg_keys[6], (D, D), (max(D // 256, 4)) ** -0.5, 2.0, ((0, 4),), jnp.float32),
        "norm2_gain": jnp.clip(1.0 + 0.18 * jax.random.normal(arg_keys[7], (D,), jnp.float32), 0.1, 1.9),
        "w_gate_up": bell_draw(arg_keys[8], (D, 2 * FF), D ** -0.5, 0.125, ((0, 4),), jnp.float32),
        "w_down": bell_draw(arg_keys[9], (FF, D), FF ** -0.5, 0.078125, ((0, 4),), jnp.float32),
    }


epsilon = 1e-06
rope_base = 10000.0
masked_score = -1e+30
highest = lax.Precision.HIGHEST

@jax.custom_vjp
def low(v):
    return lax.optimization_barrier(v.astype(jnp.bfloat16)).astype(jnp.float32)

@jax.custom_vjp
def low_back(v):
    return v

def low_keep(v):
    return (low(v), None)

def low_pass(kept, grad):
    return (grad,)

def back_keep(v):
    return (v, None)

def back_low(kept, grad):
    return (low(grad),)
low.defvjp(low_keep, low_pass)
low_back.defvjp(back_keep, back_low)

def rope_tables(within):
    freq_index = jnp.arange(HD // 2, dtype=jnp.float32)
    inverse = rope_base ** (-2.0 * freq_index / HD)
    angles = within.astype(jnp.float32)[:, None] * inverse[None, :]
    cosine_table = jnp.concatenate([jnp.cos(angles), jnp.cos(angles)], -1)
    sine_table = jnp.concatenate([jnp.sin(angles), jnp.sin(angles)], -1)
    return (cosine_table, sine_table)

def rotate(values, cosine_table, sine_table):
    half_size = values.shape[-1] // 2
    turned = jnp.concatenate([-values[..., half_size:], values[..., :half_size]], -1)
    return values * cosine_table[:, None, :] + turned * sine_table[:, None, :]

def rms_scale(values):
    return lax.rsqrt(lax.optimization_barrier(jnp.mean(values * values, -1, keepdims=True)) + epsilon)

def layer(norm1_gain, w_qkv, w_out, norm2_gain, w_gate_up, w_down, inputs, within, doc_ids):
    row_count = inputs.shape[0]
    normed_one = low(inputs * rms_scale(inputs) * low(norm1_gain)[None, :])
    projected = low_back(jnp.dot(normed_one, low(w_qkv), precision=highest))
    cosine_table, sine_table = rope_tables(within)
    queries = low(rotate(projected[:, :D].reshape(row_count, H, HD), cosine_table, sine_table))
    keys = low(rotate(projected[:, D:2 * D].reshape(row_count, H, HD), cosine_table, sine_table))
    values = low(projected[:, 2 * D:].reshape(row_count, H, HD))
    places = jnp.arange(row_count, dtype=jnp.int32)
    block_rows = min(512, row_count)
    factor = 1.0 / math.sqrt(HD)

    def attend(block):
        block_queries, block_places, block_docs = block
        logits = low_back(jnp.einsum('qhd,khd->hqk', block_queries, keys, precision=highest))
        allowed = (doc_ids[None, :] == block_docs[:, None]) & (places[None, :] <= block_places[:, None])
        scaled = jnp.where(allowed[None], logits * factor, masked_score)
        row_top = lax.optimization_barrier(jnp.max(scaled, -1, keepdims=True))
        raised = jnp.exp(scaled - row_top)
        probs = raised / lax.optimization_barrier(jnp.sum(raised, -1, keepdims=True))
        return jnp.einsum('hqk,khd->qhd', low(probs), values, precision=highest)
    blocks = row_count // block_rows
    mixed = lax.map(jax.checkpoint(attend), (queries.reshape(blocks, block_rows, H, HD), places.reshape(blocks, block_rows), doc_ids.reshape(blocks, block_rows)))
    mixed = low(low_back(mixed.reshape(row_count, D)))
    hidden = inputs + low_back(jnp.dot(mixed, low(w_out), precision=highest))
    normed_two = low(hidden * rms_scale(hidden) * low(norm2_gain)[None, :])
    both = low_back(jnp.dot(normed_two, low(w_gate_up), precision=highest))
    gate_part = both[:, :FF]
    up_part = both[:, FF:]
    activated = low(jax.nn.silu(gate_part) * up_part)
    return hidden + low_back(jnp.dot(activated, low(w_down), precision=highest))

def deal_slots(deal_table):
    device_index = jnp.arange(N_CTX, dtype=jnp.int32)
    marks = (deal_table[:, :, None] == device_index[None, None, :]).astype(jnp.int32)
    source_piece = lax.optimization_barrier(jnp.sum(marks * device_index[None, :, None], 1)).astype(jnp.int32)
    slots = device_index[None, :, None] * TOK_DEV + jnp.transpose(source_piece)[:, :, None] * PIECE + jnp.arange(PIECE, dtype=jnp.int32)[None, None, :]
    return slots.reshape(GROUP).astype(jnp.int32)

def reference(tokens, cotangent, lengths, deal, norm1_gain, w_qkv, w_out, norm2_gain, w_gate_up, w_down):
    weights = (norm1_gain, w_qkv, w_out, norm2_gain, w_gate_up, w_down)

    def group_step(totals, item):
        group_tokens, group_grad, group_lengths, deal_table = item
        places = jnp.arange(GROUP, dtype=jnp.int32)
        ends = jnp.cumsum(group_lengths).astype(jnp.int32)
        starts = (ends - group_lengths).astype(jnp.int32)
        doc_ids = lax.optimization_barrier(jnp.sum((places[:, None] >= ends[None, :]).astype(jnp.int32), 1)).astype(jnp.int32)
        within = (places - jnp.take(starts, doc_ids)).astype(jnp.int32)
        order = deal_slots(deal_table)

        def forward(gain_one, weight_qkv, weight_out, gain_two, weight_gate_up, weight_down, inputs):
            return layer(gain_one, weight_qkv, weight_out, gain_two, weight_gate_up, weight_down, inputs, within, doc_ids)
        result, pullback = jax.vjp(forward, norm1_gain, w_qkv, w_out, norm2_gain, w_gate_up, w_down, group_tokens.astype(jnp.float32))
        upstream = jnp.zeros((GROUP, D), jnp.float32).at[order].set(group_grad.astype(jnp.float32))
        grads = pullback(upstream)
        totals = jax.tree.map(jnp.add, totals, tuple(grads[:6]))
        return (totals, (jnp.take(result, order, axis=0).astype(jnp.bfloat16), grads[6].astype(jnp.bfloat16)))
    zeros = jax.tree.map(jnp.zeros_like, weights)
    totals, outputs = lax.scan(group_step, zeros, (tokens, cotangent, lengths, deal))
    return (outputs[0], outputs[1], totals[0], totals[1], totals[2], totals[3], totals[4], totals[5])
```

```python
import math

import jax
import jax.numpy as jnp
from jax import lax
from jax.sharding import PartitionSpec as P

H = 16
HD = 128

epsilon = 1e-06
rope_base = 10000.0
masked_score = -1e30
f32 = jnp.float32
bf16 = jnp.bfloat16


def rope_tables(within):
    freq_index = jnp.arange(HD // 2, dtype=f32)
    inverse = rope_base ** (-2.0 * freq_index / HD)
    angles = within.astype(f32)[:, None] * inverse[None, :]
    cosine_table = jnp.concatenate([jnp.cos(angles), jnp.cos(angles)], -1)
    sine_table = jnp.concatenate([jnp.sin(angles), jnp.sin(angles)], -1)
    return (cosine_table, sine_table)


def rotate(values, cosine_table, sine_table):
    half_size = values.shape[-1] // 2
    turned = jnp.concatenate([-values[..., half_size:], values[..., :half_size]], -1)
    return values * cosine_table[:, None, :] + turned * sine_table[:, None, :]


def unrotate(grads, cosine_table, sine_table):
    half_size = grads.shape[-1] // 2
    scaled = grads * sine_table[:, None, :]
    turned = jnp.concatenate([-scaled[..., half_size:], scaled[..., :half_size]], -1)
    return grads * cosine_table[:, None, :] - turned


def rms_scale(values):
    return lax.rsqrt(jnp.mean(values * values, -1, keepdims=True) + epsilon)


def norm_back(grad_norm, values, scale_rows, gain_float):
    scaled = grad_norm * gain_float[None, :]
    cubed = scale_rows * scale_rows * scale_rows
    return scale_rows * scaled - values * cubed * jnp.mean(scaled * values, -1, keepdims=True)


def dot(a, b, dims):
    return lax.dot_general(a, b, (dims, ((), ())), preferred_element_type=f32)


NN = ((1,), (0,))
NT = ((1,), (1,))
TN = ((0,), (0,))


def shards(
    tokens, cotangent, lengths, deal, norm1_gain, w_qkv, w_out, norm2_gain, w_gate_up, w_down
):
    n_ctx = lax.axis_size("ctx")
    n_fsdp = lax.axis_size("fsdp")
    me = lax.axis_index("ctx")
    mine = lax.axis_index("fsdp")
    rows = tokens.shape[1]
    width = tokens.shape[2]
    piece = rows // n_ctx
    all_rows = rows * n_ctx
    pieces = all_rows // piece
    heads = H // n_ctx
    hw = heads * HD
    kr = w_qkv.shape[0]
    ff = w_gate_up.shape[1] // 2
    ffs = ff // n_ctx
    ff_rows = w_down.shape[0]
    ratio = n_ctx // n_fsdp

    x_own = tokens[0]
    x_all = lax.all_gather(x_own, "ctx", axis=0, tiled=True)

    qkv_own = lax.dynamic_slice(w_qkv.reshape(kr, 3, width), (0, 0, me * hw), (kr, 3, hw))
    wq = lax.all_gather(qkv_own.reshape(kr, 3 * hw).astype(bf16), "fsdp", axis=0, tiled=True)
    gains = lax.all_gather(
        jnp.stack([norm1_gain, norm2_gain]).astype(bf16), "fsdp", axis=1, tiled=True
    )
    gain_one = gains[0].astype(f32)
    gain_two = gains[1].astype(f32)
    wo = lax.all_gather(w_out.astype(bf16), "fsdp", axis=0, tiled=True)
    wg_own = jnp.concatenate(
        [
            lax.dynamic_slice(w_gate_up, (0, me * ffs), (kr, ffs)),
            lax.dynamic_slice(w_gate_up, (0, ff + me * ffs), (kr, ffs)),
        ],
        -1,
    ).astype(bf16)
    wgu = lax.all_gather(wg_own, "fsdp", axis=0, tiled=True)
    down_own = lax.dynamic_slice(w_down, ((me % ratio) * ffs, 0), (ffs, width)).astype(bf16)
    wd = lax.psum(jnp.where(mine == me // ratio, down_own, jnp.zeros_like(down_own)), "fsdp")
    g_all = lax.all_gather(cotangent[0], "ctx", axis=0, tiled=True)

    deal_table = deal[0]
    device_index = jnp.arange(n_ctx, dtype=jnp.int32)
    marks = (deal_table[:, :, None] == device_index[None, None, :]).astype(jnp.int32)
    source_piece = jnp.sum(marks * device_index[None, :, None], 1)
    dealt_from = (device_index[None, :] * n_ctx + source_piece.T).reshape(pieces)
    given_from = (deal_table * n_ctx + device_index[:, None]).reshape(pieces)
    own_dealt = lax.dynamic_slice(dealt_from, (me * n_ctx,), (n_ctx,))
    own_given = lax.dynamic_slice(given_from, (me * n_ctx,), (n_ctx,))
    places = jnp.arange(all_rows, dtype=jnp.int32)
    doc_lengths = lengths[0]
    ends = jnp.cumsum(doc_lengths)
    starts = ends - doc_lengths
    docs = jnp.sum((places[:, None] >= ends[None, :]).astype(jnp.int32), -1)
    doc_index = jnp.arange(doc_lengths.shape[0], dtype=jnp.int32)
    firsts = jnp.sum(jnp.where(docs[:, None] == doc_index[None, :], starts[None, :], 0), -1)
    within = places - firsts
    allowed = (docs[None, :] == docs[:, None]) & (places[None, :] <= places[:, None])
    cosine_table, sine_table = rope_tables(within)
    factor = 1.0 / math.sqrt(HD)

    x_float = x_all.astype(f32)
    normed_one = (x_float * rms_scale(x_float) * gain_one[None, :]).astype(bf16)
    projected = dot(normed_one, wq, NN)
    queries = rotate(projected[:, :hw].reshape(all_rows, heads, HD), cosine_table, sine_table)
    queries = queries.astype(bf16)
    keys = rotate(projected[:, hw : 2 * hw].reshape(all_rows, heads, HD), cosine_table, sine_table)
    keys = keys.astype(bf16)
    values = projected[:, 2 * hw :].astype(bf16).reshape(all_rows, heads, HD)
    logits = jnp.einsum("qhd,khd->hqk", queries, keys, preferred_element_type=f32)
    scaled = jnp.where(allowed[None], logits * factor, masked_score)
    row_top = jnp.max(scaled, -1, keepdims=True)
    raised = jnp.exp(scaled - row_top)
    row_total = jnp.sum(raised, -1, keepdims=True)
    probs = raised / row_total
    probs_low = probs.astype(bf16)
    mixed = jnp.einsum("hqk,khd->qhd", probs_low, values, preferred_element_type=f32)
    mixed = mixed.astype(bf16).reshape(pieces, piece, hw)
    mixed_dealt = jnp.take(mixed, dealt_from, axis=0)
    mixed_own = lax.all_to_all(
        mixed_dealt.reshape(n_ctx, rows, hw), "ctx", split_axis=0, concat_axis=2, tiled=True
    ).reshape(rows, width)
    mixed_dealt = mixed_dealt.reshape(all_rows, hw)

    x_dealt = jnp.take(x_all.reshape(pieces, piece, width), own_dealt, axis=0)
    hidden = x_dealt.reshape(rows, width).astype(f32) + dot(mixed_own, wo, NN)
    scale_two = rms_scale(hidden)
    normed_two = (hidden * scale_two * gain_two[None, :]).astype(bf16)
    n2_all = lax.all_gather(normed_two, "ctx", axis=0, tiled=True)

    both = dot(n2_all, wgu, NN)
    gate = both[:, :ffs]
    up = both[:, ffs:]
    sigma = jax.nn.sigmoid(gate)
    gate_act = gate * sigma
    activated = (gate_act * up).astype(bf16)
    down_part = dot(activated, wd, NN).astype(bf16)
    down_own_rows = lax.psum_scatter(down_part, "ctx", scatter_dimension=0, tiled=True)
    block_out = (hidden + down_own_rows.astype(f32)).astype(bf16)[None]

    d_act = dot(g_all, wd, NT)
    d_both = jnp.concatenate(
        [d_act * up * sigma * (1.0 + gate * (1.0 - sigma)), d_act * gate_act], -1
    ).astype(bf16)
    d_two_part = dot(d_both, wgu, NT).astype(bf16)
    d_two = lax.psum_scatter(d_two_part, "ctx", scatter_dimension=0, tiled=True).astype(f32)
    grad_down = dot(activated, g_all, TN).astype(bf16)
    grad_gate_up = dot(n2_all, d_both, TN).astype(bf16)
    row_gate_up = lax.psum_scatter(grad_gate_up, "fsdp", scatter_dimension=0, tiled=True)
    all_gate_up = lax.all_gather(row_gate_up, "ctx", axis=0)
    final_gate_up = (
        all_gate_up.reshape(n_ctx, kr, 2, ffs).transpose(1, 2, 0, 3).reshape(kr, 2 * ff).astype(f32)
    )

    grad_norm2 = jnp.sum(d_two * hidden * scale_two, 0)
    d_hidden = cotangent[0].astype(f32) + norm_back(d_two, hidden, scale_two, gain_two)
    d_branch = d_hidden.astype(bf16)
    db_all = lax.all_gather(d_branch, "ctx", axis=0, tiled=True)

    grad_out = dot(mixed_dealt, db_all, TN).astype(bf16)
    wo_own = lax.dynamic_slice(wo, (me * hw, 0), (hw, width))
    d_mixed = dot(db_all, wo_own, NT).astype(bf16)
    d_mixed = jnp.take(d_mixed.reshape(pieces, piece, hw), given_from, axis=0)
    d_mixed = d_mixed.reshape(all_rows, heads, HD)
    d_probs = jnp.einsum("qhd,khd->hqk", d_mixed, values, preferred_element_type=f32)
    row_inner = jnp.sum(probs * d_probs, -1, keepdims=True)
    d_scores = (probs * (d_probs - row_inner) * factor).astype(bf16)
    d_queries = jnp.einsum("hqk,khd->qhd", d_scores, keys, preferred_element_type=f32)
    d_keys = jnp.einsum("hqk,qhd->khd", d_scores, queries, preferred_element_type=f32)
    d_values = jnp.einsum("hqk,qhd->khd", probs_low, d_mixed, preferred_element_type=f32)
    d_proj = jnp.concatenate(
        [
            unrotate(d_queries, cosine_table, sine_table).reshape(all_rows, hw),
            unrotate(d_keys, cosine_table, sine_table).reshape(all_rows, hw),
            d_values.reshape(all_rows, hw),
        ],
        -1,
    ).astype(bf16)
    d_one_part = dot(d_proj, wq, NT).astype(bf16)
    d_one = lax.psum_scatter(d_one_part, "ctx", scatter_dimension=0, tiled=True).astype(f32)
    grad_qkv = dot(normed_one, d_proj, TN).astype(bf16)
    row_qkv = lax.psum_scatter(grad_qkv, "fsdp", scatter_dimension=0, tiled=True)
    all_qkv = lax.all_gather(row_qkv, "ctx", axis=0)
    final_qkv = (
        all_qkv.reshape(n_ctx, kr, 3, hw).transpose(1, 2, 0, 3).reshape(kr, 3 * width).astype(f32)
    )

    own_float = x_own.astype(f32)
    scale_one = rms_scale(own_float)
    grad_norm1 = jnp.sum(d_one * own_float * scale_one, 0)
    dh_own = jnp.take(db_all.reshape(pieces, piece, width), own_given, axis=0)
    dh_own = dh_own.reshape(rows, width).astype(f32)
    grad_tokens = (dh_own + norm_back(d_one, own_float, scale_one, gain_one)).astype(bf16)[None]

    grad_rows = jnp.concatenate([grad_down, grad_out], 0)
    col_rows = lax.psum_scatter(grad_rows, "fsdp", scatter_dimension=1, tiled=True)
    all_cols = lax.all_gather(col_rows, "ctx", axis=0)
    owner_rows = all_cols.reshape(n_fsdp, ratio * (ffs + hw), width // n_fsdp)
    swapped = lax.all_to_all(owner_rows, "fsdp", split_axis=0, concat_axis=2, tiled=True)
    swapped = swapped.reshape(ratio, ffs + hw, width)
    final_down = swapped[:, :ffs].reshape(ff_rows, width).astype(f32)
    final_out = swapped[:, ffs:].reshape(ratio * hw, width).astype(f32)

    sums = lax.psum(jnp.stack([grad_norm1, grad_norm2]), ("ctx", "fsdp"))
    gain_rows = norm1_gain.shape[0]
    final_norms = lax.dynamic_slice_in_dim(sums, mine * gain_rows, gain_rows, 1)
    return (
        block_out,
        grad_tokens,
        final_norms[0],
        final_qkv,
        final_out,
        final_norms[1],
        final_gate_up,
        final_down,
    )


def solution(mesh):
    in_specs = (
        P("fsdp", "ctx", None),
        P("fsdp", "ctx", None),
        P("fsdp", None),
        P("fsdp", None, None),
        P("fsdp"),
        P("fsdp", None),
        P("fsdp", None),
        P("fsdp"),
        P("fsdp", None),
        P("fsdp", None),
    )
    out_specs = (
        P("fsdp", "ctx", None),
        P("fsdp", "ctx", None),
        P("fsdp"),
        P("fsdp", None),
        P("fsdp", None),
        P("fsdp"),
        P("fsdp", None),
        P("fsdp", None),
    )
    return jax.shard_map(shards, mesh=mesh, in_specs=in_specs, out_specs=out_specs, check_vma=False)
```

```python
import functools
import math

import jax
import jax.numpy as jnp
from jax import lax
from jax.experimental import pallas as pl
from jax.experimental.pallas import tpu as pltpu
from jax.sharding import PartitionSpec as P

MESH = pl.DeviceIdType.MESH
LINE = 4

H = 16
HD = 128

epsilon = 1e-06
rope_base = 10000.0
masked_score = -1e30
f32 = jnp.float32
bf16 = jnp.bfloat16


def greet(a, b, A, B, f):
    bar = pltpu.get_barrier_semaphore()
    conds = ((a > 0, a - 1, b), (a < A - 1, a + 1, b), (b > 0, a, b - 1), (b < B - 1, a, b + 1))
    for cond, aa, bb in conds:

        @pl.when(cond)
        def _():
            pl.semaphore_signal(bar, inc=1, device_id=(aa * B + bb, f), device_id_type=MESH)

    low = (a + A - 1) // A + (b + B - 1) // B
    high = (2 * A - 2 - a) // A + (2 * B - 2 - b) // B
    pl.semaphore_wait(bar, low + high)


def ag_kernel(n, q, x_ref, out_ref, lsem, sa, ra, sb, rb):
    A = LINE
    B = n // A
    c = lax.axis_index("ctx")
    f = lax.axis_index("fsdp")
    a = c // B
    b = c % B
    rows = x_ref.shape[0]
    cr = rows // q

    def dev(aa, bb):
        return (aa * B + bb, f)

    left, right = a > 0, a < A - 1
    low, high = b > 0, b < B - 1
    greet(a, b, A, B, f)

    def src(s, bb, i, own):
        if own:
            return x_ref.at[pl.ds(i * cr, cr)]
        return out_ref.at[s * B + bb, pl.ds(i * cr, cr)]

    def copy_a(k, d, i, own=False):
        s = a - k if d == 0 else a + k
        to = a + 1 if d == 0 else a - 1
        return pltpu.make_async_remote_copy(
            src_ref=src(s, b, i, own), dst_ref=out_ref.at[s * B + b, pl.ds(i * cr, cr)],
            send_sem=sa.at[d, k, i], recv_sem=ra.at[d, k, i], device_id=dev(to, b), device_id_type=MESH)

    def copy_b(j, s, m, d, i, own=False):
        bb = b - m if d == 0 else b + m
        to = b + 1 if d == 0 else b - 1
        return pltpu.make_async_remote_copy(
            src_ref=src(s, bb, i, own), dst_ref=out_ref.at[s * B + bb, pl.ds(i * cr, cr)],
            send_sem=sb.at[d, m, j, i], recv_sem=rb.at[d, m, j, i], device_id=dev(a, to), device_id_type=MESH)

    lst = [(0, 0, None)]
    for k in range(1, A):
        lst += [(k, k, 0), (A - 1 + k, k, 1)]

    def valid(k, side):
        if side is None:
            return True
        return (a >= k) if side == 0 else (a + k < A)

    def when(cond):
        if cond is True:
            return lambda fn: fn()
        return pl.when(cond)

    local = pltpu.make_async_copy(x_ref, out_ref.at[c], lsem)
    for i in range(q):
        @pl.when(right)
        def _():
            copy_a(0, 0, i, True).start()
        @pl.when(left)
        def _():
            copy_a(0, 1, i, True).start()
        @pl.when(high)
        def _():
            copy_b(0, a, 0, 0, i, True).start()
        @pl.when(low)
        def _():
            copy_b(0, a, 0, 1, i, True).start()
    local.start()
    for j, k, side in lst[1:]:
        s = a - k if side == 0 else a + k
        for i in range(q):
            @pl.when(valid(k, side))
            def _():
                copy_a(k - 1, side, i).wait_recv()
                if k < A - 1:
                    onward = right if side == 0 else left
                    @pl.when(onward)
                    def _():
                        copy_a(k, side, i).start()
                @pl.when(high)
                def _():
                    copy_b(j, s, 0, 0, i).start()
                @pl.when(low)
                def _():
                    copy_b(j, s, 0, 1, i).start()
    for m in range(1, B):
        for d, has, on in ((0, b >= m, high), (1, b + m < B, low)):
            for j, k, side in lst:
                s = a if side is None else (a - k if side == 0 else a + k)
                for i in range(q):
                    @pl.when(has if side is None else has & valid(k, side))
                    def _():
                        copy_b(j, s, m - 1, d, i).wait_recv()
                        if m < B - 1:
                            @pl.when(on)
                            def _():
                                copy_b(j, s, m, d, i).start()
    local.wait()
    for j, k, side in lst:
        s = a if side is None else (a - k if side == 0 else a + k)
        for i in range(q):
            for d, cond in ((0, right), (1, left)):
                if k == A - 1 or (side is not None and d != side):
                    continue
                @pl.when(cond if side is None else cond & valid(k, side))
                def _():
                    copy_a(k, d, i, side is None).wait_send()
            for m in range(B - 1):
                for d, on, has in ((0, high, b >= m), (1, low, b + m < B)):
                    @pl.when(on & has if side is None else on & has & valid(k, side))
                    def _():
                        copy_b(j, s, m, d, i, side is None and m == 0).wait_send()


def all_gather_ctx(x, n, q=1, cid=0):
    A, B = LINE, n // LINE
    return pl.pallas_call(
        functools.partial(ag_kernel, n, q),
        out_shape=jax.ShapeDtypeStruct((n,) + x.shape, x.dtype),
        in_specs=[pl.BlockSpec(memory_space=pl.ANY)],
        out_specs=pl.BlockSpec(memory_space=pl.ANY),
        scratch_shapes=[
            pltpu.SemaphoreType.DMA,
            pltpu.SemaphoreType.DMA((2, A, q)), pltpu.SemaphoreType.DMA((2, A, q)),
            pltpu.SemaphoreType.DMA((2, B, 2 * A - 1, q)), pltpu.SemaphoreType.DMA((2, B, 2 * A - 1, q)),
        ],
        compiler_params=pltpu.CompilerParams(collective_id=cid, has_side_effects=True),
        name=f"ag{cid}",
    )(x)


def rs_kernel(n, q, x_ref, o_ref, part, rb, ra, sbs, sbr, sas, sar, lsem):
    A = LINE
    B = n // A
    c = lax.axis_index("ctx")
    f = lax.axis_index("fsdp")
    a = c // B
    b = c % B
    rows = o_ref.shape[0]
    cr = rows // q
    h = a // 2
    slots = (3 - 3 * h, 2 - h, 1 - a + 4 * h, a)

    def ds(i):
        return pl.ds(i * cr, cr)

    def add(t, got):
        r = part.at[t]
        r[...] = (r[...].astype(jnp.float32) + got[...].astype(jnp.float32)).astype(r.dtype)

    def copy_b(j, d, k, i):
        s = slots[j]
        t = b + k if d == 0 else b - k
        to = b + 1 if d == 0 else b - 1
        return pltpu.make_async_remote_copy(
            src_ref=part.at[s * B + t, ds(i)], dst_ref=rb.at[d, k - 1, j, ds(i)],
            send_sem=sbs.at[d, k, j, i], recv_sem=sbr.at[d, k - 1, j, i],
            device_id=(a * B + to, f), device_id_type=MESH)

    def come_b(j, d, k, i):
        return pltpu.make_async_remote_copy(
            src_ref=part.at[c, ds(i)], dst_ref=rb.at[d, k, j, ds(i)],
            send_sem=sbs.at[d, k, j, i], recv_sem=sbr.at[d, k, j, i],
            device_id=(c, f), device_id_type=MESH)

    def copy_a(t, d, i):
        k = t - a if d == 0 else a - t
        to = a + 1 if d == 0 else a - 1
        return pltpu.make_async_remote_copy(
            src_ref=part.at[t * B + b, ds(i)], dst_ref=ra.at[d, k - 1, ds(i)],
            send_sem=sas.at[d, k, i], recv_sem=sar.at[d, k - 1, i],
            device_id=(to * B + b, f), device_id_type=MESH)

    def come_a(d, k, i):
        return pltpu.make_async_remote_copy(
            src_ref=part.at[c, ds(i)], dst_ref=ra.at[d, k, ds(i)],
            send_sem=sas.at[d, k, i], recv_sem=sar.at[d, k, i],
            device_id=(c, f), device_id_type=MESH)

    def has_b(d, k):
        return (b + k < B) if d == 0 else (b >= k)

    load = pltpu.make_async_copy(x_ref, part, lsem)
    load.start()
    greet(a, b, A, B, f)
    load.wait()
    from_b = (b > 0, b < B - 1)
    from_a = (a > 0, a < A - 1)
    for j in range(A):
        for i in range(q):
            for d in (0, 1):
                for k in range(B - 1, 0, -1):
                    @pl.when(jnp.logical_and(has_b(d, k), jnp.logical_not(from_b[d])))
                    def _():
                        copy_b(j, d, k, i).start()
    for j in range(A):
        s = slots[j]
        for i in range(q):
            for k in range(B - 1, 0, -1):
                for d in (0, 1):
                    if k < B - 1:
                        @pl.when(jnp.logical_and(has_b(d, k), from_b[d]))
                        def _():
                            come_b(j, d, k, i).wait_recv()
                            add((s * B + (b + k if d == 0 else b - k), ds(i)), rb.at[d, k, j, ds(i)])
                            copy_b(j, d, k, i).start()
            for d in (0, 1):
                @pl.when(from_b[d])
                def _():
                    come_b(j, d, 0, i).wait_recv()
                    add((s * B + b, ds(i)), rb.at[d, 0, j, ds(i)])
            if j < A - 1:
                for d in (0, 1):
                    @pl.when((s > a) if d == 0 else (s < a))
                    def _():
                        @pl.when(from_a[d])
                        def _():
                            k = s - a if d == 0 else a - s
                            come_a(d, k, i).wait_recv()
                            add((s * B + b, ds(i)), ra.at[d, k, ds(i)])
                        copy_a(s, d, i).start()
    for i in range(q):
        for d in (0, 1):
            @pl.when(from_a[d])
            def _():
                come_a(d, 0, i).wait_recv()
                add((c, ds(i)), ra.at[d, 0, ds(i)])
    o_ref[...] = part[c]
    for j in range(A):
        for i in range(q):
            for d in (0, 1):
                for k in range(B - 1, 0, -1):
                    @pl.when(has_b(d, k))
                    def _():
                        copy_b(j, d, k, i).wait_send()
                if j < A - 1:
                    @pl.when((slots[j] > a) if d == 0 else (slots[j] < a))
                    def _():
                        copy_a(slots[j], d, i).wait_send()


def reduce_scatter_ctx(x, n, q=1, cid=0):
    A, B = LINE, n // LINE
    rows = x.shape[0] // n
    w = x.shape[1]
    return pl.pallas_call(
        functools.partial(rs_kernel, n, q),
        out_shape=jax.ShapeDtypeStruct((rows, w), x.dtype),
        in_specs=[pl.BlockSpec(memory_space=pl.ANY)],
        out_specs=pl.BlockSpec(memory_space=pltpu.VMEM),
        scratch_shapes=[
            pltpu.VMEM((n, rows, w), x.dtype),
            pltpu.VMEM((2, B - 1, A, rows, w), x.dtype),
            pltpu.VMEM((2, A - 1, rows, w), x.dtype),
            pltpu.SemaphoreType.DMA((2, B, A, q)), pltpu.SemaphoreType.DMA((2, B, A, q)),
            pltpu.SemaphoreType.DMA((2, A, q)), pltpu.SemaphoreType.DMA((2, A, q)),
            pltpu.SemaphoreType.DMA,
        ],
        compiler_params=pltpu.CompilerParams(collective_id=cid, has_side_effects=True, vmem_limit_bytes=60 << 20),
        name=f"rs{cid}",
    )(x.reshape(n, rows, w))


def assemble(parts, n_groups, block=64):
    n, rows, gw = parts.shape
    w = gw // n_groups

    def body(i_ref, o_ref):
        for g in range(n_groups):
            for c in range(n):
                o_ref[:, (g * n + c) * w:(g * n + c + 1) * w] = i_ref[c, :, g * w:(g + 1) * w].astype(jnp.float32)

    return pl.pallas_call(
        body, grid=(rows // block,),
        out_shape=jax.ShapeDtypeStruct((rows, n * gw), jnp.float32),
        in_specs=[pl.BlockSpec((n, block, gw), lambda i: (0, i, 0))],
        out_specs=pl.BlockSpec((block, n * gw), lambda i: (i, 0)),
        compiler_params=pltpu.CompilerParams(vmem_limit_bytes=60 << 20),
        name="assemble")(parts)


def rope_tables(within):
    freq_index = jnp.arange(HD // 2, dtype=f32)
    inverse = rope_base ** (-2.0 * freq_index / HD)
    angles = within.astype(f32)[:, None] * inverse[None, :]
    cosine_table = jnp.concatenate([jnp.cos(angles), jnp.cos(angles)], -1)
    sine_table = jnp.concatenate([jnp.sin(angles), jnp.sin(angles)], -1)
    return (cosine_table, sine_table)


def rotate(values, cosine_table, sine_table):
    half_size = values.shape[-1] // 2
    turned = jnp.concatenate([-values[..., half_size:], values[..., :half_size]], -1)
    return values * cosine_table[:, None, :] + turned * sine_table[:, None, :]


def unrotate(grads, cosine_table, sine_table):
    half_size = grads.shape[-1] // 2
    scaled = grads * sine_table[:, None, :]
    turned = jnp.concatenate([-scaled[..., half_size:], scaled[..., :half_size]], -1)
    return grads * cosine_table[:, None, :] - turned


def rms_scale(values):
    return lax.rsqrt(jnp.mean(values * values, -1, keepdims=True) + epsilon)


def norm_back(grad_norm, values, scale_rows, gain_float):
    scaled = grad_norm * gain_float[None, :]
    cubed = scale_rows * scale_rows * scale_rows
    return scale_rows * scaled - values * cubed * jnp.mean(scaled * values, -1, keepdims=True)


def dot(a, b, dims):
    return lax.dot_general(a, b, (dims, ((), ())), preferred_element_type=f32)


NN = ((1,), (0,))
NT = ((1,), (1,))
TN = ((0,), (0,))


def shards(
    tokens, cotangent, lengths, deal, norm1_gain, w_qkv, w_out, norm2_gain, w_gate_up, w_down
):
    n_ctx = lax.axis_size("ctx")
    n_fsdp = lax.axis_size("fsdp")
    me = lax.axis_index("ctx")
    mine = lax.axis_index("fsdp")
    rows = tokens.shape[1]
    width = tokens.shape[2]
    piece = rows // n_ctx
    all_rows = rows * n_ctx
    pieces = all_rows // piece
    heads = H // n_ctx
    hw = heads * HD
    kr = w_qkv.shape[0]
    ff = w_gate_up.shape[1] // 2
    ffs = ff // n_ctx
    ff_rows = w_down.shape[0]
    ratio = n_ctx // n_fsdp

    x_own = tokens[0]
    x_all = all_gather_ctx(x_own, n_ctx, 2, 0).reshape(all_rows, width)

    qkv_own = lax.dynamic_slice(w_qkv.reshape(kr, 3, width), (0, 0, me * hw), (kr, 3, hw))
    wq = lax.all_gather(qkv_own.reshape(kr, 3 * hw).astype(bf16), "fsdp", axis=0, tiled=True)
    gains = lax.all_gather(
        jnp.stack([norm1_gain, norm2_gain]).astype(bf16), "fsdp", axis=1, tiled=True
    )
    gain_one = gains[0].astype(f32)
    gain_two = gains[1].astype(f32)
    wo = lax.all_gather(w_out.astype(bf16), "fsdp", axis=0, tiled=True)
    wg_own = jnp.concatenate(
        [
            lax.dynamic_slice(w_gate_up, (0, me * ffs), (kr, ffs)),
            lax.dynamic_slice(w_gate_up, (0, ff + me * ffs), (kr, ffs)),
        ],
        -1,
    ).astype(bf16)
    wgu = lax.all_gather(wg_own, "fsdp", axis=0, tiled=True)
    down_own = lax.dynamic_slice(w_down, ((me % ratio) * ffs, 0), (ffs, width)).astype(bf16)
    wd = lax.psum(jnp.where(mine == me // ratio, down_own, jnp.zeros_like(down_own)), "fsdp")
    g_all = all_gather_ctx(cotangent[0], n_ctx, 2, 1).reshape(all_rows, width)

    deal_table = deal[0]
    device_index = jnp.arange(n_ctx, dtype=jnp.int32)
    marks = (deal_table[:, :, None] == device_index[None, None, :]).astype(jnp.int32)
    source_piece = jnp.sum(marks * device_index[None, :, None], 1)
    dealt_from = (device_index[None, :] * n_ctx + source_piece.T).reshape(pieces)
    given_from = (deal_table * n_ctx + device_index[:, None]).reshape(pieces)
    own_dealt = lax.dynamic_slice(dealt_from, (me * n_ctx,), (n_ctx,))
    own_given = lax.dynamic_slice(given_from, (me * n_ctx,), (n_ctx,))
    places = jnp.arange(all_rows, dtype=jnp.int32)
    doc_lengths = lengths[0]
    ends = jnp.cumsum(doc_lengths)
    starts = ends - doc_lengths
    docs = jnp.sum((places[:, None] >= ends[None, :]).astype(jnp.int32), -1)
    doc_index = jnp.arange(doc_lengths.shape[0], dtype=jnp.int32)
    firsts = jnp.sum(jnp.where(docs[:, None] == doc_index[None, :], starts[None, :], 0), -1)
    within = places - firsts
    allowed = (docs[None, :] == docs[:, None]) & (places[None, :] <= places[:, None])
    cosine_table, sine_table = rope_tables(within)
    factor = 1.0 / math.sqrt(HD)

    x_float = x_all.astype(f32)
    normed_one = (x_float * rms_scale(x_float) * gain_one[None, :]).astype(bf16)
    projected = dot(normed_one, wq, NN)
    queries = rotate(projected[:, :hw].reshape(all_rows, heads, HD), cosine_table, sine_table)
    queries = queries.astype(bf16)
    keys = rotate(projected[:, hw : 2 * hw].reshape(all_rows, heads, HD), cosine_table, sine_table)
    keys = keys.astype(bf16)
    values = projected[:, 2 * hw :].astype(bf16).reshape(all_rows, heads, HD)
    logits = jnp.einsum("qhd,khd->hqk", queries, keys, preferred_element_type=f32)
    scaled = jnp.where(allowed[None], logits * factor, masked_score)
    row_top = jnp.max(scaled, -1, keepdims=True)
    raised = jnp.exp(scaled - row_top)
    row_total = jnp.sum(raised, -1, keepdims=True)
    probs = raised / row_total
    probs_low = probs.astype(bf16)
    mixed = jnp.einsum("hqk,khd->qhd", probs_low, values, preferred_element_type=f32)
    mixed = mixed.astype(bf16).reshape(pieces, piece, hw)
    mixed_dealt = jnp.take(mixed, dealt_from, axis=0)
    mixed_own = lax.all_to_all(
        mixed_dealt.reshape(n_ctx, rows, hw), "ctx", split_axis=0, concat_axis=2, tiled=True
    ).reshape(rows, width)
    mixed_dealt = mixed_dealt.reshape(all_rows, hw)

    x_dealt = jnp.take(x_all.reshape(pieces, piece, width), own_dealt, axis=0)
    hidden = x_dealt.reshape(rows, width).astype(f32) + dot(mixed_own, wo, NN)
    scale_two = rms_scale(hidden)
    normed_two = (hidden * scale_two * gain_two[None, :]).astype(bf16)
    n2_all = all_gather_ctx(normed_two, n_ctx, 2, 2).reshape(all_rows, width)

    both = dot(n2_all, wgu, NN)
    gate = both[:, :ffs]
    up = both[:, ffs:]
    sigma = jax.nn.sigmoid(gate)
    gate_act = gate * sigma
    activated = (gate_act * up).astype(bf16)
    down_part = dot(activated, wd, NN).astype(bf16)
    down_own_rows = reduce_scatter_ctx(down_part, n_ctx, 2, 4)
    block_out = (hidden + down_own_rows.astype(f32)).astype(bf16)[None]

    d_act = dot(g_all, wd, NT)
    d_both = jnp.concatenate(
        [d_act * up * sigma * (1.0 + gate * (1.0 - sigma)), d_act * gate_act], -1
    ).astype(bf16)
    d_two_part = dot(d_both, wgu, NT).astype(bf16)
    d_two = reduce_scatter_ctx(d_two_part, n_ctx, 2, 5).astype(f32)
    grad_down = dot(activated, g_all, TN).astype(bf16)
    grad_gate_up = dot(n2_all, d_both, TN).astype(bf16)
    row_gate_up = lax.psum_scatter(grad_gate_up, "fsdp", scatter_dimension=0, tiled=True)
    all_gate_up = all_gather_ctx(row_gate_up, n_ctx, 2, 7)
    final_gate_up = assemble(all_gate_up, 2)

    grad_norm2 = jnp.sum(d_two * hidden * scale_two, 0)
    d_hidden = cotangent[0].astype(f32) + norm_back(d_two, hidden, scale_two, gain_two)
    d_branch = d_hidden.astype(bf16)
    db_all = all_gather_ctx(d_branch, n_ctx, 2, 3).reshape(all_rows, width)

    grad_out = dot(mixed_dealt, db_all, TN).astype(bf16)
    wo_own = lax.dynamic_slice(wo, (me * hw, 0), (hw, width))
    d_mixed = dot(db_all, wo_own, NT).astype(bf16)
    d_mixed = jnp.take(d_mixed.reshape(pieces, piece, hw), given_from, axis=0)
    d_mixed = d_mixed.reshape(all_rows, heads, HD)
    d_probs = jnp.einsum("qhd,khd->hqk", d_mixed, values, preferred_element_type=f32)
    row_inner = jnp.sum(probs * d_probs, -1, keepdims=True)
    d_scores = (probs * (d_probs - row_inner) * factor).astype(bf16)
    d_queries = jnp.einsum("hqk,khd->qhd", d_scores, keys, preferred_element_type=f32)
    d_keys = jnp.einsum("hqk,qhd->khd", d_scores, queries, preferred_element_type=f32)
    d_values = jnp.einsum("hqk,qhd->khd", probs_low, d_mixed, preferred_element_type=f32)
    d_proj = jnp.concatenate(
        [
            unrotate(d_queries, cosine_table, sine_table).reshape(all_rows, hw),
            unrotate(d_keys, cosine_table, sine_table).reshape(all_rows, hw),
            d_values.reshape(all_rows, hw),
        ],
        -1,
    ).astype(bf16)
    d_one_part = dot(d_proj, wq, NT).astype(bf16)
    d_one = reduce_scatter_ctx(d_one_part, n_ctx, 2, 6).astype(f32)
    grad_qkv = dot(normed_one, d_proj, TN).astype(bf16)
    row_qkv = lax.psum_scatter(grad_qkv, "fsdp", scatter_dimension=0, tiled=True)
    all_qkv = all_gather_ctx(row_qkv, n_ctx, 2, 8)
    final_qkv = assemble(all_qkv, 3)

    own_float = x_own.astype(f32)
    scale_one = rms_scale(own_float)
    grad_norm1 = jnp.sum(d_one * own_float * scale_one, 0)
    dh_own = jnp.take(db_all.reshape(pieces, piece, width), own_given, axis=0)
    dh_own = dh_own.reshape(rows, width).astype(f32)
    grad_tokens = (dh_own + norm_back(d_one, own_float, scale_one, gain_one)).astype(bf16)[None]

    grad_rows = jnp.concatenate([grad_down, grad_out], 0)
    col_rows = lax.psum_scatter(grad_rows, "fsdp", scatter_dimension=1, tiled=True)
    all_cols = all_gather_ctx(col_rows, n_ctx, 1, 9)
    owner_rows = all_cols.reshape(n_fsdp, ratio * (ffs + hw), width // n_fsdp)
    swapped = lax.all_to_all(owner_rows, "fsdp", split_axis=0, concat_axis=2, tiled=True)
    swapped = swapped.reshape(ratio, ffs + hw, width)
    final_down = swapped[:, :ffs].reshape(ff_rows, width).astype(f32)
    final_out = swapped[:, ffs:].reshape(ratio * hw, width).astype(f32)

    sums = lax.psum(jnp.stack([grad_norm1, grad_norm2]), ("ctx", "fsdp"))
    gain_rows = norm1_gain.shape[0]
    final_norms = lax.dynamic_slice_in_dim(sums, mine * gain_rows, gain_rows, 1)
    return (
        block_out,
        grad_tokens,
        final_norms[0],
        final_qkv,
        final_out,
        final_norms[1],
        final_gate_up,
        final_down,
    )


def solution(mesh):
    in_specs = (
        P("fsdp", "ctx", None),
        P("fsdp", "ctx", None),
        P("fsdp", None),
        P("fsdp", None, None),
        P("fsdp"),
        P("fsdp", None),
        P("fsdp", None),
        P("fsdp"),
        P("fsdp", None),
        P("fsdp", None),
    )
    out_specs = (
        P("fsdp", "ctx", None),
        P("fsdp", "ctx", None),
        P("fsdp"),
        P("fsdp", None),
        P("fsdp", None),
        P("fsdp"),
        P("fsdp", None),
        P("fsdp", None),
    )
    return jax.shard_map(shards, mesh=mesh, in_specs=in_specs, out_specs=out_specs, check_vma=False)
```

```python
import functools
import math

import jax
import jax.numpy as jnp
from jax import lax
from jax.experimental import pallas as pl
from jax.experimental.pallas import tpu as pltpu
from jax.sharding import PartitionSpec as P

MESH = pl.DeviceIdType.MESH
LINE = 4

H = 16
HD = 128

epsilon = 1e-06
rope_base = 10000.0
masked_score = -1e30
f32 = jnp.float32
bf16 = jnp.bfloat16


def greet(a, b, n_a, n_b, f, fsdp=False):
    bar = pltpu.get_barrier_semaphore()
    conds = ((a > 0, a - 1, b), (a < n_a - 1, a + 1, b), (b > 0, a, b - 1), (b < n_b - 1, a, b + 1))
    for cond, aa, bb in conds:

        @pl.when(cond)
        def _():
            pl.semaphore_signal(bar, inc=1, device_id=(aa * n_b + bb, f), device_id_type=MESH)

    low = (a + n_a - 1) // n_a + (b + n_b - 1) // n_b
    high = (2 * n_a - 2 - a) // n_a + (2 * n_b - 2 - b) // n_b
    total = low + high
    if fsdp:
        n_y = lax.axis_size("fsdp") // 2
        y, core = f // 2, f % 2
        for cond, to in ((y > 0, f - 2), (y < n_y - 1, f + 2), (True, f + 1 - 2 * core)):
            when(cond)(
                lambda to=to: pl.semaphore_signal(
                    bar, inc=1, device_id=(a * n_b + b, to), device_id_type=MESH
                )
            )
        total = total + 1 + (y + n_y - 1) // n_y + (2 * n_y - 2 - y) // n_y
    pl.semaphore_wait(bar, total)


def both(*conds):
    out = True
    for cond in conds:
        if cond is not True:
            out = cond if out is True else jnp.logical_and(out, cond)
    return out


def when(cond):
    return (lambda fn: fn()) if cond is True else pl.when(cond)


def plan(rows, cuts=2):
    unit = rows // 16
    if rows % 16 or unit < 4:
        return ((0, rows, False),)
    swapped = max(1, (unit + 4) // 8)
    rest = unit - swapped
    marks = [rest * i // cuts for i in range(cuts + 1)]
    chunks = [(16 * lo, 16 * (hi - lo), False) for lo, hi in zip(marks, marks[1:])]
    return tuple(chunks) + ((16 * rest, 16 * swapped, True),)


def places(n):
    n_a, n_b = LINE, n // LINE
    c = lax.axis_index("ctx")
    return n_a, n_b, c // n_b, c % n_b, lax.axis_index("fsdp")


def gather_steps(n, x, out, chunk, sems):
    n_a, n_b, a, b, f = places(n)
    first, count, swapped = chunk
    s1, r1, s2, r2 = sems
    (p1, n1), (p2, n2) = ((b, n_b), (a, n_a)) if swapped else ((a, n_a), (b, n_b))

    def slot(q1, q2):
        return q2 * n_b + q1 if swapped else q1 * n_b + q2

    rows = pl.ds(first, count)
    below1, above1, below2, above2 = p1 > 0, p1 < n1 - 1, p2 > 0, p2 < n2 - 1

    def copy1(k, d):
        q1 = p1 - k if d == 0 else p1 + k
        to = p1 + 1 if d == 0 else p1 - 1
        return pltpu.make_async_remote_copy(
            src_ref=x.at[rows] if k == 0 else out.at[slot(q1, p2), rows],
            dst_ref=out.at[slot(q1, p2), rows],
            send_sem=s1.at[d, k],
            recv_sem=r1.at[d, k],
            device_id=(slot(to, p2), f),
            device_id_type=MESH,
        )

    def copy2(j, q1, m, d):
        q2 = p2 - m if d == 0 else p2 + m
        to = p2 + 1 if d == 0 else p2 - 1
        return pltpu.make_async_remote_copy(
            src_ref=x.at[rows] if j == 0 and m == 0 else out.at[slot(q1, q2), rows],
            dst_ref=out.at[slot(q1, q2), rows],
            send_sem=s2.at[d, m, j],
            recv_sem=r2.at[d, m, j],
            device_id=(slot(p1, to), f),
            device_id_type=MESH,
        )

    shards = [(0, 0, None, p1, True)]
    for k in range(1, n1):
        shards.append((k, k, 0, p1 - k, p1 >= k))
        shards.append((n1 - 1 + k, k, 1, p1 + k, p1 + k < n1))

    def own():
        for d, cond in ((0, above1), (1, below1)):
            when(cond)(lambda d=d: copy1(0, d).start())
        for d, cond in ((0, above2), (1, below2)):
            when(cond)(lambda d=d: copy2(0, p1, 0, d).start())

    def line1(k):
        for j, kk, side, q1, there in shards:
            if kk != k:
                continue

            @when(there)
            def _():
                copy1(k - 1, side).wait_recv()
                if k < n1 - 1:
                    when(above1 if side == 0 else below1)(lambda: copy1(k, side).start())
                for d, cond in ((0, above2), (1, below2)):
                    when(cond)(lambda d=d: copy2(j, q1, 0, d).start())

    def line2(m):
        for d, there2, onward in ((0, p2 >= m, above2), (1, p2 + m < n2, below2)):
            for j, _, _, q1, there in shards:

                @when(both(there2, there))
                def _():
                    copy2(j, q1, m - 1, d).wait_recv()
                    if m < n2 - 1:
                        when(onward)(lambda: copy2(j, q1, m, d).start())

    def finish():
        for j, k, side, q1, there in shards:
            for d, onward in ((0, above1), (1, below1)):
                if k < n1 - 1 and side in (None, d):
                    when(both(onward, there))(lambda d=d: copy1(k, d).wait_send())
            for m in range(n2 - 1):
                for d, onward, there2 in ((0, above2, p2 >= m), (1, below2, p2 + m < n2)):
                    when(both(onward, there, True if m == 0 else there2))(
                        lambda d=d, m=m: copy2(j, q1, m, d).wait_send()
                    )

    steps = [own]
    steps += [functools.partial(line1, k) for k in range(1, n1)]
    steps += [functools.partial(line2, m) for m in range(1, n2)]
    return steps, finish


def spread_steps(n, x, out, chunk, sems):
    f = lax.axis_index("fsdp")
    c = lax.axis_index("ctx")
    n_f = lax.axis_size("fsdp")
    n_y = n_f // 2
    y, core = f // 2, f % 2
    owner = c // (n // n_f)
    oy, oc = owner // 2, owner % 2
    first, count = chunk
    rows = pl.ds(first, count)
    up, down, side, come = sems

    def copy(own, sem, to):
        return pltpu.make_async_remote_copy(
            src_ref=x.at[rows] if own else out.at[rows],
            dst_ref=out.at[rows],
            send_sem=sem,
            recv_sem=come,
            device_id=(c, to),
            device_id_type=MESH,
        )

    on = core == oc
    ways = (
        (up, f + 2, jnp.logical_and(on, jnp.logical_and(y >= oy, y < n_y - 1))),
        (down, f - 2, jnp.logical_and(on, jnp.logical_and(y <= oy, y > 0))),
        (side, f + 1 - 2 * core, on),
    )

    def own():
        for sem, to, cond in ways:
            pl.when(jnp.logical_and(cond, f == owner))(lambda sem=sem, to=to: copy(True, sem, to).start())

    def onward():
        @pl.when(f != owner)
        def _():
            copy(False, side, f).wait_recv()
            for sem, to, cond in ways:
                pl.when(cond)(lambda sem=sem, to=to: copy(False, sem, to).start())

    def finish():
        for sem, to, cond in ways:
            pl.when(cond)(lambda sem=sem, to=to: copy(False, sem, to).wait_send())

    return own, onward, finish


def gather_sems(chunks):
    sem = pltpu.SemaphoreType.DMA
    return [sem((chunks, 2, 4)), sem((chunks, 2, 4)), sem((chunks, 2, 4, 7)), sem((chunks, 2, 4, 7))]


def gather_kernel(n, plans, spread, *refs):
    count = len(plans)
    k = count + (1 if spread else 0)
    xs, outs = refs[:k], refs[k : 2 * k]
    held = refs[2 * k : 3 * k]
    local, s1, r1, s2, r2, s3 = refs[3 * k :]
    n_a, n_b, a, b, f = places(n)
    c = a * n_b + b
    greet(a, b, n_a, n_b, f, bool(spread))
    steps, ends, at = [], [], 0
    for x, out, chunks in zip(xs, outs, plans):
        for chunk in chunks:
            sems = (s1.at[at], r1.at[at], s2.at[at], r2.at[at])
            more, end = gather_steps(n, x, out, chunk, sems)
            steps.append(more)
            ends.append(end)
            at += 1
    for i, chunk in enumerate(spread):
        begin, onward, end = spread_steps(n, xs[-1], outs[-1], chunk, [s3.at[i, j] for j in range(4)])
        steps.append([begin] + [lambda: None] * (1 + 2 * i) + [onward])
        ends.append(end)
    mine = f == c // (n // lax.axis_size("fsdp"))
    for t in range(max(map(len, steps))):
        for more in steps:
            if t < len(more):
                more[t]()
        if t < 2:
            for i in range(k):
                out = outs[i].at[c] if i < count else outs[i]

                @when(True if i < count else mine)
                def _():
                    fetch = pltpu.make_async_copy(xs[i], held[i], local.at[i])
                    if t == 0:
                        fetch.start()
                    else:
                        fetch.wait()
                        pltpu.make_async_copy(held[i], out, local.at[i]).start()
    for i in range(k):
        out = outs[i].at[c] if i < count else outs[i]
        when(True if i < count else mine)(pltpu.make_async_copy(held[i], out, local.at[i]).wait)
    for end in ends:
        end()


def gather_ctx(xs, n, cid, cuts=2, spread=None):
    plans = tuple(plan(x.shape[0], cuts) for x in xs)
    shapes = [jax.ShapeDtypeStruct((n,) + x.shape, x.dtype) for x in xs]
    parts = ()
    if spread is not None:
        rows = spread.shape[0]
        half = rows // 32 * 16
        parts = ((0, rows),) if rows % 16 else ((0, half), (half, rows - half))
        xs = xs + [spread]
        shapes = shapes + [jax.ShapeDtypeStruct(spread.shape, spread.dtype)]
    return pl.pallas_call(
        functools.partial(gather_kernel, n, plans, parts),
        out_shape=shapes,
        in_specs=[pl.BlockSpec(memory_space=pl.ANY)] * len(xs),
        out_specs=[pl.BlockSpec(memory_space=pl.ANY)] * len(xs),
        scratch_shapes=[pltpu.VMEM(x.shape, x.dtype) for x in xs]
        + [pltpu.SemaphoreType.DMA((len(xs),))]
        + gather_sems(sum(map(len, plans)))
        + [pltpu.SemaphoreType.DMA((2, 4))],
        compiler_params=pltpu.CompilerParams(
            collective_id=cid, has_side_effects=True, vmem_limit_bytes=60 << 20
        ),
        name=f"gather{cid}",
    )(*xs)


def order_of(p, n):
    if n == 2:
        return (1 - p, p)
    h = p // 2
    return (3 - 3 * h, 2 - h, 1 - p + 4 * h, p)


def reduce_steps(n, part, chunk, bufs, sems):
    n_a, n_b, a, b, f = places(n)
    first, count, swapped = chunk
    g1, g2 = bufs
    s1, r1, s2, r2 = sems
    (p1, n1), (p2, n2) = ((a, n_a), (b, n_b)) if swapped else ((b, n_b), (a, n_a))

    def slot(q1, q2):
        return q1 * n_b + q2 if swapped else q2 * n_b + q1

    rows = pl.ds(first, count)
    from1 = (p1 > 0, p1 < n1 - 1)
    from2 = (p2 > 0, p2 < n2 - 1)
    targets = order_of(p2, n2)

    def has1(d, k):
        return (p1 + k < n1) if d == 0 else (p1 >= k)

    def add(t, got):
        mine = part.at[t, rows]
        mine[...] = (mine[...].astype(f32) + got[...].astype(f32)).astype(mine.dtype)

    def remote(src, dst, send, recv, to):
        return pltpu.make_async_remote_copy(
            src_ref=src, dst_ref=dst, send_sem=send, recv_sem=recv, device_id=(to, f), device_id_type=MESH
        )

    def copy1(j, d, k):
        t = p1 + k if d == 0 else p1 - k
        to = p1 + 1 if d == 0 else p1 - 1
        src = part.at[slot(t, targets[j]), rows]
        return remote(src, g1.at[d, k - 1, j], s1.at[d, k, j], r1.at[d, k - 1, j], slot(to, p2))

    def come1(j, d, k):
        src = part.at[slot(p1, p2), rows]
        return remote(src, g1.at[d, k, j], s1.at[d, k, j], r1.at[d, k, j], slot(p1, p2))

    def copy2(t, d):
        k = t - p2 if d == 0 else p2 - t
        to = p2 + 1 if d == 0 else p2 - 1
        return remote(
            part.at[slot(p1, t), rows], g2.at[d, k - 1], s2.at[d, k], r2.at[d, k - 1], slot(p1, to)
        )

    def come2(d, k):
        src = part.at[slot(p1, p2), rows]
        return remote(src, g2.at[d, k], s2.at[d, k], r2.at[d, k], slot(p1, p2))

    def start(j):
        for d in (0, 1) if j < n2 else ():
            for k in range(n1 - 1, 0, -1):
                when(both(has1(d, k), jnp.logical_not(from1[d])))(
                    lambda d=d, k=k: copy1(j, d, k).start()
                )

    def middle1(j, k):
        for d in (0, 1):

            @when(both(has1(d, k), from1[d]))
            def _():
                come1(j, d, k).wait_recv()
                add(slot(p1 + k if d == 0 else p1 - k, targets[j]), g1.at[d, k, j])
                copy1(j, d, k).start()

    def last1(j):
        for d in (0, 1):

            @when(from1[d])
            def _():
                come1(j, d, 0).wait_recv()
                add(slot(p1, targets[j]), g1.at[d, 0, j])

    def line2(j):
        t = targets[j]
        for d in (0, 1):

            @when((t > p2) if d == 0 else (t < p2))
            def _():
                @when(from2[d])
                def _():
                    k = t - p2 if d == 0 else p2 - t
                    come2(d, k).wait_recv()
                    add(slot(p1, t), g2.at[d, k])

                copy2(t, d).start()

    def last2():
        for d in (0, 1):

            @when(from2[d])
            def _():
                come2(d, 0).wait_recv()
                add(slot(p1, p2), g2.at[d, 0])

    steps = []
    if swapped:
        for k in range(n1 - 2, 0, -1):
            steps.append(lambda k=k: [middle1(j, k) for j in range(n2)])
        steps.append(lambda: [(last1(j), line2(j) if j < n2 - 1 else None) for j in range(n2)])
        steps.append(last2)
    else:

        def item(j):
            for k in range(n1 - 2, 0, -1):
                middle1(j, k)
            last1(j)
            if j < n2 - 1:
                line2(j)

        steps += [functools.partial(item, j) for j in range(n2)] + [last2]

    def finish():
        for j in range(n2):
            for d in (0, 1):
                for k in range(n1 - 1, 0, -1):
                    when(has1(d, k))(lambda j=j, d=d, k=k: copy1(j, d, k).wait_send())
                if j < n2 - 1:
                    t = targets[j]
                    when((t > p2) if d == 0 else (t < p2))(lambda t=t, d=d: copy2(t, d).wait_send())

    return start, steps, finish


def reduce_kernel(n, chunks, nt, x_ref, w_ref, o_ref, part, *refs):
    n_a, n_b, a, b, f = places(n)
    count = len(chunks)
    rows = o_ref.shape[0]
    bufs = [refs[2 * i : 2 * i + 2] for i in range(count)]
    s1, r1, s2, r2 = refs[2 * count :]
    todo = [
        reduce_steps(n, part, chunk, bufs[i], (s1.at[i], r1.at[i], s2.at[i], r2.at[i]))
        for i, chunk in enumerate(chunks)
    ]

    def term(t):
        at = pl.multiple_of(t * rows, rows)
        part[t] = dot(x_ref[pl.ds(at, rows), :], w_ref[...], NT if nt else NN).astype(part.dtype)

    order = order_of(a, n_a)
    greet(a, b, n_a, n_b, f)
    for j in range(n_a):
        for i in range(1, n_b):
            term(order[j] * n_b + (b + i) % n_b)
        for start, _, _ in todo:
            start(j)
    for j in range(n_a):
        term(order[j] * n_b + b)
        for _, steps, _ in todo:
            steps[j]()
    for _, steps, _ in todo:
        steps[n_a]()
    o_ref[...] = part[a * n_b + b]
    for _, _, finish in todo:
        finish()


def reduce_ctx(x, w, n, cid, nt):
    n_a, n_b = LINE, n // LINE
    rows = x.shape[0] // n
    width = w.shape[0] if nt else w.shape[1]
    half = rows // 2
    chunks = ((0, half, False), (half, half, False))
    bufs = []
    for _, count, _ in chunks:
        bufs += [pltpu.VMEM((2, n_b - 1, n_a, count, width), bf16), pltpu.VMEM((2, n_a - 1, count, width), bf16)]
    sem = pltpu.SemaphoreType.DMA
    k = len(chunks)
    return pl.pallas_call(
        functools.partial(reduce_kernel, n, chunks, nt),
        out_shape=jax.ShapeDtypeStruct((rows, width), bf16),
        in_specs=[pl.BlockSpec(memory_space=pltpu.VMEM)] * 2,
        out_specs=pl.BlockSpec(memory_space=pltpu.VMEM),
        scratch_shapes=[pltpu.VMEM((n, rows, width), bf16)] + bufs
        + [sem((k, 2, 4, 4)), sem((k, 2, 4, 4)), sem((k, 2, 4)), sem((k, 2, 4))],
        compiler_params=pltpu.CompilerParams(
            collective_id=cid, has_side_effects=True, vmem_limit_bytes=60 << 20
        ),
        name=f"reduce{cid}",
    )(x, w)


def assemble_rows(parts, ratio, ffs):
    n, rows, w = parts.shape
    each = rows // ratio
    hw = each - ffs

    def body(i_ref, down_ref, out_ref):
        for j in range(ratio):
            down_ref[j * ffs : (j + 1) * ffs, :] = i_ref[0, j * each : j * each + ffs, :].astype(f32)
            out_ref[j * hw : (j + 1) * hw, :] = i_ref[0, j * each + ffs : (j + 1) * each, :].astype(f32)

    return pl.pallas_call(
        body,
        grid=(n,),
        out_shape=[
            jax.ShapeDtypeStruct((ratio * ffs, n * w), f32),
            jax.ShapeDtypeStruct((ratio * hw, n * w), f32),
        ],
        in_specs=[pl.BlockSpec((1, rows, w), lambda i: (i, 0, 0))],
        out_specs=[
            pl.BlockSpec((ratio * ffs, w), lambda i: (0, i)),
            pl.BlockSpec((ratio * hw, w), lambda i: (0, i)),
        ],
        compiler_params=pltpu.CompilerParams(vmem_limit_bytes=60 << 20),
        name="assemble_rows",
    )(parts)


def assemble(parts, n_groups, block=64):
    n, rows, gw = parts.shape
    w = gw // n_groups

    def body(i_ref, o_ref):
        for g in range(n_groups):
            for c in range(n):
                o_ref[:, (g * n + c) * w:(g * n + c + 1) * w] = i_ref[c, :, g * w:(g + 1) * w].astype(jnp.float32)

    return pl.pallas_call(
        body, grid=(rows // block,),
        out_shape=jax.ShapeDtypeStruct((rows, n * gw), jnp.float32),
        in_specs=[pl.BlockSpec((n, block, gw), lambda i: (0, i, 0))],
        out_specs=pl.BlockSpec((block, n * gw), lambda i: (i, 0)),
        compiler_params=pltpu.CompilerParams(vmem_limit_bytes=60 << 20),
        name="assemble")(parts)


def dot(a, b, dims):
    return lax.dot_general(a, b, (dims, ((), ())), preferred_element_type=f32)


NN = ((1,), (0,))
NT = ((1,), (1,))
TN = ((0,), (0,))


def turned(u):
    return pltpu.roll(u, HD // 2, 1)


def masked_probs(q, k, first, at):
    logits = dot(q, k, NT) * (1.0 / math.sqrt(HD))
    keys = lax.broadcasted_iota(jnp.int32, logits.shape, 1)
    queries = lax.broadcasted_iota(jnp.int32, logits.shape, 0) + at
    scaled = jnp.where((keys <= queries) & (keys >= first), logits, masked_score)
    raised = jnp.exp(scaled - jnp.max(scaled, -1, keepdims=True))
    return raised / jnp.sum(raised, -1, keepdims=True)


def attend_kernel(heads, block, n_ref, w_ref, cos_ref, sin_ref, first_ref, q_ref, k_ref, v_ref, o_ref):
    rows = n_ref.shape[0]
    hw = heads * HD
    for at in range(0, rows, block):
        own = slice(at, at + block)
        proj = dot(n_ref[own, :], w_ref[...], NN)
        cos, sin = cos_ref[own, :], sin_ref[own, :]
        for h in range(heads):
            head = slice(h * HD, (h + 1) * HD)
            for ref, base in ((q_ref, 0), (k_ref, hw)):
                u = proj[:, base + h * HD : base + (h + 1) * HD]
                ref[own, head] = (u * cos + turned(u) * sin).astype(bf16)
        v_ref[own, :] = proj[:, 2 * hw :].astype(bf16)
        for h in range(heads):
            head = slice(h * HD, (h + 1) * HD)
            seen = slice(0, at + block)
            probs = masked_probs(q_ref[own, head], k_ref[seen, head], first_ref[own, :], at)
            o_ref[own, head] = dot(probs.astype(bf16), v_ref[seen, head], NN).astype(bf16)


def attend(normed, wq, cos, sin, first, heads, block=256):
    rows = normed.shape[0]
    one = jax.ShapeDtypeStruct((rows, heads * HD), bf16)
    return pl.pallas_call(
        functools.partial(attend_kernel, heads, block),
        out_shape=[one] * 4,
        compiler_params=pltpu.CompilerParams(vmem_limit_bytes=60 << 20),
        name="attend",
    )(normed, wq, cos, sin, first)


def attend_back_kernel(
    heads, block, q_ref, k_ref, v_ref, d_ref, cos_ref, sin_ref, first_ref, o_ref, dk_ref, dv_ref
):
    rows = q_ref.shape[0]
    hw = heads * HD

    def back(w, own):
        return (w * cos_ref[own, :] - turned(w) * sin_ref[own, :]).astype(bf16)

    for h in range(heads):
        head = slice(h * HD, (h + 1) * HD)
        for at in reversed(range(0, rows, block)):
            own = slice(at, at + block)
            seen = slice(0, at + block)
            q, k, v, d = q_ref[own, head], k_ref[seen, head], v_ref[seen, head], d_ref[own, head]
            probs = masked_probs(q, k, first_ref[own, :], at)
            d_probs = dot(d, v, NT)
            inner = jnp.sum(probs * d_probs, -1, keepdims=True)
            d_scores = (probs * (d_probs - inner) * (1.0 / math.sqrt(HD))).astype(bf16)
            o_ref[own, head] = back(dot(d_scores, k, NN), own)
            dk = dot(d_scores, q, TN)
            dv = dot(probs.astype(bf16), d, TN)
            if at + block == rows:
                dk_ref[...] = dk
                dv_ref[...] = dv
            else:
                dk_ref[seen, :] += dk
                dv_ref[seen, :] += dv
        every = slice(0, rows)
        o_ref[:, hw + h * HD : hw + (h + 1) * HD] = back(dk_ref[...], every)
        o_ref[:, 2 * hw + h * HD : 2 * hw + (h + 1) * HD] = dv_ref[...].astype(bf16)


def attend_back(q, k, v, d_mixed, cos, sin, first, heads, block=256):
    rows = q.shape[0]
    return pl.pallas_call(
        functools.partial(attend_back_kernel, heads, block),
        out_shape=jax.ShapeDtypeStruct((rows, 3 * heads * HD), bf16),
        scratch_shapes=[pltpu.VMEM((rows, HD), f32), pltpu.VMEM((rows, HD), f32)],
        compiler_params=pltpu.CompilerParams(vmem_limit_bytes=60 << 20),
        name="attend_back",
    )(q, k, v, d_mixed, cos, sin, first)


def rope_tables(within):
    freq_index = jnp.arange(HD // 2, dtype=f32)
    inverse = rope_base ** (-2.0 * freq_index / HD)
    angles = within.astype(f32)[:, None] * inverse[None, :]
    cos, sin = jnp.cos(angles), jnp.sin(angles)
    return jnp.concatenate([cos, cos], -1), jnp.concatenate([-sin, sin], -1)


def rms_scale(values):
    return lax.rsqrt(jnp.mean(values * values, -1, keepdims=True) + epsilon)


def norm_back(grad_norm, values, scale_rows, gain_float):
    scaled = grad_norm * gain_float[None, :]
    cubed = scale_rows * scale_rows * scale_rows
    return scale_rows * scaled - values * cubed * jnp.mean(scaled * values, -1, keepdims=True)


def shards(
    tokens, cotangent, lengths, deal, norm1_gain, w_qkv, w_out, norm2_gain, w_gate_up, w_down
):
    n_ctx = lax.axis_size("ctx")
    n_fsdp = lax.axis_size("fsdp")
    me = lax.axis_index("ctx")
    mine = lax.axis_index("fsdp")
    rows = tokens.shape[1]
    width = tokens.shape[2]
    piece = rows // n_ctx
    all_rows = rows * n_ctx
    pieces = all_rows // piece
    heads = H // n_ctx
    hw = heads * HD
    kr = w_qkv.shape[0]
    ff = w_gate_up.shape[1] // 2
    ffs = ff // n_ctx
    ff_rows = w_down.shape[0]
    ratio = n_ctx // n_fsdp

    x_own = tokens[0]
    x_all = gather_ctx([x_own], n_ctx, 0)[0].reshape(all_rows, width)

    qkv_own = jnp.concatenate(
        [lax.dynamic_slice(w_qkv, (0, i * width + me * hw), (kr, hw)) for i in range(3)], -1
    )
    wq = lax.all_gather(qkv_own.astype(bf16), "fsdp", axis=0, tiled=True)
    gains = lax.all_gather(
        jnp.stack([norm1_gain, norm2_gain]).astype(bf16), "fsdp", axis=1, tiled=True
    )
    gain_one = gains[0].astype(f32)
    gain_two = gains[1].astype(f32)
    wo = lax.all_gather(w_out.astype(bf16), "fsdp", axis=0, tiled=True)
    wg_own = jnp.concatenate(
        [
            lax.dynamic_slice(w_gate_up, (0, me * ffs), (kr, ffs)),
            lax.dynamic_slice(w_gate_up, (0, ff + me * ffs), (kr, ffs)),
        ],
        -1,
    ).astype(bf16)
    wgu = lax.all_gather(wg_own, "fsdp", axis=0, tiled=True)
    down_own = lax.dynamic_slice(w_down, ((me % ratio) * ffs, 0), (ffs, width)).astype(bf16)
    g_all = gather_ctx([cotangent[0]], n_ctx, 1)[0].reshape(all_rows, width)

    deal_table = deal[0]
    device_index = jnp.arange(n_ctx, dtype=jnp.int32)
    marks = (deal_table[:, :, None] == device_index[None, None, :]).astype(jnp.int32)
    source_piece = jnp.sum(marks * device_index[None, :, None], 1)
    dealt_from = (device_index[None, :] * n_ctx + source_piece.T).reshape(pieces)
    given_from = (deal_table * n_ctx + device_index[:, None]).reshape(pieces)
    own_dealt = lax.dynamic_slice(dealt_from, (me * n_ctx,), (n_ctx,))
    own_given = lax.dynamic_slice(given_from, (me * n_ctx,), (n_ctx,))
    places = jnp.arange(all_rows, dtype=jnp.int32)
    doc_lengths = lengths[0]
    ends = jnp.cumsum(doc_lengths)
    starts = ends - doc_lengths
    docs = jnp.sum((places[:, None] >= ends[None, :]).astype(jnp.int32), -1)
    doc_index = jnp.arange(doc_lengths.shape[0], dtype=jnp.int32)
    firsts = jnp.sum(jnp.where(docs[:, None] == doc_index[None, :], starts[None, :], 0), -1)
    within = places - firsts
    first_key = firsts[:, None]
    cosine_table, sine_table = rope_tables(within)

    x_float = x_all.astype(f32)
    normed_one = (x_float * rms_scale(x_float) * gain_one[None, :]).astype(bf16)
    queries, keys, values, mixed = attend(
        normed_one, wq, cosine_table, sine_table, first_key, heads
    )
    mixed = mixed.reshape(pieces, piece, hw)
    mixed_dealt = jnp.take(mixed, dealt_from, axis=0)
    mixed_own = lax.all_to_all(
        mixed_dealt.reshape(n_ctx, rows, hw), "ctx", split_axis=0, concat_axis=2, tiled=True
    ).reshape(rows, width)
    mixed_dealt = mixed_dealt.reshape(all_rows, hw)

    x_dealt = jnp.take(x_all.reshape(pieces, piece, width), own_dealt, axis=0)
    hidden = x_dealt.reshape(rows, width).astype(f32) + dot(mixed_own, wo, NN)
    scale_two = rms_scale(hidden)
    normed_two = (hidden * scale_two * gain_two[None, :]).astype(bf16)
    n2_all, wd = gather_ctx([normed_two], n_ctx, 2, spread=down_own)
    n2_all = n2_all.reshape(all_rows, width)

    both = dot(n2_all, wgu, NN)
    gate = both[:, :ffs]
    up = both[:, ffs:]
    sigma = jax.nn.sigmoid(gate)
    gate_act = gate * sigma
    activated = (gate_act * up).astype(bf16)
    down_own_rows = reduce_ctx(activated, wd, n_ctx, 4, False)
    block_out = (hidden + down_own_rows.astype(f32)).astype(bf16)[None]

    d_act = dot(g_all, wd, NT)
    d_both = jnp.concatenate(
        [d_act * up * sigma * (1.0 + gate * (1.0 - sigma)), d_act * gate_act], -1
    ).astype(bf16)
    d_two = reduce_ctx(d_both, wgu, n_ctx, 5, True).astype(f32)
    grad_down = dot(activated, g_all, TN).astype(bf16)
    grad_gate_up = dot(n2_all, d_both, TN).astype(bf16)
    row_gate_up = lax.psum_scatter(grad_gate_up, "fsdp", scatter_dimension=0, tiled=True)
    all_gate_up = gather_ctx([row_gate_up], n_ctx, 7)[0]
    final_gate_up = assemble(all_gate_up, 2)

    grad_norm2 = jnp.sum(d_two * hidden * scale_two, 0)
    d_hidden = cotangent[0].astype(f32) + norm_back(d_two, hidden, scale_two, gain_two)
    d_branch = d_hidden.astype(bf16)
    db_all = gather_ctx([d_branch], n_ctx, 3)[0].reshape(all_rows, width)

    grad_out = dot(mixed_dealt, db_all, TN).astype(bf16)
    wo_own = lax.dynamic_slice(wo, (me * hw, 0), (hw, width))
    d_mixed = dot(db_all, wo_own, NT).astype(bf16)
    d_mixed = jnp.take(d_mixed.reshape(pieces, piece, hw), given_from, axis=0)
    d_mixed = d_mixed.reshape(all_rows, hw)
    d_proj = attend_back(
        queries, keys, values, d_mixed, cosine_table, sine_table, first_key, heads
    )
    d_one = reduce_ctx(d_proj, wq, n_ctx, 6, True).astype(f32)
    grad_qkv = dot(normed_one, d_proj, TN).astype(bf16)
    row_qkv = lax.psum_scatter(grad_qkv, "fsdp", scatter_dimension=0, tiled=True)

    own_float = x_own.astype(f32)
    scale_one = rms_scale(own_float)
    grad_norm1 = jnp.sum(d_one * own_float * scale_one, 0)
    dh_own = jnp.take(db_all.reshape(pieces, piece, width), own_given, axis=0)
    dh_own = dh_own.reshape(rows, width).astype(f32)
    grad_tokens = (dh_own + norm_back(d_one, own_float, scale_one, gain_one)).astype(bf16)[None]

    norms = lax.psum_scatter(
        jnp.stack([grad_norm1, grad_norm2]), "fsdp", scatter_dimension=1, tiled=True
    )
    norms = jnp.pad(norms, ((0, 6), (0, 0)))
    all_qkv, all_norms = gather_ctx([row_qkv, norms], n_ctx, 8)
    final_qkv = assemble(all_qkv, 3)
    final_norms = jnp.sum(all_norms, 0)

    grad_rows = jnp.concatenate([grad_down, grad_out], 0)
    col_rows = lax.psum_scatter(grad_rows, "fsdp", scatter_dimension=1, tiled=True)
    all_cols = gather_ctx([col_rows], n_ctx, 9)[0]
    owner_rows = all_cols.reshape(n_fsdp, ratio * (ffs + hw), width // n_fsdp)
    swapped = lax.all_to_all(owner_rows, "fsdp", split_axis=0, concat_axis=0, tiled=True)
    final_down, final_out = assemble_rows(swapped, ratio, ffs)
    return (
        block_out,
        grad_tokens,
        final_norms[0],
        final_qkv,
        final_out,
        final_norms[1],
        final_gate_up,
        final_down,
    )


def solution(mesh):
    in_specs = (
        P("fsdp", "ctx", None),
        P("fsdp", "ctx", None),
        P("fsdp", None),
        P("fsdp", None, None),
        P("fsdp"),
        P("fsdp", None),
        P("fsdp", None),
        P("fsdp"),
        P("fsdp", None),
        P("fsdp", None),
    )
    out_specs = (
        P("fsdp", "ctx", None),
        P("fsdp", "ctx", None),
        P("fsdp"),
        P("fsdp", None),
        P("fsdp", None),
        P("fsdp"),
        P("fsdp", None),
        P("fsdp", None),
    )
    return jax.shard_map(shards, mesh=mesh, in_specs=in_specs, out_specs=out_specs, check_vma=False)
```

```python
import functools
import math

import jax
import jax.numpy as jnp
from jax import lax
from jax.experimental import pallas as pl
from jax.experimental.pallas import tpu as pltpu
from jax.sharding import PartitionSpec as P

MESH = pl.DeviceIdType.MESH
LINE = 4

H = 16
HD = 128

epsilon = 1e-06
rope_base = 10000.0
masked_score = -1e30
f32 = jnp.float32
bf16 = jnp.bfloat16


def greet(a, b, n_a, n_b, f, fsdp=False):
    bar = pltpu.get_barrier_semaphore()
    conds = ((a > 0, a - 1, b), (a < n_a - 1, a + 1, b), (b > 0, a, b - 1), (b < n_b - 1, a, b + 1))
    for cond, aa, bb in conds:

        @pl.when(cond)
        def _():
            pl.semaphore_signal(bar, inc=1, device_id=(aa * n_b + bb, f), device_id_type=MESH)

    low = (a + n_a - 1) // n_a + (b + n_b - 1) // n_b
    high = (2 * n_a - 2 - a) // n_a + (2 * n_b - 2 - b) // n_b
    total = low + high
    if fsdp:
        n_f = lax.axis_size("fsdp")
        for m in range(1, n_f):
            pl.semaphore_signal(
                bar, inc=1, device_id=(a * n_b + b, (f + m) % n_f), device_id_type=MESH
            )
        total = total + n_f - 1
    pl.semaphore_wait(bar, total)


def both(*conds):
    out = True
    for cond in conds:
        if cond is not True:
            out = cond if out is True else jnp.logical_and(out, cond)
    return out


def when(cond):
    return (lambda fn: fn()) if cond is True else pl.when(cond)


def plan(rows, cuts=2):
    unit = rows // 16
    if rows % 16 or unit < 4:
        return ((0, rows, False),)
    swapped = max(1, (unit + 4) // 8)
    rest = unit - swapped
    marks = [rest * i // cuts for i in range(cuts + 1)]
    chunks = [(16 * lo, 16 * (hi - lo), False) for lo, hi in zip(marks, marks[1:])]
    return tuple(chunks) + ((16 * rest, 16 * swapped, True),)


def places(n):
    n_a, n_b = LINE, n // LINE
    c = lax.axis_index("ctx")
    return n_a, n_b, c // n_b, c % n_b, lax.axis_index("fsdp")


def gather_steps(n, x, out, chunk, sems):
    n_a, n_b, a, b, f = places(n)
    first, count, swapped = chunk
    s1, r1, s2, r2 = sems
    (p1, n1), (p2, n2) = ((b, n_b), (a, n_a)) if swapped else ((a, n_a), (b, n_b))

    def slot(q1, q2):
        return q2 * n_b + q1 if swapped else q1 * n_b + q2

    rows = pl.ds(first, count)
    below1, above1, below2, above2 = p1 > 0, p1 < n1 - 1, p2 > 0, p2 < n2 - 1

    def copy1(k, d):
        q1 = p1 - k if d == 0 else p1 + k
        to = p1 + 1 if d == 0 else p1 - 1
        return pltpu.make_async_remote_copy(
            src_ref=x.at[rows] if k == 0 else out.at[slot(q1, p2), rows],
            dst_ref=out.at[slot(q1, p2), rows],
            send_sem=s1.at[d, k],
            recv_sem=r1.at[d, k],
            device_id=(slot(to, p2), f),
            device_id_type=MESH,
        )

    def copy2(j, q1, m, d):
        q2 = p2 - m if d == 0 else p2 + m
        to = p2 + 1 if d == 0 else p2 - 1
        return pltpu.make_async_remote_copy(
            src_ref=x.at[rows] if j == 0 and m == 0 else out.at[slot(q1, q2), rows],
            dst_ref=out.at[slot(q1, q2), rows],
            send_sem=s2.at[d, m, j],
            recv_sem=r2.at[d, m, j],
            device_id=(slot(p1, to), f),
            device_id_type=MESH,
        )

    shards = [(0, 0, None, p1, True)]
    for k in range(1, n1):
        shards.append((k, k, 0, p1 - k, p1 >= k))
        shards.append((n1 - 1 + k, k, 1, p1 + k, p1 + k < n1))

    def own():
        for d, cond in ((0, above1), (1, below1)):
            when(cond)(lambda d=d: copy1(0, d).start())
        for d, cond in ((0, above2), (1, below2)):
            when(cond)(lambda d=d: copy2(0, p1, 0, d).start())

    def line1(k):
        for j, kk, side, q1, there in shards:
            if kk != k:
                continue

            @when(there)
            def _():
                copy1(k - 1, side).wait_recv()
                if k < n1 - 1:
                    when(above1 if side == 0 else below1)(lambda: copy1(k, side).start())
                for d, cond in ((0, above2), (1, below2)):
                    when(cond)(lambda d=d: copy2(j, q1, 0, d).start())

    def line2(m):
        for d, there2, onward in ((0, p2 >= m, above2), (1, p2 + m < n2, below2)):
            for j, _, _, q1, there in shards:

                @when(both(there2, there))
                def _():
                    copy2(j, q1, m - 1, d).wait_recv()
                    if m < n2 - 1:
                        when(onward)(lambda: copy2(j, q1, m, d).start())

    def finish():
        for j, k, side, q1, there in shards:
            for d, onward in ((0, above1), (1, below1)):
                if k < n1 - 1 and side in (None, d):
                    when(both(onward, there))(lambda d=d: copy1(k, d).wait_send())
            for m in range(n2 - 1):
                for d, onward, there2 in ((0, above2, p2 >= m), (1, below2, p2 + m < n2)):
                    when(both(onward, there, True if m == 0 else there2))(
                        lambda d=d, m=m: copy2(j, q1, m, d).wait_send()
                    )

    steps = [own]
    steps += [functools.partial(line1, k) for k in range(1, n1)]
    steps += [functools.partial(line2, m) for m in range(1, n2)]
    return steps, finish


def spread_steps(n, x, out, chunk, sems):
    f = lax.axis_index("fsdp")
    c = lax.axis_index("ctx")
    n_f = lax.axis_size("fsdp")
    n_y = n_f // 2
    y, core = f // 2, f % 2
    owner = c // (n // n_f)
    oy, oc = owner // 2, owner % 2
    first, count = chunk
    rows = pl.ds(first, count)
    up, down, side, come = sems

    def copy(own, sem, to):
        return pltpu.make_async_remote_copy(
            src_ref=x.at[rows] if own else out.at[rows],
            dst_ref=out.at[rows],
            send_sem=sem,
            recv_sem=come,
            device_id=(c, to),
            device_id_type=MESH,
        )

    on = core == oc
    ways = (
        (up, f + 2, jnp.logical_and(on, jnp.logical_and(y >= oy, y < n_y - 1))),
        (down, f - 2, jnp.logical_and(on, jnp.logical_and(y <= oy, y > 0))),
        (side, f + 1 - 2 * core, on),
    )

    def own():
        for sem, to, cond in ways:
            pl.when(jnp.logical_and(cond, f == owner))(lambda sem=sem, to=to: copy(True, sem, to).start())

    def onward():
        @pl.when(f != owner)
        def _():
            copy(False, side, f).wait_recv()
            for sem, to, cond in ways:
                pl.when(cond)(lambda sem=sem, to=to: copy(False, sem, to).start())

    def finish():
        for sem, to, cond in ways:
            pl.when(cond)(lambda sem=sem, to=to: copy(False, sem, to).wait_send())

    return own, onward, finish


def gather_sems(chunks):
    sem = pltpu.SemaphoreType.DMA
    return [sem((chunks, 2, 4)), sem((chunks, 2, 4)), sem((chunks, 2, 4, 7)), sem((chunks, 2, 4, 7))]


def gather_kernel(n, plans, spread, *refs):
    count = len(plans)
    k = count + (1 if spread else 0)
    xs, outs = refs[:k], refs[k : 2 * k]
    held = refs[2 * k : 3 * k]
    local, s1, r1, s2, r2, s3 = refs[3 * k :]
    n_a, n_b, a, b, f = places(n)
    c = a * n_b + b
    greet(a, b, n_a, n_b, f, bool(spread))
    steps, ends, at = [], [], 0
    for x, out, chunks in zip(xs, outs, plans):
        for chunk in chunks:
            sems = (s1.at[at], r1.at[at], s2.at[at], r2.at[at])
            more, end = gather_steps(n, x, out, chunk, sems)
            steps.append(more)
            ends.append(end)
            at += 1
    for i, chunk in enumerate(spread):
        begin, onward, end = spread_steps(n, xs[-1], outs[-1], chunk, [s3.at[i, j] for j in range(4)])
        steps.append([begin] + [lambda: None] * (1 + 2 * i) + [onward])
        ends.append(end)
    mine = f == c // (n // lax.axis_size("fsdp"))
    for t in range(max(map(len, steps))):
        for more in steps:
            if t < len(more):
                more[t]()
        if t < 2:
            for i in range(k):
                out = outs[i].at[c] if i < count else outs[i]

                @when(True if i < count else mine)
                def _():
                    fetch = pltpu.make_async_copy(xs[i], held[i], local.at[i])
                    if t == 0:
                        fetch.start()
                    else:
                        fetch.wait()
                        pltpu.make_async_copy(held[i], out, local.at[i]).start()
    for i in range(k):
        out = outs[i].at[c] if i < count else outs[i]
        when(True if i < count else mine)(pltpu.make_async_copy(held[i], out, local.at[i]).wait)
    for end in ends:
        end()


def gather_ctx(xs, n, cid, cuts=2, spread=None):
    plans = tuple(plan(x.shape[0], cuts) for x in xs)
    shapes = [jax.ShapeDtypeStruct((n,) + x.shape, x.dtype) for x in xs]
    parts = ()
    if spread is not None:
        rows = spread.shape[0]
        half = rows // 32 * 16
        parts = ((0, rows),) if rows % 16 else ((0, half), (half, rows - half))
        xs = xs + [spread]
        shapes = shapes + [jax.ShapeDtypeStruct(spread.shape, spread.dtype)]
    return pl.pallas_call(
        functools.partial(gather_kernel, n, plans, parts),
        out_shape=shapes,
        in_specs=[pl.BlockSpec(memory_space=pl.ANY)] * len(xs),
        out_specs=[pl.BlockSpec(memory_space=pl.ANY)] * len(xs),
        scratch_shapes=[pltpu.VMEM(x.shape, x.dtype) for x in xs]
        + [pltpu.SemaphoreType.DMA((len(xs),))]
        + gather_sems(sum(map(len, plans)))
        + [pltpu.SemaphoreType.DMA((2, 4))],
        compiler_params=pltpu.CompilerParams(
            collective_id=cid, has_side_effects=True, vmem_limit_bytes=60 << 20
        ),
        name=f"gather{cid}",
    )(*xs)


def cast_rows(src, dst):
    rows = src.shape[0]
    if rows % 16:
        dst[...] = src[...].astype(dst.dtype)
        return

    def one(i, carry):
        at = pl.ds(pl.multiple_of(i * 16, 16), 16)
        dst[at, :] = src[at, :].astype(dst.dtype)
        return carry

    lax.fori_loop(0, rows // 16, one, 0)


def first_kernel(n, chunks, ratio, *refs):
    x, wo, wd, g, out, wo_out, wd_out, g_out = refs[:8]
    held, wo_wide, wo_low, wd_wide, wd_low, g_held, local, s1, r1, s2, r2, gs, gr = refs[8:]
    n_a, n_b, a, b, f = places(n)
    c = a * n_b + b
    n_f = lax.axis_size("fsdp")
    ffs = wd_low.shape[0]
    own = pl.ds(pl.multiple_of((c % ratio) * ffs, 8), ffs)
    loads = [
        pltpu.make_async_copy(src, dst, local.at[i])
        for i, (src, dst) in enumerate(((x, held), (wo, wo_wide), (wd.at[own], wd_wide), (g, g_held)))
    ]
    stores = [
        pltpu.make_async_copy(src, dst, local.at[i])
        for i, (src, dst) in enumerate(
            ((held, out.at[c]), (wo_low, wo_out), (wd_low, wd_out), (g_held, g_out.at[f]))
        )
    ]
    for copy in loads:
        copy.start()
    greet(a, b, n_a, n_b, f, True)
    steps, ends = [], []
    for i, chunk in enumerate(chunks):
        more, end = gather_steps(n, x, out, chunk, (s1.at[i], r1.at[i], s2.at[i], r2.at[i]))
        steps.append(more)
        ends.append(end)

    def gain(m):
        return pltpu.make_async_remote_copy(
            src_ref=g,
            dst_ref=g_out.at[f],
            send_sem=gs.at[m],
            recv_sem=gr.at[m],
            device_id=(c, (f + m) % n_f),
            device_id_type=MESH,
        )

    for t in range(n_a + n_b - 1):
        for more in steps:
            if t < len(more):
                more[t]()
        if t == 0:
            for m in range(1, n_f):
                gain(m).start()
            loads[0].wait()
            stores[0].start()
            loads[3].wait()
            stores[3].start()
            loads[1].wait()
            cast_rows(wo_wide, wo_low)
            stores[1].start()
        if t == 1:
            loads[2].wait()
            cast_rows(wd_wide, wd_low)
            stores[2].start()
    for copy in stores:
        copy.wait()
    for m in range(1, n_f):
        gain(m).wait()
    for end in ends:
        end()


def gather_first(x, w_out, w_down, gains, n, ratio, ffs, cid):
    n_f = lax.axis_size("fsdp")
    chunks = plan(x.shape[0])
    low = [jax.ShapeDtypeStruct(w_out.shape, bf16), jax.ShapeDtypeStruct((ffs, w_down.shape[1]), bf16)]
    sem = pltpu.SemaphoreType.DMA
    return pl.pallas_call(
        functools.partial(first_kernel, n, chunks, ratio),
        out_shape=[jax.ShapeDtypeStruct((n,) + x.shape, x.dtype)]
        + low
        + [jax.ShapeDtypeStruct((n_f,) + gains.shape, gains.dtype)],
        in_specs=[pl.BlockSpec(memory_space=pl.ANY)] * 4,
        out_specs=[pl.BlockSpec(memory_space=pl.ANY)] * 4,
        scratch_shapes=[
            pltpu.VMEM(x.shape, x.dtype),
            pltpu.VMEM(w_out.shape, f32),
            pltpu.VMEM(w_out.shape, bf16),
            pltpu.VMEM((ffs, w_down.shape[1]), f32),
            pltpu.VMEM((ffs, w_down.shape[1]), bf16),
            pltpu.VMEM(gains.shape, gains.dtype),
            sem((4,)),
        ]
        + gather_sems(len(chunks))
        + [sem((n_f,)), sem((n_f,))],
        compiler_params=pltpu.CompilerParams(
            collective_id=cid, has_side_effects=True, vmem_limit_bytes=60 << 20
        ),
        name=f"gather{cid}",
    )(x, w_out, w_down, gains)


def order_of(p, n):
    if n == 2:
        return (1 - p, p)
    h = p // 2
    return (3 - 3 * h, 2 - h, 1 - p + 4 * h, p)


def reduce_steps(n, part, chunk, bufs, sems):
    n_a, n_b, a, b, f = places(n)
    first, count, swapped = chunk
    g1, g2 = bufs
    s1, r1, s2, r2 = sems
    (p1, n1), (p2, n2) = ((a, n_a), (b, n_b)) if swapped else ((b, n_b), (a, n_a))

    def slot(q1, q2):
        return q1 * n_b + q2 if swapped else q2 * n_b + q1

    rows = pl.ds(first, count)
    from1 = (p1 > 0, p1 < n1 - 1)
    from2 = (p2 > 0, p2 < n2 - 1)
    targets = order_of(p2, n2)

    def has1(d, k):
        return (p1 + k < n1) if d == 0 else (p1 >= k)

    def add(t, got):
        mine = part.at[t, rows]
        mine[...] = (mine[...].astype(f32) + got[...].astype(f32)).astype(mine.dtype)

    def remote(src, dst, send, recv, to):
        return pltpu.make_async_remote_copy(
            src_ref=src, dst_ref=dst, send_sem=send, recv_sem=recv, device_id=(to, f), device_id_type=MESH
        )

    def side1(d):
        return d if n1 > 2 else 0

    def copy1(j, d, k):
        t = p1 + k if d == 0 else p1 - k
        to = p1 + 1 if d == 0 else p1 - 1
        src = part.at[slot(t, targets[j]), rows]
        return remote(src, g1.at[side1(d), k - 1, j], s1.at[d, k, j], r1.at[d, k - 1, j], slot(to, p2))

    def come1(j, d, k):
        src = part.at[slot(p1, p2), rows]
        return remote(src, g1.at[side1(d), k, j], s1.at[d, k, j], r1.at[d, k, j], slot(p1, p2))

    def copy2(t, d):
        k = t - p2 if d == 0 else p2 - t
        to = p2 + 1 if d == 0 else p2 - 1
        return remote(
            part.at[slot(p1, t), rows], g2.at[d, k - 1], s2.at[d, k], r2.at[d, k - 1], slot(p1, to)
        )

    def come2(d, k):
        src = part.at[slot(p1, p2), rows]
        return remote(src, g2.at[d, k], s2.at[d, k], r2.at[d, k], slot(p1, p2))

    def start(j):
        for d in (0, 1) if j < n2 else ():
            for k in range(n1 - 1, 0, -1):
                when(both(has1(d, k), jnp.logical_not(from1[d])))(
                    lambda d=d, k=k: copy1(j, d, k).start()
                )

    def middle1(j, k):
        for d in (0, 1):

            @when(both(has1(d, k), from1[d]))
            def _():
                come1(j, d, k).wait_recv()
                add(slot(p1 + k if d == 0 else p1 - k, targets[j]), g1.at[side1(d), k, j])
                copy1(j, d, k).start()

    def last1(j):
        for d in (0, 1):

            @when(from1[d])
            def _():
                come1(j, d, 0).wait_recv()
                add(slot(p1, targets[j]), g1.at[side1(d), 0, j])

    def line2(j):
        t = targets[j]
        for d in (0, 1):

            @when((t > p2) if d == 0 else (t < p2))
            def _():
                @when(from2[d])
                def _():
                    k = t - p2 if d == 0 else p2 - t
                    come2(d, k).wait_recv()
                    add(slot(p1, t), g2.at[d, k])

                copy2(t, d).start()

    def last2():
        for d in (0, 1):

            @when(from2[d])
            def _():
                come2(d, 0).wait_recv()
                add(slot(p1, p2), g2.at[d, 0])

    steps = []
    if swapped:
        for k in range(n1 - 2, 0, -1):
            steps.append(lambda k=k: [middle1(j, k) for j in range(n2)])
        steps.append(lambda: [(last1(j), line2(j) if j < n2 - 1 else None) for j in range(n2)])
        steps.append(last2)
    else:

        def item(j):
            for k in range(n1 - 2, 0, -1):
                middle1(j, k)
            last1(j)
            if j < n2 - 1:
                line2(j)

        steps += [functools.partial(item, j) for j in range(n2)] + [last2]

    def finish():
        for j in range(n2):
            for d in (0, 1):
                for k in range(n1 - 1, 0, -1):
                    when(has1(d, k))(lambda j=j, d=d, k=k: copy1(j, d, k).wait_send())
                if j < n2 - 1:
                    t = targets[j]
                    when((t > p2) if d == 0 else (t < p2))(lambda t=t, d=d: copy2(t, d).wait_send())

    return start, steps, finish


def reduce_kernel(n, chunks, jobs, extras, count, *refs):
    n_a, n_b, a, b, f = places(n)
    k, e = len(jobs), len(extras)
    hbm, rest = refs[:count], refs[count:]
    o_refs, p_refs, rest = rest[:k], rest[k : k + e], rest[k + e :]
    held, parts, made, rest = rest[:count], rest[count : count + k], rest[count + k : count + k + e], rest[count + k + e :]
    cuts = len(chunks)
    bufs, rest = rest[: 2 * k * cuts], rest[2 * k * cuts :]
    load, stored, s1, r1, s2, r2 = rest
    rows = o_refs[0].shape[0]
    first = sorted({i for x, w, _ in jobs for i in (x, w)})
    order_in = first + [i for i in range(count) if i not in first]
    loads = [pltpu.make_async_copy(hbm[i], held[i], load.at[i]) for i in range(count)]
    for i in order_in:
        loads[i].start()
    todo = []
    for i in range(k):
        for m, chunk in enumerate(chunks):
            at = i * cuts + m
            sems = (s1.at[at], r1.at[at], s2.at[at], r2.at[at])
            todo.append(reduce_steps(n, parts[i], chunk, bufs[2 * at : 2 * at + 2], sems))

    def term(i, t):
        x, w, nt = jobs[i]
        at = pl.multiple_of(t * rows, rows)
        parts[i][t] = dot(held[x][pl.ds(at, rows), :], held[w][...], NT if nt else NN).astype(bf16)

    tiles, stores = [], []
    for i, (x, y) in enumerate(extras):
        high = held[x].shape[1]
        for lo in range(0, high, 256):
            hi = min(lo + 256, high)

            def tile(i=i, x=x, y=y, lo=lo, hi=hi):
                made[i][lo:hi, :] = dot(held[x][:, lo:hi], held[y][...], TN).astype(bf16)

            tiles.append(tile)
        stores.append((len(tiles), i))

    order = order_of(a, n_a)
    greet(a, b, n_a, n_b, f)
    for i in first:
        loads[i].wait()
    for j in range(n_a):
        for i in range(k):
            for m in range(1, n_b):
                term(i, order[j] * n_b + (b + m) % n_b)
            for start, _, _ in todo[i * cuts : (i + 1) * cuts]:
                start(j)
    for i in order_in[len(first) :]:
        loads[i].wait()
    done = 0
    for j in range(n_a):
        for i in range(k):
            term(i, order[j] * n_b + b)
        upto = len(tiles) * (j + 1) // n_a
        for at in range(done, upto):
            tiles[at]()
            for last, i in stores:
                if last == at + 1:
                    pltpu.make_async_copy(made[i], p_refs[i], stored.at[i]).start()
        done = upto
        for _, steps, _ in todo:
            steps[j]()
    for _, steps, _ in todo:
        steps[n_a]()
    for i in range(k):
        o_refs[i][...] = parts[i][a * n_b + b]
    for _, _, finish in todo:
        finish()
    for i in range(e):
        pltpu.make_async_copy(made[i], p_refs[i], stored.at[i]).wait()


def reduce_ctx(arrays, jobs, extras, n, cid):
    n_a, n_b = LINE, n // LINE
    rows = arrays[jobs[0][0]].shape[0] // n
    half = rows // 2
    chunks = ((0, half, False), (half, half, False))
    widths = [arrays[w].shape[0 if nt else 1] for _, w, nt in jobs]
    bufs = []
    for width in widths:
        for _, count, _ in chunks:
            bufs += [
                pltpu.VMEM((min(2, n_b - 1), n_b - 1, n_a, count, width), bf16),
                pltpu.VMEM((2, n_a - 1, count, width), bf16),
            ]
    made = [(arrays[x].shape[1], arrays[y].shape[1]) for x, y in extras]
    sem = pltpu.SemaphoreType.DMA
    k = len(jobs) * len(chunks)
    return pl.pallas_call(
        functools.partial(reduce_kernel, n, chunks, jobs, extras, len(arrays)),
        out_shape=[jax.ShapeDtypeStruct((rows, width), bf16) for width in widths]
        + [jax.ShapeDtypeStruct(shape, bf16) for shape in made],
        in_specs=[pl.BlockSpec(memory_space=pl.ANY)] * len(arrays),
        out_specs=[pl.BlockSpec(memory_space=pltpu.VMEM)] * len(widths)
        + [pl.BlockSpec(memory_space=pl.ANY)] * len(made),
        scratch_shapes=[pltpu.VMEM(x.shape, x.dtype) for x in arrays]
        + [pltpu.VMEM((n, rows, width), bf16) for width in widths]
        + [pltpu.VMEM(shape, bf16) for shape in made]
        + bufs
        + [sem((len(arrays),)), sem((max(1, len(made)),))]
        + [sem((k, 2, 4, 4)), sem((k, 2, 4, 4)), sem((k, 2, 4)), sem((k, 2, 4))],
        compiler_params=pltpu.CompilerParams(
            collective_id=cid, has_side_effects=True, vmem_limit_bytes=60 << 20
        ),
        name=f"reduce{cid}",
    )(*arrays)


def assemble_rows(parts, ratio, ffs):
    n, rows, w = parts.shape
    each = rows // ratio
    hw = each - ffs

    def body(i_ref, down_ref, out_ref):
        for j in range(ratio):
            down_ref[j * ffs : (j + 1) * ffs, :] = i_ref[0, j * each : j * each + ffs, :].astype(f32)
            out_ref[j * hw : (j + 1) * hw, :] = i_ref[0, j * each + ffs : (j + 1) * each, :].astype(f32)

    return pl.pallas_call(
        body,
        grid=(n,),
        out_shape=[
            jax.ShapeDtypeStruct((ratio * ffs, n * w), f32),
            jax.ShapeDtypeStruct((ratio * hw, n * w), f32),
        ],
        in_specs=[pl.BlockSpec((1, rows, w), lambda i: (i, 0, 0))],
        out_specs=[
            pl.BlockSpec((ratio * ffs, w), lambda i: (0, i)),
            pl.BlockSpec((ratio * hw, w), lambda i: (0, i)),
        ],
        compiler_params=pltpu.CompilerParams(vmem_limit_bytes=60 << 20),
        name="assemble_rows",
    )(parts)


def assemble(parts, n_groups, block=64):
    n, rows, gw = parts.shape
    w = gw // n_groups

    def body(i_ref, o_ref):
        for g in range(n_groups):
            for c in range(n):
                o_ref[:, (g * n + c) * w:(g * n + c + 1) * w] = i_ref[c, :, g * w:(g + 1) * w].astype(jnp.float32)

    return pl.pallas_call(
        body, grid=(rows // block,),
        out_shape=jax.ShapeDtypeStruct((rows, n * gw), jnp.float32),
        in_specs=[pl.BlockSpec((n, block, gw), lambda i: (0, i, 0))],
        out_specs=pl.BlockSpec((block, n * gw), lambda i: (i, 0)),
        compiler_params=pltpu.CompilerParams(vmem_limit_bytes=60 << 20),
        name="assemble")(parts)


def dot(a, b, dims):
    return lax.dot_general(a, b, (dims, ((), ())), preferred_element_type=f32)


NN = ((1,), (0,))
NT = ((1,), (1,))
TN = ((0,), (0,))


def turned(u):
    return pltpu.roll(u, HD // 2, 1)


def masked_probs(q, k, first, at):
    logits = dot(q, k, NT) * (1.0 / math.sqrt(HD))
    keys = lax.broadcasted_iota(jnp.int32, logits.shape, 1)
    queries = lax.broadcasted_iota(jnp.int32, logits.shape, 0) + at
    scaled = jnp.where((keys <= queries) & (keys >= first), logits, masked_score)
    raised = jnp.exp(scaled - jnp.max(scaled, -1, keepdims=True))
    return raised / jnp.sum(raised, -1, keepdims=True)


def attend_kernel(heads, block, n_ref, w_ref, cos_ref, sin_ref, first_ref, q_ref, k_ref, v_ref, o_ref):
    rows = n_ref.shape[0]
    hw = heads * HD
    for at in range(0, rows, block):
        own = slice(at, at + block)
        proj = dot(n_ref[own, :], w_ref[...], NN)
        cos, sin = cos_ref[own, :], sin_ref[own, :]
        for h in range(heads):
            head = slice(h * HD, (h + 1) * HD)
            for ref, base in ((q_ref, 0), (k_ref, hw)):
                u = proj[:, base + h * HD : base + (h + 1) * HD]
                ref[own, head] = (u * cos + turned(u) * sin).astype(bf16)
        v_ref[own, :] = proj[:, 2 * hw :].astype(bf16)
        for h in range(heads):
            head = slice(h * HD, (h + 1) * HD)
            seen = slice(0, at + block)
            probs = masked_probs(q_ref[own, head], k_ref[seen, head], first_ref[own, :], at)
            o_ref[own, head] = dot(probs.astype(bf16), v_ref[seen, head], NN).astype(bf16)


def attend(normed, wq, cos, sin, first, heads, block=256):
    rows = normed.shape[0]
    one = jax.ShapeDtypeStruct((rows, heads * HD), bf16)
    return pl.pallas_call(
        functools.partial(attend_kernel, heads, block),
        out_shape=[one] * 4,
        compiler_params=pltpu.CompilerParams(vmem_limit_bytes=60 << 20),
        name="attend",
    )(normed, wq, cos, sin, first)


def attend_back_kernel(
    heads, block, q_ref, k_ref, v_ref, d_ref, cos_ref, sin_ref, first_ref, o_ref, dk_ref, dv_ref
):
    rows = q_ref.shape[0]
    hw = heads * HD

    def back(w, own):
        return (w * cos_ref[own, :] - turned(w) * sin_ref[own, :]).astype(bf16)

    for h in range(heads):
        head = slice(h * HD, (h + 1) * HD)
        for at in reversed(range(0, rows, block)):
            own = slice(at, at + block)
            seen = slice(0, at + block)
            q, k, v, d = q_ref[own, head], k_ref[seen, head], v_ref[seen, head], d_ref[own, head]
            probs = masked_probs(q, k, first_ref[own, :], at)
            d_probs = dot(d, v, NT)
            inner = jnp.sum(probs * d_probs, -1, keepdims=True)
            d_scores = (probs * (d_probs - inner) * (1.0 / math.sqrt(HD))).astype(bf16)
            o_ref[own, head] = back(dot(d_scores, k, NN), own)
            dk = dot(d_scores, q, TN)
            dv = dot(probs.astype(bf16), d, TN)
            if at + block == rows:
                dk_ref[...] = dk
                dv_ref[...] = dv
            else:
                dk_ref[seen, :] += dk
                dv_ref[seen, :] += dv
        every = slice(0, rows)
        o_ref[:, hw + h * HD : hw + (h + 1) * HD] = back(dk_ref[...], every)
        o_ref[:, 2 * hw + h * HD : 2 * hw + (h + 1) * HD] = dv_ref[...].astype(bf16)


def attend_back(q, k, v, d_mixed, cos, sin, first, heads, block=256):
    rows = q.shape[0]
    return pl.pallas_call(
        functools.partial(attend_back_kernel, heads, block),
        out_shape=jax.ShapeDtypeStruct((rows, 3 * heads * HD), bf16),
        scratch_shapes=[pltpu.VMEM((rows, HD), f32), pltpu.VMEM((rows, HD), f32)],
        compiler_params=pltpu.CompilerParams(vmem_limit_bytes=60 << 20),
        name="attend_back",
    )(q, k, v, d_mixed, cos, sin, first)


def rope_tables(within):
    freq_index = jnp.arange(HD // 2, dtype=f32)
    inverse = rope_base ** (-2.0 * freq_index / HD)
    angles = within.astype(f32)[:, None] * inverse[None, :]
    cos, sin = jnp.cos(angles), jnp.sin(angles)
    return jnp.concatenate([cos, cos], -1), jnp.concatenate([-sin, sin], -1)


def rms_scale(values):
    return lax.rsqrt(jnp.mean(values * values, -1, keepdims=True) + epsilon)


def norm_back(grad_norm, values, scale_rows, gain_float):
    scaled = grad_norm * gain_float[None, :]
    cubed = scale_rows * scale_rows * scale_rows
    return scale_rows * scaled - values * cubed * jnp.mean(scaled * values, -1, keepdims=True)


def shards(
    tokens, cotangent, lengths, deal, norm1_gain, w_qkv, w_out, norm2_gain, w_gate_up, w_down
):
    n_ctx = lax.axis_size("ctx")
    n_fsdp = lax.axis_size("fsdp")
    me = lax.axis_index("ctx")
    mine = lax.axis_index("fsdp")
    rows = tokens.shape[1]
    width = tokens.shape[2]
    piece = rows // n_ctx
    all_rows = rows * n_ctx
    pieces = all_rows // piece
    heads = H // n_ctx
    hw = heads * HD
    kr = w_qkv.shape[0]
    ff = w_gate_up.shape[1] // 2
    ffs = ff // n_ctx
    ff_rows = w_down.shape[0]
    ratio = n_ctx // n_fsdp

    x_own = tokens[0]
    gains = jnp.pad(jnp.stack([norm1_gain, norm2_gain]), ((0, 6), (0, 0)))
    x_all, wo_own, down_own, gains = gather_first(
        x_own, w_out, w_down, gains, n_ctx, ratio, ffs, 0
    )
    x_all = x_all.reshape(all_rows, width)

    qkv_own = jnp.concatenate(
        [lax.dynamic_slice(w_qkv, (0, i * width + me * hw), (kr, hw)) for i in range(3)], -1
    )
    wq = lax.all_gather(qkv_own.astype(bf16), "fsdp", axis=0, tiled=True)
    gain_one = gains[:, 0].reshape(width).astype(bf16).astype(f32)
    gain_two = gains[:, 1].reshape(width).astype(bf16).astype(f32)
    wo = lax.all_gather(wo_own, "fsdp", axis=0, tiled=True)
    wg_own = jnp.concatenate(
        [
            lax.dynamic_slice(w_gate_up, (0, me * ffs), (kr, ffs)),
            lax.dynamic_slice(w_gate_up, (0, ff + me * ffs), (kr, ffs)),
        ],
        -1,
    ).astype(bf16)
    wgu = lax.all_gather(wg_own, "fsdp", axis=0, tiled=True)
    g_all = gather_ctx([cotangent[0]], n_ctx, 1)[0].reshape(all_rows, width)

    deal_table = deal[0]
    device_index = jnp.arange(n_ctx, dtype=jnp.int32)
    marks = (deal_table[:, :, None] == device_index[None, None, :]).astype(jnp.int32)
    source_piece = jnp.sum(marks * device_index[None, :, None], 1)
    dealt_from = (device_index[None, :] * n_ctx + source_piece.T).reshape(pieces)
    given_from = (deal_table * n_ctx + device_index[:, None]).reshape(pieces)
    own_dealt = lax.dynamic_slice(dealt_from, (me * n_ctx,), (n_ctx,))
    own_given = lax.dynamic_slice(given_from, (me * n_ctx,), (n_ctx,))
    places = jnp.arange(all_rows, dtype=jnp.int32)
    doc_lengths = lengths[0]
    ends = jnp.cumsum(doc_lengths)
    starts = ends - doc_lengths
    docs = jnp.sum((places[:, None] >= ends[None, :]).astype(jnp.int32), -1)
    doc_index = jnp.arange(doc_lengths.shape[0], dtype=jnp.int32)
    firsts = jnp.sum(jnp.where(docs[:, None] == doc_index[None, :], starts[None, :], 0), -1)
    within = places - firsts
    first_key = firsts[:, None]
    cosine_table, sine_table = rope_tables(within)

    x_float = x_all.astype(f32)
    normed_one = (x_float * rms_scale(x_float) * gain_one[None, :]).astype(bf16)
    queries, keys, values, mixed = attend(
        normed_one, wq, cosine_table, sine_table, first_key, heads
    )
    mixed = mixed.reshape(pieces, piece, hw)
    mixed_dealt = jnp.take(mixed, dealt_from, axis=0)
    mixed_own = lax.all_to_all(
        mixed_dealt.reshape(n_ctx, rows, hw), "ctx", split_axis=0, concat_axis=2, tiled=True
    ).reshape(rows, width)
    mixed_dealt = mixed_dealt.reshape(all_rows, hw)

    x_dealt = jnp.take(x_all.reshape(pieces, piece, width), own_dealt, axis=0)
    hidden = x_dealt.reshape(rows, width).astype(f32) + dot(mixed_own, wo, NN)
    scale_two = rms_scale(hidden)
    normed_two = (hidden * scale_two * gain_two[None, :]).astype(bf16)
    n2_all, wd = gather_ctx([normed_two], n_ctx, 2, spread=down_own)
    n2_all = n2_all.reshape(all_rows, width)

    both = dot(n2_all, wgu, NN)
    gate = both[:, :ffs]
    up = both[:, ffs:]
    sigma = jax.nn.sigmoid(gate)
    gate_act = gate * sigma
    activated = (gate_act * up).astype(bf16)

    d_act = dot(g_all, wd, NT)
    d_both = jnp.concatenate(
        [d_act * up * sigma * (1.0 + gate * (1.0 - sigma)), d_act * gate_act], -1
    ).astype(bf16)
    if n_ctx == 8:
        arrays = [activated, wd, d_both, wgu, n2_all, g_all]
        down_rows, d_two, grad_gate_up, grad_down = reduce_ctx(
            arrays, ((0, 1, False), (2, 3, True)), ((4, 2), (0, 5)), n_ctx, 4
        )
    else:
        down_rows, grad_down = reduce_ctx(
            [activated, wd, g_all], ((0, 1, False),), ((0, 2),), n_ctx, 4
        )
        d_two, grad_gate_up = reduce_ctx(
            [d_both, wgu, n2_all], ((0, 1, True),), ((2, 0),), n_ctx, 5
        )
    d_two = d_two.astype(f32)
    block_out = (hidden + down_rows.astype(f32)).astype(bf16)[None]
    row_gate_up = lax.psum_scatter(grad_gate_up, "fsdp", scatter_dimension=0, tiled=True)

    grad_norm2 = jnp.sum(d_two * hidden * scale_two, 0)
    d_hidden = cotangent[0].astype(f32) + norm_back(d_two, hidden, scale_two, gain_two)
    d_branch = d_hidden.astype(bf16)
    db_all = gather_ctx([d_branch], n_ctx, 3)[0].reshape(all_rows, width)

    grad_out = dot(mixed_dealt, db_all, TN).astype(bf16)
    wo_rows = lax.dynamic_slice(wo, (me * hw, 0), (hw, width))
    d_mixed = dot(db_all, wo_rows, NT).astype(bf16)
    d_mixed = jnp.take(d_mixed.reshape(pieces, piece, hw), given_from, axis=0)
    d_mixed = d_mixed.reshape(all_rows, hw)
    d_proj = attend_back(
        queries, keys, values, d_mixed, cosine_table, sine_table, first_key, heads
    )
    d_one, grad_qkv = reduce_ctx([d_proj, wq, normed_one], ((0, 1, True),), ((2, 0),), n_ctx, 6)
    d_one = d_one.astype(f32)
    row_qkv = lax.psum_scatter(grad_qkv, "fsdp", scatter_dimension=0, tiled=True)

    own_float = x_own.astype(f32)
    scale_one = rms_scale(own_float)
    grad_norm1 = jnp.sum(d_one * own_float * scale_one, 0)
    dh_own = jnp.take(db_all.reshape(pieces, piece, width), own_given, axis=0)
    dh_own = dh_own.reshape(rows, width).astype(f32)
    grad_tokens = (dh_own + norm_back(d_one, own_float, scale_one, gain_one)).astype(bf16)[None]

    norms = lax.psum_scatter(
        jnp.stack([grad_norm1, grad_norm2]), "fsdp", scatter_dimension=1, tiled=True
    )
    norms = jnp.pad(norms, ((0, 6), (0, 0)))

    grad_rows = jnp.concatenate([grad_down, grad_out], 0)
    grad_rows, row_gate_up = lax.optimization_barrier((grad_rows, row_gate_up))
    col_rows = lax.psum_scatter(grad_rows, "fsdp", scatter_dimension=1, tiled=True)
    all_cols = gather_ctx([col_rows], n_ctx, 9)[0]
    owner_rows = all_cols.reshape(n_fsdp, ratio * (ffs + hw), width // n_fsdp)
    swapped = lax.all_to_all(owner_rows, "fsdp", split_axis=0, concat_axis=0, tiled=True)
    row_gate_up, all_cols = lax.optimization_barrier((row_gate_up, all_cols))
    all_gate_up, all_qkv, all_norms = gather_ctx([row_gate_up, row_qkv, norms], n_ctx, 8)
    final_gate_up = assemble(all_gate_up, 2)
    final_qkv = assemble(all_qkv, 3)
    final_norms = jnp.sum(all_norms, 0)
    final_down, final_out = assemble_rows(swapped, ratio, ffs)
    return (
        block_out,
        grad_tokens,
        final_norms[0],
        final_qkv,
        final_out,
        final_norms[1],
        final_gate_up,
        final_down,
    )


def solution(mesh):
    in_specs = (
        P("fsdp", "ctx", None),
        P("fsdp", "ctx", None),
        P("fsdp", None),
        P("fsdp", None, None),
        P("fsdp"),
        P("fsdp", None),
        P("fsdp", None),
        P("fsdp"),
        P("fsdp", None),
        P("fsdp", None),
    )
    out_specs = (
        P("fsdp", "ctx", None),
        P("fsdp", "ctx", None),
        P("fsdp"),
        P("fsdp", None),
        P("fsdp", None),
        P("fsdp"),
        P("fsdp", None),
        P("fsdp", None),
    )
    return jax.shard_map(shards, mesh=mesh, in_specs=in_specs, out_specs=out_specs, check_vma=False)
```

```python
import functools
import math

import jax
import jax.numpy as jnp
from jax import lax
from jax.experimental import pallas as pl
from jax.experimental.pallas import tpu as pltpu
from jax.sharding import PartitionSpec as P

MESH = pl.DeviceIdType.MESH
LINE = 4

H = 16
HD = 128

epsilon = 1e-06
rope_base = 10000.0
masked_score = -1e30
f32 = jnp.float32
bf16 = jnp.bfloat16


def greet(a, b, n_a, n_b, f, fsdp=False):
    bar = pltpu.get_barrier_semaphore()
    conds = ((a > 0, a - 1, b), (a < n_a - 1, a + 1, b), (b > 0, a, b - 1), (b < n_b - 1, a, b + 1))
    for cond, aa, bb in conds:

        @pl.when(cond)
        def _():
            pl.semaphore_signal(bar, inc=1, device_id=(aa * n_b + bb, f), device_id_type=MESH)

    low = (a + n_a - 1) // n_a + (b + n_b - 1) // n_b
    high = (2 * n_a - 2 - a) // n_a + (2 * n_b - 2 - b) // n_b
    total = low + high
    if fsdp:
        n_f = lax.axis_size("fsdp")
        for m in range(1, n_f):
            pl.semaphore_signal(
                bar, inc=1, device_id=(a * n_b + b, (f + m) % n_f), device_id_type=MESH
            )
        total = total + n_f - 1
    pl.semaphore_wait(bar, total)


def both(*conds):
    out = True
    for cond in conds:
        if cond is not True:
            out = cond if out is True else jnp.logical_and(out, cond)
    return out


def when(cond):
    return (lambda fn: fn()) if cond is True else pl.when(cond)


def plan(rows, cuts=2):
    unit = rows // 16
    if rows % 16 or unit < 4:
        return ((0, rows, False),)
    swapped = max(1, (unit + 4) // 8)
    rest = unit - swapped
    marks = [rest * i // cuts for i in range(cuts + 1)]
    chunks = [(16 * lo, 16 * (hi - lo), False) for lo, hi in zip(marks, marks[1:])]
    return tuple(chunks) + ((16 * rest, 16 * swapped, True),)


def places(n):
    n_a, n_b = LINE, n // LINE
    c = lax.axis_index("ctx")
    return n_a, n_b, c // n_b, c % n_b, lax.axis_index("fsdp")


def gather_steps(n, x, out, chunk, sems):
    n_a, n_b, a, b, f = places(n)
    first, count, swapped = chunk
    s1, r1, s2, r2 = sems
    (p1, n1), (p2, n2) = ((b, n_b), (a, n_a)) if swapped else ((a, n_a), (b, n_b))

    def slot(q1, q2):
        return q2 * n_b + q1 if swapped else q1 * n_b + q2

    rows = pl.ds(first, count)
    below1, above1, below2, above2 = p1 > 0, p1 < n1 - 1, p2 > 0, p2 < n2 - 1

    def copy1(k, d):
        q1 = p1 - k if d == 0 else p1 + k
        to = p1 + 1 if d == 0 else p1 - 1
        return pltpu.make_async_remote_copy(
            src_ref=x.at[rows] if k == 0 else out.at[slot(q1, p2), rows],
            dst_ref=out.at[slot(q1, p2), rows],
            send_sem=s1.at[d, k],
            recv_sem=r1.at[d, k],
            device_id=(slot(to, p2), f),
            device_id_type=MESH,
        )

    def copy2(j, q1, m, d):
        q2 = p2 - m if d == 0 else p2 + m
        to = p2 + 1 if d == 0 else p2 - 1
        return pltpu.make_async_remote_copy(
            src_ref=x.at[rows] if j == 0 and m == 0 else out.at[slot(q1, q2), rows],
            dst_ref=out.at[slot(q1, q2), rows],
            send_sem=s2.at[d, m, j],
            recv_sem=r2.at[d, m, j],
            device_id=(slot(p1, to), f),
            device_id_type=MESH,
        )

    shards = [(0, 0, None, p1, True)]
    for k in range(1, n1):
        shards.append((k, k, 0, p1 - k, p1 >= k))
        shards.append((n1 - 1 + k, k, 1, p1 + k, p1 + k < n1))

    def own():
        for d, cond in ((0, above1), (1, below1)):
            when(cond)(lambda d=d: copy1(0, d).start())
        for d, cond in ((0, above2), (1, below2)):
            when(cond)(lambda d=d: copy2(0, p1, 0, d).start())

    def line1(k):
        for j, kk, side, q1, there in shards:
            if kk != k:
                continue

            @when(there)
            def _():
                copy1(k - 1, side).wait_recv()
                if k < n1 - 1:
                    when(above1 if side == 0 else below1)(lambda: copy1(k, side).start())
                for d, cond in ((0, above2), (1, below2)):
                    when(cond)(lambda d=d: copy2(j, q1, 0, d).start())

    def line2(m):
        for d, there2, onward in ((0, p2 >= m, above2), (1, p2 + m < n2, below2)):
            for j, _, _, q1, there in shards:

                @when(both(there2, there))
                def _():
                    copy2(j, q1, m - 1, d).wait_recv()
                    if m < n2 - 1:
                        when(onward)(lambda: copy2(j, q1, m, d).start())

    def finish():
        for j, k, side, q1, there in shards:
            for d, onward in ((0, above1), (1, below1)):
                if k < n1 - 1 and side in (None, d):
                    when(both(onward, there))(lambda d=d: copy1(k, d).wait_send())
            for m in range(n2 - 1):
                for d, onward, there2 in ((0, above2, p2 >= m), (1, below2, p2 + m < n2)):
                    when(both(onward, there, True if m == 0 else there2))(
                        lambda d=d, m=m: copy2(j, q1, m, d).wait_send()
                    )

    steps = [own]
    steps += [functools.partial(line1, k) for k in range(1, n1)]
    steps += [functools.partial(line2, m) for m in range(1, n2)]
    return steps, finish


def spread_steps(n, x, out, chunk, sems):
    f = lax.axis_index("fsdp")
    c = lax.axis_index("ctx")
    n_f = lax.axis_size("fsdp")
    n_y = n_f // 2
    y, core = f // 2, f % 2
    owner = c // (n // n_f)
    oy, oc = owner // 2, owner % 2
    first, count = chunk
    rows = pl.ds(first, count)
    up, down, side, come = sems

    def copy(own, sem, to):
        return pltpu.make_async_remote_copy(
            src_ref=x.at[rows] if own else out.at[rows],
            dst_ref=out.at[rows],
            send_sem=sem,
            recv_sem=come,
            device_id=(c, to),
            device_id_type=MESH,
        )

    on = core == oc
    ways = (
        (up, f + 2, jnp.logical_and(on, jnp.logical_and(y >= oy, y < n_y - 1))),
        (down, f - 2, jnp.logical_and(on, jnp.logical_and(y <= oy, y > 0))),
        (side, f + 1 - 2 * core, on),
    )

    def own():
        for sem, to, cond in ways:
            pl.when(jnp.logical_and(cond, f == owner))(lambda sem=sem, to=to: copy(True, sem, to).start())

    def onward():
        @pl.when(f != owner)
        def _():
            copy(False, side, f).wait_recv()
            for sem, to, cond in ways:
                pl.when(cond)(lambda sem=sem, to=to: copy(False, sem, to).start())

    def finish():
        for sem, to, cond in ways:
            pl.when(cond)(lambda sem=sem, to=to: copy(False, sem, to).wait_send())

    return own, onward, finish


def gather_sems(chunks):
    sem = pltpu.SemaphoreType.DMA
    return [sem((chunks, 2, 4)), sem((chunks, 2, 4)), sem((chunks, 2, 4, 7)), sem((chunks, 2, 4, 7))]


def gather_kernel(n, plans, spread, *refs):
    count = len(plans)
    k = count + (1 if spread else 0)
    xs, outs = refs[:k], refs[k : 2 * k]
    held = refs[2 * k : 3 * k]
    local, s1, r1, s2, r2, s3 = refs[3 * k :]
    n_a, n_b, a, b, f = places(n)
    c = a * n_b + b
    greet(a, b, n_a, n_b, f, bool(spread))
    steps, ends, at = [], [], 0
    for x, out, chunks in zip(xs, outs, plans):
        for chunk in chunks:
            sems = (s1.at[at], r1.at[at], s2.at[at], r2.at[at])
            more, end = gather_steps(n, x, out, chunk, sems)
            steps.append(more)
            ends.append(end)
            at += 1
    for i, chunk in enumerate(spread):
        begin, onward, end = spread_steps(n, xs[-1], outs[-1], chunk, [s3.at[i, j] for j in range(4)])
        steps.append([begin] + [lambda: None] * (1 + 2 * i) + [onward])
        ends.append(end)
    mine = f == c // (n // lax.axis_size("fsdp"))
    for t in range(max(map(len, steps))):
        for more in steps:
            if t < len(more):
                more[t]()
        if t < 2:
            for i in range(k):
                out = outs[i].at[c] if i < count else outs[i]

                @when(True if i < count else mine)
                def _():
                    fetch = pltpu.make_async_copy(xs[i], held[i], local.at[i])
                    if t == 0:
                        fetch.start()
                    else:
                        fetch.wait()
                        pltpu.make_async_copy(held[i], out, local.at[i]).start()
    for i in range(k):
        out = outs[i].at[c] if i < count else outs[i]
        when(True if i < count else mine)(pltpu.make_async_copy(held[i], out, local.at[i]).wait)
    for end in ends:
        end()


def gather_ctx(xs, n, cid, cuts=2, spread=None):
    plans = tuple(plan(x.shape[0], cuts) for x in xs)
    shapes = [jax.ShapeDtypeStruct((n,) + x.shape, x.dtype) for x in xs]
    parts = ()
    if spread is not None:
        rows = spread.shape[0]
        half = rows // 32 * 16
        parts = ((0, rows),) if rows % 16 else ((0, half), (half, rows - half))
        xs = xs + [spread]
        shapes = shapes + [jax.ShapeDtypeStruct(spread.shape, spread.dtype)]
    return pl.pallas_call(
        functools.partial(gather_kernel, n, plans, parts),
        out_shape=shapes,
        in_specs=[pl.BlockSpec(memory_space=pl.ANY)] * len(xs),
        out_specs=[pl.BlockSpec(memory_space=pl.ANY)] * len(xs),
        scratch_shapes=[pltpu.VMEM(x.shape, x.dtype) for x in xs]
        + [pltpu.SemaphoreType.DMA((len(xs),))]
        + gather_sems(sum(map(len, plans)))
        + [pltpu.SemaphoreType.DMA((2, 4))],
        compiler_params=pltpu.CompilerParams(
            collective_id=cid, has_side_effects=True, vmem_limit_bytes=60 << 20
        ),
        name=f"gather{cid}",
    )(*xs)


def cast_rows(src, dst):
    rows = src.shape[0]
    if rows % 16:
        dst[...] = src[...].astype(dst.dtype)
        return

    def one(i, carry):
        at = pl.ds(pl.multiple_of(i * 16, 16), 16)
        dst[at, :] = src[at, :].astype(dst.dtype)
        return carry

    lax.fori_loop(0, rows // 16, one, 0)


def first_kernel(n, chunks, ratio, *refs):
    x, wo, wd, g, out, wo_out, wd_out, g_out = refs[:8]
    held, wo_wide, wo_low, wd_wide, wd_low, g_held, local, s1, r1, s2, r2, gs, gr = refs[8:]
    n_a, n_b, a, b, f = places(n)
    c = a * n_b + b
    n_f = lax.axis_size("fsdp")
    ffs = wd_low.shape[0]
    own = pl.ds(pl.multiple_of((c % ratio) * ffs, 8), ffs)
    loads = [
        pltpu.make_async_copy(src, dst, local.at[i])
        for i, (src, dst) in enumerate(((x, held), (wo, wo_wide), (wd.at[own], wd_wide), (g, g_held)))
    ]
    stores = [
        pltpu.make_async_copy(src, dst, local.at[i])
        for i, (src, dst) in enumerate(
            ((held, out.at[c]), (wo_low, wo_out), (wd_low, wd_out), (g_held, g_out.at[f]))
        )
    ]
    for copy in loads:
        copy.start()
    greet(a, b, n_a, n_b, f, True)
    steps, ends = [], []
    for i, chunk in enumerate(chunks):
        more, end = gather_steps(n, x, out, chunk, (s1.at[i], r1.at[i], s2.at[i], r2.at[i]))
        steps.append(more)
        ends.append(end)

    def gain(m):
        return pltpu.make_async_remote_copy(
            src_ref=g,
            dst_ref=g_out.at[f],
            send_sem=gs.at[m],
            recv_sem=gr.at[m],
            device_id=(c, (f + m) % n_f),
            device_id_type=MESH,
        )

    for t in range(n_a + n_b - 1):
        for more in steps:
            if t < len(more):
                more[t]()
        if t == 0:
            for m in range(1, n_f):
                gain(m).start()
            loads[0].wait()
            stores[0].start()
            loads[3].wait()
            stores[3].start()
            loads[1].wait()
            cast_rows(wo_wide, wo_low)
            stores[1].start()
        if t == 1:
            loads[2].wait()
            cast_rows(wd_wide, wd_low)
            stores[2].start()
    for copy in stores:
        copy.wait()
    for m in range(1, n_f):
        gain(m).wait()
    for end in ends:
        end()


def gather_first(x, w_out, w_down, gains, n, ratio, ffs, cid):
    n_f = lax.axis_size("fsdp")
    chunks = plan(x.shape[0])
    low = [jax.ShapeDtypeStruct(w_out.shape, bf16), jax.ShapeDtypeStruct((ffs, w_down.shape[1]), bf16)]
    sem = pltpu.SemaphoreType.DMA
    return pl.pallas_call(
        functools.partial(first_kernel, n, chunks, ratio),
        out_shape=[jax.ShapeDtypeStruct((n,) + x.shape, x.dtype)]
        + low
        + [jax.ShapeDtypeStruct((n_f,) + gains.shape, gains.dtype)],
        in_specs=[pl.BlockSpec(memory_space=pl.ANY)] * 4,
        out_specs=[pl.BlockSpec(memory_space=pl.ANY)] * 4,
        scratch_shapes=[
            pltpu.VMEM(x.shape, x.dtype),
            pltpu.VMEM(w_out.shape, f32),
            pltpu.VMEM(w_out.shape, bf16),
            pltpu.VMEM((ffs, w_down.shape[1]), f32),
            pltpu.VMEM((ffs, w_down.shape[1]), bf16),
            pltpu.VMEM(gains.shape, gains.dtype),
            sem((4,)),
        ]
        + gather_sems(len(chunks))
        + [sem((n_f,)), sem((n_f,))],
        compiler_params=pltpu.CompilerParams(
            collective_id=cid, has_side_effects=True, vmem_limit_bytes=60 << 20
        ),
        name=f"gather{cid}",
    )(x, w_out, w_down, gains)


def attend_gather_kernel(n, chunks, heads, block, *refs):
    x, n_hbm, w_hbm, cos_ref, sin_ref, first_ref, order_ref = refs[:7]
    out, q_ref, k_ref, v_ref, dealt_ref, all_ref = refs[7:13]
    held, n_ref, w_ref, mixed, local, s1, r1, s2, r2, sa, ra = refs[13:]
    n_a, n_b, a, b, f = places(n)
    c = a * n_b + b
    all_rows = n_ref.shape[0]
    rows = all_rows // n
    hw = heads * HD
    loads = [
        pltpu.make_async_copy(src, dst, local.at[i])
        for i, (src, dst) in enumerate(((x, held), (n_hbm, n_ref), (w_hbm, w_ref)))
    ]
    for copy in loads:
        copy.start()
    bar = pltpu.get_barrier_semaphore()
    for m in range(1, n):
        pl.semaphore_signal(bar, inc=1, device_id=((c + m) % n, f), device_id_type=MESH)
    pl.semaphore_wait(bar, n - 1)
    steps, ends = [], []
    for i, chunk in enumerate(chunks):
        more, end = gather_steps(n, x, out, chunk, (s1.at[i], r1.at[i], s2.at[i], r2.at[i]))
        steps.append(more)
        ends.append(end)

    def run(t):
        for more in steps:
            if t < len(more):
                more[t]()

    def exchange(m):
        to = (c + m) % n
        return pltpu.make_async_remote_copy(
            src_ref=dealt_ref.at[to],
            dst_ref=all_ref.at[c],
            send_sem=sa.at[m],
            recv_sem=ra.at[m],
            device_id=(to, f),
            device_id_type=MESH,
        )

    def attend_block(at):
        own = slice(at, at + block)
        proj = dot(n_ref[own, :], w_ref[...], NN)
        cos, sin = cos_ref[own, :], sin_ref[own, :]
        for h in range(heads):
            head = slice(h * HD, (h + 1) * HD)
            for ref, base in ((q_ref, 0), (k_ref, hw)):
                u = proj[:, base + h * HD : base + (h + 1) * HD]
                ref[own, head] = (u * cos + turned(u) * sin).astype(bf16)
        v_ref[own, :] = proj[:, 2 * hw :].astype(bf16)
        for h in range(heads):
            head = slice(h * HD, (h + 1) * HD)
            seen = slice(0, at + block)
            probs = masked_probs(q_ref[own, head], k_ref[seen, head], first_ref[own, :], at)
            mixed[own, head] = dot(probs.astype(bf16), v_ref[seen, head], NN).astype(bf16)

    run(0)
    keep = pltpu.make_async_copy(held, out.at[c], local.at[0])
    loads[0].wait()
    keep.start()
    loads[1].wait()
    loads[2].wait()
    for at in range(0, all_rows, block):
        attend_block(at)
        if at + block == all_rows // 2:
            run(1)
    for m in range(n):
        own = slice(m * rows, (m + 1) * rows)
        given = lax.broadcasted_iota(jnp.int32, (rows, all_rows), 1)
        picks = jnp.where(given == order_ref[own, :], 1.0, 0.0).astype(bf16)
        dealt_ref[m] = dot(picks, mixed[...], NN).astype(bf16)
    for m in range(1, n):
        exchange(m).start()
    mine = pltpu.make_async_copy(dealt_ref.at[c], all_ref.at[c], local.at[1])
    mine.start()
    for t in range(2, n_a + n_b - 1):
        run(t)
    keep.wait()
    mine.wait()
    for m in range(1, n):
        exchange(m).wait()
    for end in ends:
        end()


def attend_gather(x, normed, wq, cos, sin, first, order, heads, n, cid, block=256):
    all_rows = normed.shape[0]
    rows = all_rows // n
    hw = heads * HD
    chunks = plan(x.shape[0])
    one = jax.ShapeDtypeStruct((all_rows, hw), bf16)
    split = jax.ShapeDtypeStruct((n, rows, hw), bf16)
    hbm = pl.BlockSpec(memory_space=pl.ANY)
    vmem = pl.BlockSpec(memory_space=pltpu.VMEM)
    sem = pltpu.SemaphoreType.DMA
    return pl.pallas_call(
        functools.partial(attend_gather_kernel, n, chunks, heads, block),
        out_shape=[jax.ShapeDtypeStruct((n,) + x.shape, x.dtype), one, one, one, split, split],
        in_specs=[hbm] * 3 + [vmem] * 4,
        out_specs=[hbm] + [vmem] * 4 + [hbm],
        scratch_shapes=[
            pltpu.VMEM(x.shape, x.dtype),
            pltpu.VMEM(normed.shape, bf16),
            pltpu.VMEM(wq.shape, bf16),
            pltpu.VMEM((all_rows, hw), bf16),
            sem((3,)),
        ]
        + gather_sems(len(chunks))
        + [sem((n,)), sem((n,))],
        compiler_params=pltpu.CompilerParams(
            collective_id=cid, has_side_effects=True, vmem_limit_bytes=60 << 20
        ),
        name=f"attend{cid}",
    )(x, normed, wq, cos, sin, first, order)


def back_gather_kernel(n, chunks, heads, block, *refs):
    x, db_hbm, wo_hbm, down_hbm, q_ref, k_ref, v_ref, mixed_ref = refs[:8]
    cos_ref, sin_ref, first_ref, order_ref = refs[8:12]
    out, proj_ref, rows_hbm = refs[12:15]
    held, db, wo, down, rows_ref, dealt, given, dk_ref, dv_ref, local, s1, r1, s2, r2 = refs[15:]
    n_a, n_b, a, b, f = places(n)
    c = a * n_b + b
    hw = heads * HD
    all_rows = db.shape[0]
    part = all_rows // n
    ffs = down.shape[0]
    own_rows = pl.ds(pl.multiple_of(c * hw, hw), hw)
    loads = [
        pltpu.make_async_copy(src, dst, local.at[i])
        for i, (src, dst) in enumerate(((x, held), (db_hbm, db), (wo_hbm.at[own_rows], wo), (down_hbm, down)))
    ]
    for copy in loads:
        copy.start()
    greet(a, b, n_a, n_b, f)
    steps, ends = [], []
    for i, chunk in enumerate(chunks):
        more, end = gather_steps(n, x, out, chunk, (s1.at[i], r1.at[i], s2.at[i], r2.at[i]))
        steps.append(more)
        ends.append(end)

    def run(t):
        for more in steps:
            if t < len(more):
                more[t]()

    run(0)
    keep = pltpu.make_async_copy(held, out.at[c], local.at[0])
    loads[0].wait()
    keep.start()
    for copy in loads[1:]:
        copy.wait()
    dealt[...] = dot(db[...], wo[...], NT).astype(bf16)
    for m in range(n):
        own = slice(m * part, (m + 1) * part)
        slots = lax.broadcasted_iota(jnp.int32, (part, all_rows), 1)
        picks = jnp.where(slots == order_ref[own, :], 1.0, 0.0).astype(bf16)
        given[own, :] = dot(picks, dealt[...], NN).astype(bf16)
    rows_ref[:ffs, :] = down[...]
    rows_ref[ffs:, :] = dot(mixed_ref[...], db[...], TN).astype(bf16)
    stored = pltpu.make_async_copy(rows_ref, rows_hbm, local.at[1])
    stored.start()
    attend_back_kernel(
        heads, block, q_ref, k_ref, v_ref, given, cos_ref, sin_ref, first_ref, proj_ref, dk_ref, dv_ref
    )
    for t in range(1, n_a + n_b - 1):
        run(t)
    keep.wait()
    stored.wait()
    for end in ends:
        end()


def back_gather(x, db, wo, down, q, k, v, mixed, cos, sin, first, order, heads, n, cid, block=256):
    all_rows, width = db.shape
    hw = heads * HD
    chunks = plan(x.shape[0])
    hbm = pl.BlockSpec(memory_space=pl.ANY)
    vmem = pl.BlockSpec(memory_space=pltpu.VMEM)
    both_rows = (down.shape[0] + hw, width)
    return pl.pallas_call(
        functools.partial(back_gather_kernel, n, chunks, heads, block),
        out_shape=[
            jax.ShapeDtypeStruct((n,) + x.shape, x.dtype),
            jax.ShapeDtypeStruct((all_rows, 3 * hw), bf16),
            jax.ShapeDtypeStruct(both_rows, bf16),
        ],
        in_specs=[hbm] * 4 + [vmem] * 8,
        out_specs=[hbm, vmem, hbm],
        scratch_shapes=[
            pltpu.VMEM(x.shape, x.dtype),
            pltpu.VMEM(db.shape, bf16),
            pltpu.VMEM((hw, width), bf16),
            pltpu.VMEM(down.shape, bf16),
            pltpu.VMEM(both_rows, bf16),
            pltpu.VMEM((all_rows, hw), bf16),
            pltpu.VMEM((all_rows, hw), bf16),
            pltpu.VMEM((all_rows, HD), f32),
            pltpu.VMEM((all_rows, HD), f32),
            pltpu.SemaphoreType.DMA((4,)),
        ]
        + gather_sems(len(chunks)),
        compiler_params=pltpu.CompilerParams(
            collective_id=cid, has_side_effects=True, vmem_limit_bytes=60 << 20
        ),
        name=f"back{cid}",
    )(x, db, wo, down, q, k, v, mixed, cos, sin, first, order)


def order_of(p, n):
    if n == 2:
        return (1 - p, p)
    h = p // 2
    return (3 - 3 * h, 2 - h, 1 - p + 4 * h, p)


def reduce_steps(n, part, chunk, bufs, sems):
    n_a, n_b, a, b, f = places(n)
    first, count, swapped = chunk
    g1, g2 = bufs
    s1, r1, s2, r2 = sems
    (p1, n1), (p2, n2) = ((a, n_a), (b, n_b)) if swapped else ((b, n_b), (a, n_a))

    def slot(q1, q2):
        return q1 * n_b + q2 if swapped else q2 * n_b + q1

    rows = pl.ds(first, count)
    from1 = (p1 > 0, p1 < n1 - 1)
    from2 = (p2 > 0, p2 < n2 - 1)
    targets = order_of(p2, n2)

    def has1(d, k):
        return (p1 + k < n1) if d == 0 else (p1 >= k)

    def add(t, got):
        mine = part.at[t, rows]
        mine[...] = (mine[...].astype(f32) + got[...].astype(f32)).astype(mine.dtype)

    def remote(src, dst, send, recv, to):
        return pltpu.make_async_remote_copy(
            src_ref=src, dst_ref=dst, send_sem=send, recv_sem=recv, device_id=(to, f), device_id_type=MESH
        )

    def side1(d):
        return d if n1 > 2 else 0

    def copy1(j, d, k):
        t = p1 + k if d == 0 else p1 - k
        to = p1 + 1 if d == 0 else p1 - 1
        src = part.at[slot(t, targets[j]), rows]
        return remote(src, g1.at[side1(d), k - 1, j], s1.at[d, k, j], r1.at[d, k - 1, j], slot(to, p2))

    def come1(j, d, k):
        src = part.at[slot(p1, p2), rows]
        return remote(src, g1.at[side1(d), k, j], s1.at[d, k, j], r1.at[d, k, j], slot(p1, p2))

    def copy2(t, d):
        k = t - p2 if d == 0 else p2 - t
        to = p2 + 1 if d == 0 else p2 - 1
        return remote(
            part.at[slot(p1, t), rows], g2.at[d, k - 1], s2.at[d, k], r2.at[d, k - 1], slot(p1, to)
        )

    def come2(d, k):
        src = part.at[slot(p1, p2), rows]
        return remote(src, g2.at[d, k], s2.at[d, k], r2.at[d, k], slot(p1, p2))

    def start(j):
        for d in (0, 1) if j < n2 else ():
            for k in range(n1 - 1, 0, -1):
                when(both(has1(d, k), jnp.logical_not(from1[d])))(
                    lambda d=d, k=k: copy1(j, d, k).start()
                )

    def middle1(j, k):
        for d in (0, 1):

            @when(both(has1(d, k), from1[d]))
            def _():
                come1(j, d, k).wait_recv()
                add(slot(p1 + k if d == 0 else p1 - k, targets[j]), g1.at[side1(d), k, j])
                copy1(j, d, k).start()

    def last1(j):
        for d in (0, 1):

            @when(from1[d])
            def _():
                come1(j, d, 0).wait_recv()
                add(slot(p1, targets[j]), g1.at[side1(d), 0, j])

    def line2(j):
        t = targets[j]
        for d in (0, 1):

            @when((t > p2) if d == 0 else (t < p2))
            def _():
                @when(from2[d])
                def _():
                    k = t - p2 if d == 0 else p2 - t
                    come2(d, k).wait_recv()
                    add(slot(p1, t), g2.at[d, k])

                copy2(t, d).start()

    def last2():
        for d in (0, 1):

            @when(from2[d])
            def _():
                come2(d, 0).wait_recv()
                add(slot(p1, p2), g2.at[d, 0])

    steps = []
    if swapped:
        for k in range(n1 - 2, 0, -1):
            steps.append(lambda k=k: [middle1(j, k) for j in range(n2)])
        steps.append(lambda: [(last1(j), line2(j) if j < n2 - 1 else None) for j in range(n2)])
        steps.append(last2)
    else:

        def item(j):
            for k in range(n1 - 2, 0, -1):
                middle1(j, k)
            last1(j)
            if j < n2 - 1:
                line2(j)

        steps += [functools.partial(item, j) for j in range(n2)] + [last2]

    def finish():
        for j in range(n2):
            for d in (0, 1):
                for k in range(n1 - 1, 0, -1):
                    when(has1(d, k))(lambda j=j, d=d, k=k: copy1(j, d, k).wait_send())
                if j < n2 - 1:
                    t = targets[j]
                    when((t > p2) if d == 0 else (t < p2))(lambda t=t, d=d: copy2(t, d).wait_send())

    return start, steps, finish


def reduce_kernel(n, chunks, jobs, extras, count, *refs):
    n_a, n_b, a, b, f = places(n)
    k, e = len(jobs), len(extras)
    hbm, rest = refs[:count], refs[count:]
    o_refs, p_refs, rest = rest[:k], rest[k : k + e], rest[k + e :]
    held, parts, made, rest = rest[:count], rest[count : count + k], rest[count + k : count + k + e], rest[count + k + e :]
    cuts = len(chunks)
    bufs, rest = rest[: 2 * k * cuts], rest[2 * k * cuts :]
    load, stored, s1, r1, s2, r2 = rest
    rows = o_refs[0].shape[0]
    first = sorted({i for x, w, _ in jobs for i in (x, w)})
    order_in = first + [i for i in range(count) if i not in first]
    loads = [pltpu.make_async_copy(hbm[i], held[i], load.at[i]) for i in range(count)]
    for i in order_in:
        loads[i].start()
    todo = []
    for i in range(k):
        for m, chunk in enumerate(chunks):
            at = i * cuts + m
            sems = (s1.at[at], r1.at[at], s2.at[at], r2.at[at])
            todo.append(reduce_steps(n, parts[i], chunk, bufs[2 * at : 2 * at + 2], sems))

    def term(i, t):
        x, w, nt = jobs[i]
        at = pl.multiple_of(t * rows, rows)
        parts[i][t] = dot(held[x][pl.ds(at, rows), :], held[w][...], NT if nt else NN).astype(bf16)

    tiles, stores = [], []
    for i, (x, y) in enumerate(extras):
        high = held[x].shape[1]
        for lo in range(0, high, 256):
            hi = min(lo + 256, high)

            def tile(i=i, x=x, y=y, lo=lo, hi=hi):
                made[i][lo:hi, :] = dot(held[x][:, lo:hi], held[y][...], TN).astype(bf16)

            tiles.append(tile)
        stores.append((len(tiles), i))

    order = order_of(a, n_a)
    greet(a, b, n_a, n_b, f)
    for i in first:
        loads[i].wait()
    for j in range(n_a):
        for i in range(k):
            for m in range(1, n_b):
                term(i, order[j] * n_b + (b + m) % n_b)
            for start, _, _ in todo[i * cuts : (i + 1) * cuts]:
                start(j)
    for i in order_in[len(first) :]:
        loads[i].wait()
    done = 0
    for j in range(n_a):
        for i in range(k):
            term(i, order[j] * n_b + b)
        upto = len(tiles) * (j + 1) // n_a
        for at in range(done, upto):
            tiles[at]()
            for last, i in stores:
                if last == at + 1:
                    pltpu.make_async_copy(made[i], p_refs[i], stored.at[i]).start()
        done = upto
        for _, steps, _ in todo:
            steps[j]()
    for _, steps, _ in todo:
        steps[n_a]()
    for i in range(k):
        o_refs[i][...] = parts[i][a * n_b + b]
    for _, _, finish in todo:
        finish()
    for i in range(e):
        pltpu.make_async_copy(made[i], p_refs[i], stored.at[i]).wait()


def reduce_ctx(arrays, jobs, extras, n, cid):
    n_a, n_b = LINE, n // LINE
    rows = arrays[jobs[0][0]].shape[0] // n
    half = rows // 2
    chunks = ((0, half, False), (half, half, False))
    widths = [arrays[w].shape[0 if nt else 1] for _, w, nt in jobs]
    bufs = []
    for width in widths:
        for _, count, _ in chunks:
            bufs += [
                pltpu.VMEM((min(2, n_b - 1), n_b - 1, n_a, count, width), bf16),
                pltpu.VMEM((2, n_a - 1, count, width), bf16),
            ]
    made = [(arrays[x].shape[1], arrays[y].shape[1]) for x, y in extras]
    sem = pltpu.SemaphoreType.DMA
    k = len(jobs) * len(chunks)
    return pl.pallas_call(
        functools.partial(reduce_kernel, n, chunks, jobs, extras, len(arrays)),
        out_shape=[jax.ShapeDtypeStruct((rows, width), bf16) for width in widths]
        + [jax.ShapeDtypeStruct(shape, bf16) for shape in made],
        in_specs=[pl.BlockSpec(memory_space=pl.ANY)] * len(arrays),
        out_specs=[pl.BlockSpec(memory_space=pltpu.VMEM)] * len(widths)
        + [pl.BlockSpec(memory_space=pl.ANY)] * len(made),
        scratch_shapes=[pltpu.VMEM(x.shape, x.dtype) for x in arrays]
        + [pltpu.VMEM((n, rows, width), bf16) for width in widths]
        + [pltpu.VMEM(shape, bf16) for shape in made]
        + bufs
        + [sem((len(arrays),)), sem((max(1, len(made)),))]
        + [sem((k, 2, 4, 4)), sem((k, 2, 4, 4)), sem((k, 2, 4)), sem((k, 2, 4))],
        compiler_params=pltpu.CompilerParams(
            collective_id=cid, has_side_effects=True, vmem_limit_bytes=60 << 20
        ),
        name=f"reduce{cid}",
    )(*arrays)


def assemble_rows(parts, ratio, ffs):
    n, rows, w = parts.shape
    each = rows // ratio
    hw = each - ffs

    def body(i_ref, down_ref, out_ref):
        for j in range(ratio):
            down_ref[j * ffs : (j + 1) * ffs, :] = i_ref[0, j * each : j * each + ffs, :].astype(f32)
            out_ref[j * hw : (j + 1) * hw, :] = i_ref[0, j * each + ffs : (j + 1) * each, :].astype(f32)

    return pl.pallas_call(
        body,
        grid=(n,),
        out_shape=[
            jax.ShapeDtypeStruct((ratio * ffs, n * w), f32),
            jax.ShapeDtypeStruct((ratio * hw, n * w), f32),
        ],
        in_specs=[pl.BlockSpec((1, rows, w), lambda i: (i, 0, 0))],
        out_specs=[
            pl.BlockSpec((ratio * ffs, w), lambda i: (0, i)),
            pl.BlockSpec((ratio * hw, w), lambda i: (0, i)),
        ],
        compiler_params=pltpu.CompilerParams(vmem_limit_bytes=60 << 20),
        name="assemble_rows",
    )(parts)


def assemble(parts, n_groups, block=64):
    n, rows, gw = parts.shape
    w = gw // n_groups

    def body(i_ref, o_ref):
        for g in range(n_groups):
            for c in range(n):
                o_ref[:, (g * n + c) * w:(g * n + c + 1) * w] = i_ref[c, :, g * w:(g + 1) * w].astype(jnp.float32)

    return pl.pallas_call(
        body, grid=(rows // block,),
        out_shape=jax.ShapeDtypeStruct((rows, n * gw), jnp.float32),
        in_specs=[pl.BlockSpec((n, block, gw), lambda i: (0, i, 0))],
        out_specs=pl.BlockSpec((block, n * gw), lambda i: (i, 0)),
        compiler_params=pltpu.CompilerParams(vmem_limit_bytes=60 << 20),
        name="assemble")(parts)


def dot(a, b, dims):
    return lax.dot_general(a, b, (dims, ((), ())), preferred_element_type=f32)


NN = ((1,), (0,))
NT = ((1,), (1,))
TN = ((0,), (0,))


def turned(u):
    return pltpu.roll(u, HD // 2, 1)


def masked_probs(q, k, first, at):
    logits = dot(q, k, NT) * (1.0 / math.sqrt(HD))
    keys = lax.broadcasted_iota(jnp.int32, logits.shape, 1)
    queries = lax.broadcasted_iota(jnp.int32, logits.shape, 0) + at
    scaled = jnp.where((keys <= queries) & (keys >= first), logits, masked_score)
    raised = jnp.exp(scaled - jnp.max(scaled, -1, keepdims=True))
    return raised / jnp.sum(raised, -1, keepdims=True)


def attend_back_kernel(
    heads, block, q_ref, k_ref, v_ref, d_ref, cos_ref, sin_ref, first_ref, o_ref, dk_ref, dv_ref
):
    rows = q_ref.shape[0]
    hw = heads * HD

    def back(w, own):
        return (w * cos_ref[own, :] - turned(w) * sin_ref[own, :]).astype(bf16)

    for h in range(heads):
        head = slice(h * HD, (h + 1) * HD)
        for at in reversed(range(0, rows, block)):
            own = slice(at, at + block)
            seen = slice(0, at + block)
            q, k, v, d = q_ref[own, head], k_ref[seen, head], v_ref[seen, head], d_ref[own, head]
            probs = masked_probs(q, k, first_ref[own, :], at)
            d_probs = dot(d, v, NT)
            inner = jnp.sum(probs * d_probs, -1, keepdims=True)
            d_scores = (probs * (d_probs - inner) * (1.0 / math.sqrt(HD))).astype(bf16)
            o_ref[own, head] = back(dot(d_scores, k, NN), own)
            dk = dot(d_scores, q, TN)
            dv = dot(probs.astype(bf16), d, TN)
            if at + block == rows:
                dk_ref[...] = dk
                dv_ref[...] = dv
            else:
                dk_ref[seen, :] += dk
                dv_ref[seen, :] += dv
        every = slice(0, rows)
        o_ref[:, hw + h * HD : hw + (h + 1) * HD] = back(dk_ref[...], every)
        o_ref[:, 2 * hw + h * HD : 2 * hw + (h + 1) * HD] = dv_ref[...].astype(bf16)


def rope_tables(within):
    freq_index = jnp.arange(HD // 2, dtype=f32)
    inverse = rope_base ** (-2.0 * freq_index / HD)
    angles = within.astype(f32)[:, None] * inverse[None, :]
    cos, sin = jnp.cos(angles), jnp.sin(angles)
    return jnp.concatenate([cos, cos], -1), jnp.concatenate([-sin, sin], -1)


def rms_scale(values):
    return lax.rsqrt(jnp.mean(values * values, -1, keepdims=True) + epsilon)


def norm_back(grad_norm, values, scale_rows, gain_float):
    scaled = grad_norm * gain_float[None, :]
    cubed = scale_rows * scale_rows * scale_rows
    return scale_rows * scaled - values * cubed * jnp.mean(scaled * values, -1, keepdims=True)


def shards(
    tokens, cotangent, lengths, deal, norm1_gain, w_qkv, w_out, norm2_gain, w_gate_up, w_down
):
    n_ctx = lax.axis_size("ctx")
    n_fsdp = lax.axis_size("fsdp")
    me = lax.axis_index("ctx")
    mine = lax.axis_index("fsdp")
    rows = tokens.shape[1]
    width = tokens.shape[2]
    piece = rows // n_ctx
    all_rows = rows * n_ctx
    pieces = all_rows // piece
    heads = H // n_ctx
    hw = heads * HD
    kr = w_qkv.shape[0]
    ff = w_gate_up.shape[1] // 2
    ffs = ff // n_ctx
    ff_rows = w_down.shape[0]
    ratio = n_ctx // n_fsdp

    x_own = tokens[0]
    gains = jnp.pad(jnp.stack([norm1_gain, norm2_gain]), ((0, 6), (0, 0)))
    x_all, wo_own, down_own, gains = gather_first(
        x_own, w_out, w_down, gains, n_ctx, ratio, ffs, 0
    )
    x_all = x_all.reshape(all_rows, width)

    qkv_own = jnp.concatenate(
        [lax.dynamic_slice(w_qkv, (0, i * width + me * hw), (kr, hw)) for i in range(3)], -1
    )
    wq = lax.all_gather(qkv_own.astype(bf16), "fsdp", axis=0, tiled=True)
    gain_one = gains[:, 0].reshape(width).astype(bf16).astype(f32)
    gain_two = gains[:, 1].reshape(width).astype(bf16).astype(f32)
    wo = lax.all_gather(wo_own, "fsdp", axis=0, tiled=True)
    wg_own = jnp.concatenate(
        [
            lax.dynamic_slice(w_gate_up, (0, me * ffs), (kr, ffs)),
            lax.dynamic_slice(w_gate_up, (0, ff + me * ffs), (kr, ffs)),
        ],
        -1,
    ).astype(bf16)
    wgu = lax.all_gather(wg_own, "fsdp", axis=0, tiled=True)

    deal_table = deal[0]
    device_index = jnp.arange(n_ctx, dtype=jnp.int32)
    marks = (deal_table[:, :, None] == device_index[None, None, :]).astype(jnp.int32)
    source_piece = jnp.sum(marks * device_index[None, :, None], 1)
    dealt_from = (device_index[None, :] * n_ctx + source_piece.T).reshape(pieces)
    given_from = (deal_table * n_ctx + device_index[:, None]).reshape(pieces)
    own_dealt = lax.dynamic_slice(dealt_from, (me * n_ctx,), (n_ctx,))
    own_given = lax.dynamic_slice(given_from, (me * n_ctx,), (n_ctx,))
    places = jnp.arange(all_rows, dtype=jnp.int32)
    doc_lengths = lengths[0]
    ends = jnp.cumsum(doc_lengths)
    starts = ends - doc_lengths
    docs = jnp.sum((places[:, None] >= ends[None, :]).astype(jnp.int32), -1)
    doc_index = jnp.arange(doc_lengths.shape[0], dtype=jnp.int32)
    firsts = jnp.sum(jnp.where(docs[:, None] == doc_index[None, :], starts[None, :], 0), -1)
    within = places - firsts
    first_key = firsts[:, None]
    cosine_table, sine_table = rope_tables(within)

    x_float = x_all.astype(f32)
    normed_one = (x_float * rms_scale(x_float) * gain_one[None, :]).astype(bf16)
    order = (dealt_from[:, None] * piece + jnp.arange(piece, dtype=jnp.int32)).reshape(all_rows, 1)
    g_all, queries, keys, values, mixed_dealt, mixed_own = attend_gather(
        cotangent[0], normed_one, wq, cosine_table, sine_table, first_key, order, heads, n_ctx, 1
    )
    g_all = g_all.reshape(all_rows, width)
    mixed_own = mixed_own.transpose(1, 0, 2).reshape(rows, width)
    mixed_dealt = mixed_dealt.reshape(all_rows, hw)

    x_dealt = jnp.take(x_all.reshape(pieces, piece, width), own_dealt, axis=0)
    hidden = x_dealt.reshape(rows, width).astype(f32) + dot(mixed_own, wo, NN)
    scale_two = rms_scale(hidden)
    normed_two = (hidden * scale_two * gain_two[None, :]).astype(bf16)
    n2_all, wd = gather_ctx([normed_two], n_ctx, 2, spread=down_own)
    n2_all = n2_all.reshape(all_rows, width)

    both = dot(n2_all, wgu, NN)
    gate = both[:, :ffs]
    up = both[:, ffs:]
    sigma = jax.nn.sigmoid(gate)
    gate_act = gate * sigma
    activated = (gate_act * up).astype(bf16)

    d_act = dot(g_all, wd, NT)
    d_both = jnp.concatenate(
        [d_act * up * sigma * (1.0 + gate * (1.0 - sigma)), d_act * gate_act], -1
    ).astype(bf16)
    if n_ctx == 8:
        arrays = [activated, wd, d_both, wgu, n2_all, g_all]
        down_rows, d_two, grad_gate_up, grad_down = reduce_ctx(
            arrays, ((0, 1, False), (2, 3, True)), ((4, 2), (0, 5)), n_ctx, 4
        )
    else:
        down_rows, grad_down = reduce_ctx(
            [activated, wd, g_all], ((0, 1, False),), ((0, 2),), n_ctx, 4
        )
        d_two, grad_gate_up = reduce_ctx(
            [d_both, wgu, n2_all], ((0, 1, True),), ((2, 0),), n_ctx, 5
        )
    d_two = d_two.astype(f32)
    block_out = (hidden + down_rows.astype(f32)).astype(bf16)[None]
    row_gate_up = lax.psum_scatter(grad_gate_up, "fsdp", scatter_dimension=0, tiled=True)

    grad_norm2 = jnp.sum(d_two * hidden * scale_two, 0)
    d_hidden = cotangent[0].astype(f32) + norm_back(d_two, hidden, scale_two, gain_two)
    d_branch = d_hidden.astype(bf16)
    db_all = gather_ctx([d_branch], n_ctx, 3)[0].reshape(all_rows, width)

    order_back = (given_from[:, None] * piece + jnp.arange(piece, dtype=jnp.int32)).reshape(
        all_rows, 1
    )
    all_gate_up, d_proj, grad_rows = back_gather(
        row_gate_up,
        db_all,
        wo,
        grad_down,
        queries,
        keys,
        values,
        mixed_dealt,
        cosine_table,
        sine_table,
        first_key,
        order_back,
        heads,
        n_ctx,
        7,
    )
    d_one, grad_qkv = reduce_ctx([d_proj, wq, normed_one], ((0, 1, True),), ((2, 0),), n_ctx, 6)
    d_one = d_one.astype(f32)
    row_qkv = lax.psum_scatter(grad_qkv, "fsdp", scatter_dimension=0, tiled=True)

    own_float = x_own.astype(f32)
    scale_one = rms_scale(own_float)
    grad_norm1 = jnp.sum(d_one * own_float * scale_one, 0)
    dh_own = jnp.take(db_all.reshape(pieces, piece, width), own_given, axis=0)
    dh_own = dh_own.reshape(rows, width).astype(f32)
    grad_tokens = (dh_own + norm_back(d_one, own_float, scale_one, gain_one)).astype(bf16)[None]

    norms = lax.psum_scatter(
        jnp.stack([grad_norm1, grad_norm2]), "fsdp", scatter_dimension=1, tiled=True
    )
    norms = jnp.pad(norms, ((0, 6), (0, 0)))

    col_rows = lax.psum_scatter(grad_rows, "fsdp", scatter_dimension=1, tiled=True)
    all_cols = gather_ctx([col_rows], n_ctx, 9)[0]
    owner_rows = all_cols.reshape(n_fsdp, ratio * (ffs + hw), width // n_fsdp)
    swapped = lax.all_to_all(owner_rows, "fsdp", split_axis=0, concat_axis=0, tiled=True)
    row_qkv, all_cols = lax.optimization_barrier((row_qkv, all_cols))
    all_qkv, all_norms = gather_ctx([row_qkv, norms], n_ctx, 8)
    final_gate_up = assemble(all_gate_up, 2)
    final_qkv = assemble(all_qkv, 3)
    final_norms = jnp.sum(all_norms, 0)
    final_down, final_out = assemble_rows(swapped, ratio, ffs)
    return (
        block_out,
        grad_tokens,
        final_norms[0],
        final_qkv,
        final_out,
        final_norms[1],
        final_gate_up,
        final_down,
    )


def solution(mesh):
    in_specs = (
        P("fsdp", "ctx", None),
        P("fsdp", "ctx", None),
        P("fsdp", None),
        P("fsdp", None, None),
        P("fsdp"),
        P("fsdp", None),
        P("fsdp", None),
        P("fsdp"),
        P("fsdp", None),
        P("fsdp", None),
    )
    out_specs = (
        P("fsdp", "ctx", None),
        P("fsdp", "ctx", None),
        P("fsdp"),
        P("fsdp", None),
        P("fsdp", None),
        P("fsdp"),
        P("fsdp", None),
        P("fsdp", None),
    )
    return jax.shard_map(shards, mesh=mesh, in_specs=in_specs, out_specs=out_specs, check_vma=False)
```

```python
import functools
import math

import jax
import jax.numpy as jnp
from jax import lax
from jax.experimental import pallas as pl
from jax.experimental.pallas import tpu as pltpu
from jax.sharding import PartitionSpec as P

MESH = pl.DeviceIdType.MESH
LINE = 4

H = 16
HD = 128

epsilon = 1e-06
rope_base = 10000.0
masked_score = -1e30
f32 = jnp.float32
bf16 = jnp.bfloat16


def greet(a, b, n_a, n_b, f, fsdp=False):
    bar = pltpu.get_barrier_semaphore()
    conds = ((a > 0, a - 1, b), (a < n_a - 1, a + 1, b), (b > 0, a, b - 1), (b < n_b - 1, a, b + 1))
    for cond, aa, bb in conds:

        @pl.when(cond)
        def _():
            pl.semaphore_signal(bar, inc=1, device_id=(aa * n_b + bb, f), device_id_type=MESH)

    low = (a + n_a - 1) // n_a + (b + n_b - 1) // n_b
    high = (2 * n_a - 2 - a) // n_a + (2 * n_b - 2 - b) // n_b
    total = low + high
    if fsdp:
        n_f = lax.axis_size("fsdp")
        for m in range(1, n_f):
            pl.semaphore_signal(
                bar, inc=1, device_id=(a * n_b + b, (f + m) % n_f), device_id_type=MESH
            )
        total = total + n_f - 1
    pl.semaphore_wait(bar, total)


def both(*conds):
    out = True
    for cond in conds:
        if cond is not True:
            out = cond if out is True else jnp.logical_and(out, cond)
    return out


def when(cond):
    return (lambda fn: fn()) if cond is True else pl.when(cond)


def plan(rows, cuts=2):
    unit = rows // 16
    if rows % 16 or unit < 4:
        return ((0, rows, False),)
    swapped = max(1, (unit + 4) // 8)
    rest = unit - swapped
    marks = [rest * i // cuts for i in range(cuts + 1)]
    chunks = [(16 * lo, 16 * (hi - lo), False) for lo, hi in zip(marks, marks[1:])]
    return tuple(chunks) + ((16 * rest, 16 * swapped, True),)


def places(n):
    n_a, n_b = LINE, n // LINE
    c = lax.axis_index("ctx")
    return n_a, n_b, c // n_b, c % n_b, lax.axis_index("fsdp")


def gather_steps(n, x, out, chunk, sems, late=None):
    n_a, n_b, a, b, f = places(n)
    first, count, swapped = chunk
    s1, r1, s2, r2 = sems
    (p1, n1), (p2, n2) = ((b, n_b), (a, n_a)) if swapped else ((a, n_a), (b, n_b))

    def slot(q1, q2):
        return q2 * n_b + q1 if swapped else q1 * n_b + q2

    rows = pl.ds(first, count)
    below1, above1, below2, above2 = p1 > 0, p1 < n1 - 1, p2 > 0, p2 < n2 - 1

    def copy1(k, d):
        q1 = p1 - k if d == 0 else p1 + k
        to = p1 + 1 if d == 0 else p1 - 1
        return pltpu.make_async_remote_copy(
            src_ref=x.at[rows] if k == 0 else out.at[slot(q1, p2), rows],
            dst_ref=out.at[slot(q1, p2), rows],
            send_sem=s1.at[d, k],
            recv_sem=r1.at[d, k],
            device_id=(slot(to, p2), f),
            device_id_type=MESH,
        )

    def copy2(j, q1, m, d):
        q2 = p2 - m if d == 0 else p2 + m
        to = p2 + 1 if d == 0 else p2 - 1
        return pltpu.make_async_remote_copy(
            src_ref=x.at[rows] if j == 0 and m == 0 else out.at[slot(q1, q2), rows],
            dst_ref=out.at[slot(q1, q2), rows],
            send_sem=s2.at[d, m, j],
            recv_sem=r2.at[d, m, j],
            device_id=(slot(p1, to), f),
            device_id_type=MESH,
        )

    shards = [(0, 0, None, p1, True)]
    for k in range(1, n1):
        shards.append((k, k, 0, p1 - k, p1 >= k))
        shards.append((n1 - 1 + k, k, 1, p1 + k, p1 + k < n1))

    def own():
        for d, cond in ((0, above1), (1, below1)):
            when(cond)(lambda d=d: copy1(0, d).start())
        for d, cond in ((0, above2), (1, below2)):
            when(cond)(lambda d=d: copy2(0, p1, 0, d).start())

    def line1(k):
        for j, kk, side, q1, there in shards:
            if kk != k:
                continue

            @when(there)
            def _():
                copy1(k - 1, side).wait_recv()
                if k < n1 - 1:
                    when(above1 if side == 0 else below1)(lambda: copy1(k, side).start())
                for d, cond in ((0, above2), (1, below2)):
                    when(cond)(lambda d=d: copy2(j, q1, 0, d).start())

    def arrive2(m, d, onward, j, q1):
        copy2(j, q1, m - 1, d).wait_recv()
        if m < n2 - 1:
            when(onward)(lambda: copy2(j, q1, m, d).start())

    def arrivals2(m):
        return [
            (both(there2, there), functools.partial(arrive2, m, d, onward, j, q1), m, d, k < 2)
            for j, k, _, q1, there in shards
            for d, there2, onward in ((0, p2 >= m, above2), (1, p2 + m < n2, below2))
        ]

    def line2(m):
        for cond, arrive, _, _, _ in arrivals2(m):
            when(cond)(arrive)

    if late is not None:
        for m in range(1, n2):
            late.extend(arrivals2(m))

    def finish():
        for j, k, side, q1, there in shards:
            for d, onward in ((0, above1), (1, below1)):
                if k < n1 - 1 and side in (None, d):
                    when(both(onward, there))(lambda d=d: copy1(k, d).wait_send())
            for m in range(n2 - 1):
                for d, onward, there2 in ((0, above2, p2 >= m), (1, below2, p2 + m < n2)):
                    when(both(onward, there, True if m == 0 else there2))(
                        lambda d=d, m=m: copy2(j, q1, m, d).wait_send()
                    )

    steps = [own]
    steps += [functools.partial(line1, k) for k in range(1, n1)]
    steps += [functools.partial(line2, m) for m in range(1, n2)]
    return steps, finish


def spread_steps(n, x, out, chunk, sems):
    f = lax.axis_index("fsdp")
    c = lax.axis_index("ctx")
    n_f = lax.axis_size("fsdp")
    n_y = n_f // 2
    y, core = f // 2, f % 2
    owner = c // (n // n_f)
    oy, oc = owner // 2, owner % 2
    first, count = chunk
    rows = pl.ds(first, count)
    up, down, side, come = sems

    def copy(own, sem, to):
        return pltpu.make_async_remote_copy(
            src_ref=x.at[rows] if own else out.at[rows],
            dst_ref=out.at[rows],
            send_sem=sem,
            recv_sem=come,
            device_id=(c, to),
            device_id_type=MESH,
        )

    on = core == oc
    ways = (
        (up, f + 2, jnp.logical_and(on, jnp.logical_and(y >= oy, y < n_y - 1))),
        (down, f - 2, jnp.logical_and(on, jnp.logical_and(y <= oy, y > 0))),
        (side, f + 1 - 2 * core, on),
    )

    def own():
        for sem, to, cond in ways:
            pl.when(jnp.logical_and(cond, f == owner))(lambda sem=sem, to=to: copy(True, sem, to).start())

    def onward():
        @pl.when(f != owner)
        def _():
            copy(False, side, f).wait_recv()
            for sem, to, cond in ways:
                pl.when(cond)(lambda sem=sem, to=to: copy(False, sem, to).start())

    def finish():
        for sem, to, cond in ways:
            pl.when(cond)(lambda sem=sem, to=to: copy(False, sem, to).wait_send())

    return own, onward, finish


def gather_sems(chunks):
    sem = pltpu.SemaphoreType.DMA
    return [sem((chunks, 2, 4)), sem((chunks, 2, 4)), sem((chunks, 2, 4, 7)), sem((chunks, 2, 4, 7))]


def gather_kernel(n, plans, spread, *refs):
    count = len(plans)
    k = count + (1 if spread else 0)
    xs, outs = refs[:k], refs[k : 2 * k]
    held = refs[2 * k : 3 * k]
    local, s1, r1, s2, r2, s3 = refs[3 * k :]
    n_a, n_b, a, b, f = places(n)
    c = a * n_b + b
    greet(a, b, n_a, n_b, f, bool(spread))
    steps, ends, at = [], [], 0
    for x, out, chunks in zip(xs, outs, plans):
        for chunk in chunks:
            sems = (s1.at[at], r1.at[at], s2.at[at], r2.at[at])
            more, end = gather_steps(n, x, out, chunk, sems)
            steps.append(more)
            ends.append(end)
            at += 1
    for i, chunk in enumerate(spread):
        begin, onward, end = spread_steps(n, xs[-1], outs[-1], chunk, [s3.at[i, j] for j in range(4)])
        steps.append([begin] + [lambda: None] * (1 + 2 * i) + [onward])
        ends.append(end)
    mine = f == c // (n // lax.axis_size("fsdp"))
    for t in range(max(map(len, steps))):
        for more in steps:
            if t < len(more):
                more[t]()
        if t < 2:
            for i in range(k):
                out = outs[i].at[c] if i < count else outs[i]

                @when(True if i < count else mine)
                def _():
                    fetch = pltpu.make_async_copy(xs[i], held[i], local.at[i])
                    if t == 0:
                        fetch.start()
                    else:
                        fetch.wait()
                        pltpu.make_async_copy(held[i], out, local.at[i]).start()
    for i in range(k):
        out = outs[i].at[c] if i < count else outs[i]
        when(True if i < count else mine)(pltpu.make_async_copy(held[i], out, local.at[i]).wait)
    for end in ends:
        end()


def gather_ctx(xs, n, cid, cuts=2, spread=None):
    plans = tuple(plan(x.shape[0], cuts) for x in xs)
    shapes = [jax.ShapeDtypeStruct((n,) + x.shape, x.dtype) for x in xs]
    parts = ()
    if spread is not None:
        rows = spread.shape[0]
        half = rows // 32 * 16
        parts = ((0, rows),) if rows % 16 else ((0, half), (half, rows - half))
        xs = xs + [spread]
        shapes = shapes + [jax.ShapeDtypeStruct(spread.shape, spread.dtype)]
    return pl.pallas_call(
        functools.partial(gather_kernel, n, plans, parts),
        out_shape=shapes,
        in_specs=[pl.BlockSpec(memory_space=pl.ANY)] * len(xs),
        out_specs=[pl.BlockSpec(memory_space=pl.ANY)] * len(xs),
        scratch_shapes=[pltpu.VMEM(x.shape, x.dtype) for x in xs]
        + [pltpu.SemaphoreType.DMA((len(xs),))]
        + gather_sems(sum(map(len, plans)))
        + [pltpu.SemaphoreType.DMA((2, 4))],
        compiler_params=pltpu.CompilerParams(
            collective_id=cid, has_side_effects=True, vmem_limit_bytes=60 << 20
        ),
        name=f"gather{cid}",
    )(*xs)


def cast_rows(src, dst):
    rows = src.shape[0]
    if rows % 16:
        dst[...] = src[...].astype(dst.dtype)
        return

    def one(i, carry):
        at = pl.ds(pl.multiple_of(i * 16, 16), 16)
        dst[at, :] = src[at, :].astype(dst.dtype)
        return carry

    lax.fori_loop(0, rows // 16, one, 0)


def first_kernel(n, chunks, ratio, *refs):
    x, wo, wd, g, out, wo_out, wd_out, g_out = refs[:8]
    held, wo_wide, wo_low, wd_wide, wd_low, g_held, local, s1, r1, s2, r2, gs, gr = refs[8:]
    n_a, n_b, a, b, f = places(n)
    c = a * n_b + b
    n_f = lax.axis_size("fsdp")
    ffs = wd_low.shape[0]
    own = pl.ds(pl.multiple_of((c % ratio) * ffs, 8), ffs)
    loads = [
        pltpu.make_async_copy(src, dst, local.at[i])
        for i, (src, dst) in enumerate(((x, held), (wo, wo_wide), (wd.at[own], wd_wide), (g, g_held)))
    ]
    stores = [
        pltpu.make_async_copy(src, dst, local.at[i])
        for i, (src, dst) in enumerate(
            ((held, out.at[c]), (wo_low, wo_out), (wd_low, wd_out), (g_held, g_out.at[f]))
        )
    ]
    for copy in loads:
        copy.start()
    greet(a, b, n_a, n_b, f, True)
    steps, ends = [], []
    for i, chunk in enumerate(chunks):
        more, end = gather_steps(n, x, out, chunk, (s1.at[i], r1.at[i], s2.at[i], r2.at[i]))
        steps.append(more)
        ends.append(end)

    def gain(m):
        return pltpu.make_async_remote_copy(
            src_ref=g,
            dst_ref=g_out.at[f],
            send_sem=gs.at[m],
            recv_sem=gr.at[m],
            device_id=(c, (f + m) % n_f),
            device_id_type=MESH,
        )

    for t in range(n_a + n_b - 1):
        for more in steps:
            if t < len(more):
                more[t]()
        if t == 0:
            for m in range(1, n_f):
                gain(m).start()
            loads[0].wait()
            stores[0].start()
            loads[3].wait()
            stores[3].start()
            loads[1].wait()
            cast_rows(wo_wide, wo_low)
            stores[1].start()
        if t == 1:
            loads[2].wait()
            cast_rows(wd_wide, wd_low)
            stores[2].start()
    for copy in stores:
        copy.wait()
    for m in range(1, n_f):
        gain(m).wait()
    for end in ends:
        end()


def gather_first(x, w_out, w_down, gains, n, ratio, ffs, cid):
    n_f = lax.axis_size("fsdp")
    chunks = plan(x.shape[0])
    low = [jax.ShapeDtypeStruct(w_out.shape, bf16), jax.ShapeDtypeStruct((ffs, w_down.shape[1]), bf16)]
    sem = pltpu.SemaphoreType.DMA
    return pl.pallas_call(
        functools.partial(first_kernel, n, chunks, ratio),
        out_shape=[jax.ShapeDtypeStruct((n,) + x.shape, x.dtype)]
        + low
        + [jax.ShapeDtypeStruct((n_f,) + gains.shape, gains.dtype)],
        in_specs=[pl.BlockSpec(memory_space=pl.ANY)] * 4,
        out_specs=[pl.BlockSpec(memory_space=pl.ANY)] * 4,
        scratch_shapes=[
            pltpu.VMEM(x.shape, x.dtype),
            pltpu.VMEM(w_out.shape, f32),
            pltpu.VMEM(w_out.shape, bf16),
            pltpu.VMEM((ffs, w_down.shape[1]), f32),
            pltpu.VMEM((ffs, w_down.shape[1]), bf16),
            pltpu.VMEM(gains.shape, gains.dtype),
            sem((4,)),
        ]
        + gather_sems(len(chunks))
        + [sem((n_f,)), sem((n_f,))],
        compiler_params=pltpu.CompilerParams(
            collective_id=cid, has_side_effects=True, vmem_limit_bytes=60 << 20
        ),
        name=f"gather{cid}",
    )(x, w_out, w_down, gains)


def attend_gather_kernel(n, chunks, heads, block, *refs):
    x, n_hbm, w_hbm, cos_ref, sin_ref, first_ref, order_ref = refs[:7]
    out, q_ref, k_ref, v_ref, dealt_ref, all_ref = refs[7:13]
    held, n_ref, w_ref, mixed, local, s1, r1, s2, r2, sa, ra = refs[13:]
    n_a, n_b, a, b, f = places(n)
    c = a * n_b + b
    all_rows = n_ref.shape[0]
    rows = all_rows // n
    hw = heads * HD
    loads = [
        pltpu.make_async_copy(src, dst, local.at[i])
        for i, (src, dst) in enumerate(((x, held), (n_hbm, n_ref), (w_hbm, w_ref)))
    ]
    for copy in loads:
        copy.start()
    bar = pltpu.get_barrier_semaphore()
    for m in range(1, n):
        pl.semaphore_signal(bar, inc=1, device_id=((c + m) % n, f), device_id_type=MESH)
    pl.semaphore_wait(bar, n - 1)
    steps, ends = [], []
    for i, chunk in enumerate(chunks):
        more, end = gather_steps(n, x, out, chunk, (s1.at[i], r1.at[i], s2.at[i], r2.at[i]))
        steps.append(more)
        ends.append(end)

    def run(t):
        for more in steps:
            if t < len(more):
                more[t]()

    def exchange(m):
        to = (c + m) % n
        return pltpu.make_async_remote_copy(
            src_ref=dealt_ref.at[to],
            dst_ref=all_ref.at[c],
            send_sem=sa.at[m],
            recv_sem=ra.at[m],
            device_id=(to, f),
            device_id_type=MESH,
        )

    def attend_block(at):
        own = slice(at, at + block)
        proj = dot(n_ref[own, :], w_ref[...], NN)
        cos, sin = cos_ref[own, :], sin_ref[own, :]
        for h in range(heads):
            head = slice(h * HD, (h + 1) * HD)
            for ref, base in ((q_ref, 0), (k_ref, hw)):
                u = proj[:, base + h * HD : base + (h + 1) * HD]
                ref[own, head] = (u * cos + turned(u) * sin).astype(bf16)
        v_ref[own, :] = proj[:, 2 * hw :].astype(bf16)
        for h in range(heads):
            head = slice(h * HD, (h + 1) * HD)
            seen = slice(0, at + block)
            probs = masked_probs(q_ref[own, head], k_ref[seen, head], first_ref[own, :], at)
            mixed[own, head] = dot(probs.astype(bf16), v_ref[seen, head], NN).astype(bf16)

    run(0)
    keep = pltpu.make_async_copy(held, out.at[c], local.at[0])
    loads[0].wait()
    keep.start()
    loads[1].wait()
    loads[2].wait()
    for at in range(0, all_rows, block):
        attend_block(at)
        if at + block == all_rows // 2:
            run(1)
    for m in range(n):
        own = slice(m * rows, (m + 1) * rows)
        given = lax.broadcasted_iota(jnp.int32, (rows, all_rows), 1)
        picks = jnp.where(given == order_ref[own, :], 1.0, 0.0).astype(bf16)
        dealt_ref[m] = dot(picks, mixed[...], NN).astype(bf16)
    for m in range(1, n):
        exchange(m).start()
    mine = pltpu.make_async_copy(dealt_ref.at[c], all_ref.at[c], local.at[1])
    mine.start()
    for t in range(2, n_a + n_b - 1):
        run(t)
    keep.wait()
    mine.wait()
    for m in range(1, n):
        exchange(m).wait()
    for end in ends:
        end()


def attend_gather(x, normed, wq, cos, sin, first, order, heads, n, cid, block=256):
    all_rows = normed.shape[0]
    rows = all_rows // n
    hw = heads * HD
    chunks = plan(x.shape[0])
    one = jax.ShapeDtypeStruct((all_rows, hw), bf16)
    split = jax.ShapeDtypeStruct((n, rows, hw), bf16)
    hbm = pl.BlockSpec(memory_space=pl.ANY)
    vmem = pl.BlockSpec(memory_space=pltpu.VMEM)
    sem = pltpu.SemaphoreType.DMA
    return pl.pallas_call(
        functools.partial(attend_gather_kernel, n, chunks, heads, block),
        out_shape=[jax.ShapeDtypeStruct((n,) + x.shape, x.dtype), one, one, one, split, split],
        in_specs=[hbm] * 3 + [vmem] * 4,
        out_specs=[hbm] + [vmem] * 4 + [hbm],
        scratch_shapes=[
            pltpu.VMEM(x.shape, x.dtype),
            pltpu.VMEM(normed.shape, bf16),
            pltpu.VMEM(wq.shape, bf16),
            pltpu.VMEM((all_rows, hw), bf16),
            sem((3,)),
        ]
        + gather_sems(len(chunks))
        + [sem((n,)), sem((n,))],
        compiler_params=pltpu.CompilerParams(
            collective_id=cid, has_side_effects=True, vmem_limit_bytes=60 << 20
        ),
        name=f"attend{cid}",
    )(x, normed, wq, cos, sin, first, order)


def back_gather_kernel(n, chunks, heads, block, *refs):
    x, db_hbm, wo_hbm, down_hbm, q_ref, k_ref, v_ref, mixed_ref = refs[:8]
    cos_ref, sin_ref, first_ref, order_ref = refs[8:12]
    out, proj_ref, rows_hbm = refs[12:15]
    held, db, wo, down, rows_ref, dealt, given, dk_ref, dv_ref, local, s1, r1, s2, r2 = refs[15:]
    n_a, n_b, a, b, f = places(n)
    c = a * n_b + b
    hw = heads * HD
    all_rows = db.shape[0]
    part = all_rows // n
    ffs = down.shape[0]
    own_rows = pl.ds(pl.multiple_of(c * hw, hw), hw)
    loads = [
        pltpu.make_async_copy(src, dst, local.at[i])
        for i, (src, dst) in enumerate(((x, held), (db_hbm, db), (wo_hbm.at[own_rows], wo), (down_hbm, down)))
    ]
    for copy in loads:
        copy.start()
    greet(a, b, n_a, n_b, f)
    steps, ends = [], []
    for i, chunk in enumerate(chunks):
        more, end = gather_steps(n, x, out, chunk, (s1.at[i], r1.at[i], s2.at[i], r2.at[i]))
        steps.append(more)
        ends.append(end)

    def run(t):
        for more in steps:
            if t < len(more):
                more[t]()

    run(0)
    keep = pltpu.make_async_copy(held, out.at[c], local.at[0])
    loads[0].wait()
    keep.start()
    for copy in loads[1:]:
        copy.wait()
    dealt[...] = dot(db[...], wo[...], NT).astype(bf16)
    for m in range(n):
        own = slice(m * part, (m + 1) * part)
        slots = lax.broadcasted_iota(jnp.int32, (part, all_rows), 1)
        picks = jnp.where(slots == order_ref[own, :], 1.0, 0.0).astype(bf16)
        given[own, :] = dot(picks, dealt[...], NN).astype(bf16)
    rows_ref[:ffs, :] = down[...]
    rows_ref[ffs:, :] = dot(mixed_ref[...], db[...], TN).astype(bf16)
    stored = pltpu.make_async_copy(rows_ref, rows_hbm, local.at[1])
    stored.start()
    attend_back_kernel(
        heads, block, q_ref, k_ref, v_ref, given, cos_ref, sin_ref, first_ref, proj_ref, dk_ref, dv_ref
    )
    for t in range(1, n_a + n_b - 1):
        run(t)
    keep.wait()
    stored.wait()
    for end in ends:
        end()


def back_gather(x, db, wo, down, q, k, v, mixed, cos, sin, first, order, heads, n, cid, block=256):
    all_rows, width = db.shape
    hw = heads * HD
    chunks = plan(x.shape[0])
    hbm = pl.BlockSpec(memory_space=pl.ANY)
    vmem = pl.BlockSpec(memory_space=pltpu.VMEM)
    both_rows = (down.shape[0] + hw, width)
    return pl.pallas_call(
        functools.partial(back_gather_kernel, n, chunks, heads, block),
        out_shape=[
            jax.ShapeDtypeStruct((n,) + x.shape, x.dtype),
            jax.ShapeDtypeStruct((all_rows, 3 * hw), bf16),
            jax.ShapeDtypeStruct(both_rows, bf16),
        ],
        in_specs=[hbm] * 4 + [vmem] * 8,
        out_specs=[hbm, vmem, hbm],
        scratch_shapes=[
            pltpu.VMEM(x.shape, x.dtype),
            pltpu.VMEM(db.shape, bf16),
            pltpu.VMEM((hw, width), bf16),
            pltpu.VMEM(down.shape, bf16),
            pltpu.VMEM(both_rows, bf16),
            pltpu.VMEM((all_rows, hw), bf16),
            pltpu.VMEM((all_rows, hw), bf16),
            pltpu.VMEM((all_rows, HD), f32),
            pltpu.VMEM((all_rows, HD), f32),
            pltpu.SemaphoreType.DMA((4,)),
        ]
        + gather_sems(len(chunks)),
        compiler_params=pltpu.CompilerParams(
            collective_id=cid, has_side_effects=True, vmem_limit_bytes=60 << 20
        ),
        name=f"back{cid}",
    )(x, db, wo, down, q, k, v, mixed, cos, sin, first, order)


def feed_kernel(n, chunks, halves, *refs):
    x, down, w_hbm, g_hbm = refs[:4]
    out, wd_out, act_ref, back_ref = refs[4:8]
    held, down_held, shard, w, g, wd, pre, local, gsem, s1, r1, s2, r2, s3 = refs[8:]
    n_a, n_b, a, b, f = places(n)
    c = a * n_b + b
    rows = x.shape[0]
    pair = 2 * rows
    ffs = wd.shape[0]
    h = a // 2
    mine = f == c // (n // lax.axis_size("fsdp"))
    loads = [
        pltpu.make_async_copy(src, dst, local.at[i])
        for i, (src, dst) in enumerate(((x, held), (w_hbm, w), (down, down_held)))
    ]
    loads += [
        pltpu.make_async_copy(
            g_hbm.at[q * n_b + p], g.at[pl.ds((p * n_a + q) * rows, rows)], gsem.at[q * n_b + p]
        )
        for q in range(n_a)
        for p in range(n_b)
    ]
    for copy in loads:
        copy.start()
    greet(a, b, n_a, n_b, f, True)
    steps, parts, ends = [], [], []
    for i, chunk in enumerate(chunks):
        late = []
        more, end = gather_steps(n, x, out, chunk, (s1.at[i], r1.at[i], s2.at[i], r2.at[i]), late)
        steps.append(more)
        parts.append(late)
        ends.append(end)
    spread = [
        spread_steps(n, down, wd_out, half, [s3.at[i, j] for j in range(4)])
        for i, half in enumerate(halves)
    ]

    def forward(p, half, buf):
        fetches = [
            pltpu.make_async_copy(
                out.at[(2 * half + i) * n_b + p], shard.at[pl.ds(i * rows, rows)], local.at[3 + i]
            )
            for i in (0, 1)
        ]
        for copy in fetches:
            copy.start()
        for copy in fetches:
            copy.wait()
        pre[buf] = dot(shard[...], w[...], NN)

    def backward(p, half, buf):
        gate, up = pre[buf, :, :ffs], pre[buf, :, ffs:]
        sigma = jax.nn.sigmoid(gate)
        gate_act = gate * sigma
        at = pl.multiple_of((p * n_a + 2 * half) * rows, pair)
        d_act = dot(g[pl.ds(at, pair), :], wd[...], NT)
        act = (gate_act * up).astype(bf16)
        d_gate = (d_act * up * sigma * (1.0 + gate * (1.0 - sigma))).astype(bf16)
        d_up = (d_act * gate_act).astype(bf16)
        for i in (0, 1):
            to = pl.ds(pl.multiple_of(((2 * half + i) * n_b + p) * rows, rows), rows)
            own = slice(i * rows, (i + 1) * rows)
            act_ref[to, :] = act[own]
            back_ref[to, :ffs] = d_gate[own]
            back_ref[to, ffs:] = d_up[own]

    for more in steps:
        more[0]()
    for begin, _, _ in spread:
        begin()
    loads[0].wait()
    keep = pltpu.make_async_copy(held, out.at[c], local.at[0])
    keep.start()
    loads[2].wait()
    keep_down = pltpu.make_async_copy(down_held, wd_out, local.at[2])
    pl.when(mine)(keep_down.start)
    loads[1].wait()
    keep.wait()
    for k in range(1, n_a):
        for more in steps:
            more[k]()
        if k == 1:
            forward(b, h, 0)
    forward(b, 1 - h, 1)
    for _, onward, _ in spread:
        onward()
    pl.when(mine)(keep_down.wait)
    fetch = pltpu.make_async_copy(wd_out, wd, local.at[5])
    fetch.start()
    fetch.wait()
    for copy in loads[3:]:
        copy.wait()
    backward(b, h, 0)
    backward(b, 1 - h, 1)
    for m in range(1, n_b):
        for d, p, there in ((0, b - m, b >= m), (1, b + m, b + m < n_b)):
            for half, near in ((h, True), (1 - h, False)):
                for late in zip(*parts):
                    if late[0][2:] == (m, d, near):
                        for cond, arrive, _, _, _ in late:
                            pl.when(cond)(arrive)

                @pl.when(there)
                def _():
                    forward(p, half, 0)
                    backward(p, half, 0)

    for _, _, end in spread:
        end()
    for end in ends:
        end()


def feed_gather(x, down, wgu, g, n, cid):
    rows, width = x.shape
    ffs = down.shape[0]
    half = rows // 2
    chunks = ((0, half, False), (half, half, False))
    cut = ffs // 32 * 16
    halves = ((0, ffs),) if ffs % 16 else ((0, cut), (cut, ffs - cut))
    hbm = pl.BlockSpec(memory_space=pl.ANY)
    vmem = pl.BlockSpec(memory_space=pltpu.VMEM)
    return pl.pallas_call(
        functools.partial(feed_kernel, n, chunks, halves),
        out_shape=[
            jax.ShapeDtypeStruct((n, rows, width), bf16),
            jax.ShapeDtypeStruct((ffs, width), bf16),
            jax.ShapeDtypeStruct((n * rows, ffs), bf16),
            jax.ShapeDtypeStruct((n * rows, 2 * ffs), bf16),
        ],
        in_specs=[hbm] * 4,
        out_specs=[hbm, hbm, vmem, vmem],
        scratch_shapes=[
            pltpu.VMEM((rows, width), bf16),
            pltpu.VMEM((ffs, width), bf16),
            pltpu.VMEM((2 * rows, width), bf16),
            pltpu.VMEM(wgu.shape, bf16),
            pltpu.VMEM((n * rows, width), bf16),
            pltpu.VMEM((ffs, width), bf16),
            pltpu.VMEM((2, 2 * rows, 2 * ffs), f32),
            pltpu.SemaphoreType.DMA((6,)),
            pltpu.SemaphoreType.DMA((n,)),
        ]
        + gather_sems(len(chunks))
        + [pltpu.SemaphoreType.DMA((2, 4))],
        compiler_params=pltpu.CompilerParams(
            collective_id=cid, has_side_effects=True, vmem_limit_bytes=60 << 20
        ),
        name=f"feed{cid}",
    )(x, down, wgu, g)


def order_of(p, n):
    if n == 2:
        return (1 - p, p)
    h = p // 2
    return (3 - 3 * h, 2 - h, 1 - p + 4 * h, p)


def reduce_steps(n, part, chunk, bufs, sems):
    n_a, n_b, a, b, f = places(n)
    first, count, swapped = chunk
    g1, g2 = bufs
    s1, r1, s2, r2 = sems
    (p1, n1), (p2, n2) = ((a, n_a), (b, n_b)) if swapped else ((b, n_b), (a, n_a))

    def slot(q1, q2):
        return q1 * n_b + q2 if swapped else q2 * n_b + q1

    rows = pl.ds(first, count)
    from1 = (p1 > 0, p1 < n1 - 1)
    from2 = (p2 > 0, p2 < n2 - 1)
    targets = order_of(p2, n2)

    def has1(d, k):
        return (p1 + k < n1) if d == 0 else (p1 >= k)

    def add(t, got):
        mine = part.at[t, rows]
        mine[...] = (mine[...].astype(f32) + got[...].astype(f32)).astype(mine.dtype)

    def remote(src, dst, send, recv, to):
        return pltpu.make_async_remote_copy(
            src_ref=src, dst_ref=dst, send_sem=send, recv_sem=recv, device_id=(to, f), device_id_type=MESH
        )

    def side1(d):
        return d if n1 > 2 else 0

    def copy1(j, d, k):
        t = p1 + k if d == 0 else p1 - k
        to = p1 + 1 if d == 0 else p1 - 1
        src = part.at[slot(t, targets[j]), rows]
        return remote(src, g1.at[side1(d), k - 1, j], s1.at[d, k, j], r1.at[d, k - 1, j], slot(to, p2))

    def come1(j, d, k):
        src = part.at[slot(p1, p2), rows]
        return remote(src, g1.at[side1(d), k, j], s1.at[d, k, j], r1.at[d, k, j], slot(p1, p2))

    def copy2(t, d):
        k = t - p2 if d == 0 else p2 - t
        to = p2 + 1 if d == 0 else p2 - 1
        return remote(
            part.at[slot(p1, t), rows], g2.at[d, k - 1], s2.at[d, k], r2.at[d, k - 1], slot(p1, to)
        )

    def come2(d, k):
        src = part.at[slot(p1, p2), rows]
        return remote(src, g2.at[d, k], s2.at[d, k], r2.at[d, k], slot(p1, p2))

    def start(j):
        for d in (0, 1) if j < n2 else ():
            for k in range(n1 - 1, 0, -1):
                when(both(has1(d, k), jnp.logical_not(from1[d])))(
                    lambda d=d, k=k: copy1(j, d, k).start()
                )

    def middle1(j, k):
        for d in (0, 1):

            @when(both(has1(d, k), from1[d]))
            def _():
                come1(j, d, k).wait_recv()
                add(slot(p1 + k if d == 0 else p1 - k, targets[j]), g1.at[side1(d), k, j])
                copy1(j, d, k).start()

    def last1(j):
        for d in (0, 1):

            @when(from1[d])
            def _():
                come1(j, d, 0).wait_recv()
                add(slot(p1, targets[j]), g1.at[side1(d), 0, j])

    def line2(j):
        t = targets[j]
        for d in (0, 1):

            @when((t > p2) if d == 0 else (t < p2))
            def _():
                @when(from2[d])
                def _():
                    k = t - p2 if d == 0 else p2 - t
                    come2(d, k).wait_recv()
                    add(slot(p1, t), g2.at[d, k])

                copy2(t, d).start()

    def last2():
        for d in (0, 1):

            @when(from2[d])
            def _():
                come2(d, 0).wait_recv()
                add(slot(p1, p2), g2.at[d, 0])

    steps = []
    if swapped:
        for k in range(n1 - 2, 0, -1):
            steps.append(lambda k=k: [middle1(j, k) for j in range(n2)])
        steps.append(lambda: [(last1(j), line2(j) if j < n2 - 1 else None) for j in range(n2)])
        steps.append(last2)
    else:

        def item(j):
            for k in range(n1 - 2, 0, -1):
                middle1(j, k)
            last1(j)
            if j < n2 - 1:
                line2(j)

        steps += [functools.partial(item, j) for j in range(n2)] + [last2]

    def finish():
        for j in range(n2):
            for d in (0, 1):
                for k in range(n1 - 1, 0, -1):
                    when(has1(d, k))(lambda j=j, d=d, k=k: copy1(j, d, k).wait_send())
                if j < n2 - 1:
                    t = targets[j]
                    when((t > p2) if d == 0 else (t < p2))(lambda t=t, d=d: copy2(t, d).wait_send())

    return start, steps, finish


def reduce_kernel(n, chunks, jobs, extras, count, *refs):
    n_a, n_b, a, b, f = places(n)
    k, e = len(jobs), len(extras)
    hbm, rest = refs[:count], refs[count:]
    o_refs, p_refs, rest = rest[:k], rest[k : k + e], rest[k + e :]
    held, parts, made, rest = rest[:count], rest[count : count + k], rest[count + k : count + k + e], rest[count + k + e :]
    cuts = len(chunks)
    bufs, rest = rest[: 2 * k * cuts], rest[2 * k * cuts :]
    load, stored, s1, r1, s2, r2 = rest
    rows = o_refs[0].shape[0]
    first = sorted({i for x, w, _ in jobs for i in (x, w)})
    order_in = first + [i for i in range(count) if i not in first]
    loads = [pltpu.make_async_copy(hbm[i], held[i], load.at[i]) for i in range(count)]
    for i in order_in:
        loads[i].start()
    todo = []
    for i in range(k):
        for m, chunk in enumerate(chunks):
            at = i * cuts + m
            sems = (s1.at[at], r1.at[at], s2.at[at], r2.at[at])
            todo.append(reduce_steps(n, parts[i], chunk, bufs[2 * at : 2 * at + 2], sems))

    def term(i, t):
        x, w, nt = jobs[i]
        at = pl.multiple_of(t * rows, rows)
        parts[i][t] = dot(held[x][pl.ds(at, rows), :], held[w][...], NT if nt else NN).astype(bf16)

    tiles, stores = [], []
    for i, (x, y) in enumerate(extras):
        high = held[x].shape[1]
        for lo in range(0, high, 256):
            hi = min(lo + 256, high)

            def tile(i=i, x=x, y=y, lo=lo, hi=hi):
                made[i][lo:hi, :] = dot(held[x][:, lo:hi], held[y][...], TN).astype(bf16)

            tiles.append(tile)
        stores.append((len(tiles), i))

    order = order_of(a, n_a)
    greet(a, b, n_a, n_b, f)
    for i in first:
        loads[i].wait()
    for j in range(n_a):
        for i in range(k):
            for m in range(1, n_b):
                term(i, order[j] * n_b + (b + m) % n_b)
            for start, _, _ in todo[i * cuts : (i + 1) * cuts]:
                start(j)
    for i in order_in[len(first) :]:
        loads[i].wait()
    done = 0
    for j in range(n_a):
        for i in range(k):
            term(i, order[j] * n_b + b)
        upto = len(tiles) * (j + 1) // n_a
        for at in range(done, upto):
            tiles[at]()
            for last, i in stores:
                if last == at + 1:
                    pltpu.make_async_copy(made[i], p_refs[i], stored.at[i]).start()
        done = upto
        for _, steps, _ in todo:
            steps[j]()
    for _, steps, _ in todo:
        steps[n_a]()
    for i in range(k):
        o_refs[i][...] = parts[i][a * n_b + b]
    for _, _, finish in todo:
        finish()
    for i in range(e):
        pltpu.make_async_copy(made[i], p_refs[i], stored.at[i]).wait()


def reduce_ctx(arrays, jobs, extras, n, cid):
    n_a, n_b = LINE, n // LINE
    rows = arrays[jobs[0][0]].shape[0] // n
    half = rows // 2
    chunks = ((0, half, False), (half, half, False))
    widths = [arrays[w].shape[0 if nt else 1] for _, w, nt in jobs]
    bufs = []
    for width in widths:
        for _, count, _ in chunks:
            bufs += [
                pltpu.VMEM((min(2, n_b - 1), n_b - 1, n_a, count, width), bf16),
                pltpu.VMEM((2, n_a - 1, count, width), bf16),
            ]
    made = [(arrays[x].shape[1], arrays[y].shape[1]) for x, y in extras]
    sem = pltpu.SemaphoreType.DMA
    k = len(jobs) * len(chunks)
    return pl.pallas_call(
        functools.partial(reduce_kernel, n, chunks, jobs, extras, len(arrays)),
        out_shape=[jax.ShapeDtypeStruct((rows, width), bf16) for width in widths]
        + [jax.ShapeDtypeStruct(shape, bf16) for shape in made],
        in_specs=[pl.BlockSpec(memory_space=pl.ANY)] * len(arrays),
        out_specs=[pl.BlockSpec(memory_space=pltpu.VMEM)] * len(widths)
        + [pl.BlockSpec(memory_space=pl.ANY)] * len(made),
        scratch_shapes=[pltpu.VMEM(x.shape, x.dtype) for x in arrays]
        + [pltpu.VMEM((n, rows, width), bf16) for width in widths]
        + [pltpu.VMEM(shape, bf16) for shape in made]
        + bufs
        + [sem((len(arrays),)), sem((max(1, len(made)),))]
        + [sem((k, 2, 4, 4)), sem((k, 2, 4, 4)), sem((k, 2, 4)), sem((k, 2, 4))],
        compiler_params=pltpu.CompilerParams(
            collective_id=cid, has_side_effects=True, vmem_limit_bytes=60 << 20
        ),
        name=f"reduce{cid}",
    )(*arrays)


def assemble_rows(parts, ratio, ffs):
    n, rows, w = parts.shape
    each = rows // ratio
    hw = each - ffs

    def body(i_ref, down_ref, out_ref):
        for j in range(ratio):
            down_ref[j * ffs : (j + 1) * ffs, :] = i_ref[0, j * each : j * each + ffs, :].astype(f32)
            out_ref[j * hw : (j + 1) * hw, :] = i_ref[0, j * each + ffs : (j + 1) * each, :].astype(f32)

    return pl.pallas_call(
        body,
        grid=(n,),
        out_shape=[
            jax.ShapeDtypeStruct((ratio * ffs, n * w), f32),
            jax.ShapeDtypeStruct((ratio * hw, n * w), f32),
        ],
        in_specs=[pl.BlockSpec((1, rows, w), lambda i: (i, 0, 0))],
        out_specs=[
            pl.BlockSpec((ratio * ffs, w), lambda i: (0, i)),
            pl.BlockSpec((ratio * hw, w), lambda i: (0, i)),
        ],
        compiler_params=pltpu.CompilerParams(vmem_limit_bytes=60 << 20),
        name="assemble_rows",
    )(parts)


def assemble(parts, n_groups, block=64):
    n, rows, gw = parts.shape
    w = gw // n_groups

    def body(i_ref, o_ref):
        for g in range(n_groups):
            for c in range(n):
                o_ref[:, (g * n + c) * w:(g * n + c + 1) * w] = i_ref[c, :, g * w:(g + 1) * w].astype(jnp.float32)

    return pl.pallas_call(
        body, grid=(rows // block,),
        out_shape=jax.ShapeDtypeStruct((rows, n * gw), jnp.float32),
        in_specs=[pl.BlockSpec((n, block, gw), lambda i: (0, i, 0))],
        out_specs=pl.BlockSpec((block, n * gw), lambda i: (i, 0)),
        compiler_params=pltpu.CompilerParams(vmem_limit_bytes=60 << 20),
        name="assemble")(parts)


def dot(a, b, dims):
    return lax.dot_general(a, b, (dims, ((), ())), preferred_element_type=f32)


NN = ((1,), (0,))
NT = ((1,), (1,))
TN = ((0,), (0,))


def turned(u):
    return pltpu.roll(u, HD // 2, 1)


def masked_probs(q, k, first, at):
    logits = dot(q, k, NT) * (1.0 / math.sqrt(HD))
    keys = lax.broadcasted_iota(jnp.int32, logits.shape, 1)
    queries = lax.broadcasted_iota(jnp.int32, logits.shape, 0) + at
    scaled = jnp.where((keys <= queries) & (keys >= first), logits, masked_score)
    raised = jnp.exp(scaled - jnp.max(scaled, -1, keepdims=True))
    return raised / jnp.sum(raised, -1, keepdims=True)


def attend_back_kernel(
    heads, block, q_ref, k_ref, v_ref, d_ref, cos_ref, sin_ref, first_ref, o_ref, dk_ref, dv_ref
):
    rows = q_ref.shape[0]
    hw = heads * HD

    def back(w, own):
        return (w * cos_ref[own, :] - turned(w) * sin_ref[own, :]).astype(bf16)

    for h in range(heads):
        head = slice(h * HD, (h + 1) * HD)
        for at in reversed(range(0, rows, block)):
            own = slice(at, at + block)
            seen = slice(0, at + block)
            q, k, v, d = q_ref[own, head], k_ref[seen, head], v_ref[seen, head], d_ref[own, head]
            probs = masked_probs(q, k, first_ref[own, :], at)
            d_probs = dot(d, v, NT)
            inner = jnp.sum(probs * d_probs, -1, keepdims=True)
            d_scores = (probs * (d_probs - inner) * (1.0 / math.sqrt(HD))).astype(bf16)
            o_ref[own, head] = back(dot(d_scores, k, NN), own)
            dk = dot(d_scores, q, TN)
            dv = dot(probs.astype(bf16), d, TN)
            if at + block == rows:
                dk_ref[...] = dk
                dv_ref[...] = dv
            else:
                dk_ref[seen, :] += dk
                dv_ref[seen, :] += dv
        every = slice(0, rows)
        o_ref[:, hw + h * HD : hw + (h + 1) * HD] = back(dk_ref[...], every)
        o_ref[:, 2 * hw + h * HD : 2 * hw + (h + 1) * HD] = dv_ref[...].astype(bf16)


def rope_tables(within):
    freq_index = jnp.arange(HD // 2, dtype=f32)
    inverse = rope_base ** (-2.0 * freq_index / HD)
    angles = within.astype(f32)[:, None] * inverse[None, :]
    cos, sin = jnp.cos(angles), jnp.sin(angles)
    return jnp.concatenate([cos, cos], -1), jnp.concatenate([-sin, sin], -1)


def rms_scale(values):
    return lax.rsqrt(jnp.mean(values * values, -1, keepdims=True) + epsilon)


def norm_back(grad_norm, values, scale_rows, gain_float):
    scaled = grad_norm * gain_float[None, :]
    cubed = scale_rows * scale_rows * scale_rows
    return scale_rows * scaled - values * cubed * jnp.mean(scaled * values, -1, keepdims=True)


def shards(
    tokens, cotangent, lengths, deal, norm1_gain, w_qkv, w_out, norm2_gain, w_gate_up, w_down
):
    n_ctx = lax.axis_size("ctx")
    n_fsdp = lax.axis_size("fsdp")
    me = lax.axis_index("ctx")
    mine = lax.axis_index("fsdp")
    rows = tokens.shape[1]
    width = tokens.shape[2]
    piece = rows // n_ctx
    all_rows = rows * n_ctx
    pieces = all_rows // piece
    heads = H // n_ctx
    hw = heads * HD
    kr = w_qkv.shape[0]
    ff = w_gate_up.shape[1] // 2
    ffs = ff // n_ctx
    ff_rows = w_down.shape[0]
    ratio = n_ctx // n_fsdp

    x_own = tokens[0]
    gains = jnp.pad(jnp.stack([norm1_gain, norm2_gain]), ((0, 6), (0, 0)))
    wg_own = jnp.concatenate(
        [
            lax.dynamic_slice(w_gate_up, (0, me * ffs), (kr, ffs)),
            lax.dynamic_slice(w_gate_up, (0, ff + me * ffs), (kr, ffs)),
        ],
        -1,
    ).astype(bf16)
    first_x, wg_own = lax.optimization_barrier((x_own, wg_own))
    x_all, wo_own, down_own, gains = gather_first(
        first_x, w_out, w_down, gains, n_ctx, ratio, ffs, 0
    )
    x_all = x_all.reshape(all_rows, width)

    qkv_own = jnp.concatenate(
        [lax.dynamic_slice(w_qkv, (0, i * width + me * hw), (kr, hw)) for i in range(3)], -1
    )
    wq = lax.all_gather(qkv_own.astype(bf16), "fsdp", axis=0, tiled=True)
    gain_one = gains[:, 0].reshape(width).astype(bf16).astype(f32)
    gain_two = gains[:, 1].reshape(width).astype(bf16).astype(f32)
    wgu = lax.all_gather(wg_own, "fsdp", axis=0, tiled=True)
    wo_own, wgu = lax.optimization_barrier((wo_own, wgu))
    wo = lax.all_gather(wo_own, "fsdp", axis=0, tiled=True)

    deal_table = deal[0]
    device_index = jnp.arange(n_ctx, dtype=jnp.int32)
    marks = (deal_table[:, :, None] == device_index[None, None, :]).astype(jnp.int32)
    source_piece = jnp.sum(marks * device_index[None, :, None], 1)
    dealt_from = (device_index[None, :] * n_ctx + source_piece.T).reshape(pieces)
    given_from = (deal_table * n_ctx + device_index[:, None]).reshape(pieces)
    own_dealt = lax.dynamic_slice(dealt_from, (me * n_ctx,), (n_ctx,))
    own_given = lax.dynamic_slice(given_from, (me * n_ctx,), (n_ctx,))
    places = jnp.arange(all_rows, dtype=jnp.int32)
    doc_lengths = lengths[0]
    ends = jnp.cumsum(doc_lengths)
    starts = ends - doc_lengths
    docs = jnp.sum((places[:, None] >= ends[None, :]).astype(jnp.int32), -1)
    doc_index = jnp.arange(doc_lengths.shape[0], dtype=jnp.int32)
    firsts = jnp.sum(jnp.where(docs[:, None] == doc_index[None, :], starts[None, :], 0), -1)
    within = places - firsts
    first_key = firsts[:, None]
    cosine_table, sine_table = rope_tables(within)

    x_float = x_all.astype(f32)
    normed_one = (x_float * rms_scale(x_float) * gain_one[None, :]).astype(bf16)
    order = (dealt_from[:, None] * piece + jnp.arange(piece, dtype=jnp.int32)).reshape(all_rows, 1)
    g_all, queries, keys, values, mixed_dealt, mixed_own = attend_gather(
        cotangent[0], normed_one, wq, cosine_table, sine_table, first_key, order, heads, n_ctx, 1
    )
    g_all = g_all.reshape(all_rows, width)
    mixed_own = mixed_own.transpose(1, 0, 2).reshape(rows, width)
    mixed_dealt = mixed_dealt.reshape(all_rows, hw)

    x_dealt = jnp.take(x_all.reshape(pieces, piece, width), own_dealt, axis=0)
    hidden = x_dealt.reshape(rows, width).astype(f32) + dot(mixed_own, wo, NN)
    scale_two = rms_scale(hidden)
    normed_two = (hidden * scale_two * gain_two[None, :]).astype(bf16)
    n2_all, wd, activated, d_both = feed_gather(normed_two, down_own, wgu, g_all.reshape(n_ctx, rows, width), n_ctx, 2)
    n2_all = n2_all.reshape(all_rows, width)
    if n_ctx == 8:
        arrays = [activated, wd, d_both, wgu, n2_all, g_all]
        down_rows, d_two, grad_gate_up, grad_down = reduce_ctx(
            arrays, ((0, 1, False), (2, 3, True)), ((4, 2), (0, 5)), n_ctx, 4
        )
    else:
        down_rows, grad_down = reduce_ctx(
            [activated, wd, g_all], ((0, 1, False),), ((0, 2),), n_ctx, 4
        )
        d_two, grad_gate_up = reduce_ctx(
            [d_both, wgu, n2_all], ((0, 1, True),), ((2, 0),), n_ctx, 5
        )
    d_two = d_two.astype(f32)
    block_out = (hidden + down_rows.astype(f32)).astype(bf16)[None]
    row_gate_up = lax.psum_scatter(grad_gate_up, "fsdp", scatter_dimension=0, tiled=True)

    grad_norm2 = jnp.sum(d_two * hidden * scale_two, 0)
    d_hidden = cotangent[0].astype(f32) + norm_back(d_two, hidden, scale_two, gain_two)
    d_branch = d_hidden.astype(bf16)
    db_all = gather_ctx([d_branch], n_ctx, 3)[0].reshape(all_rows, width)

    order_back = (given_from[:, None] * piece + jnp.arange(piece, dtype=jnp.int32)).reshape(
        all_rows, 1
    )
    all_gate_up, d_proj, grad_rows = back_gather(
        row_gate_up,
        db_all,
        wo,
        grad_down,
        queries,
        keys,
        values,
        mixed_dealt,
        cosine_table,
        sine_table,
        first_key,
        order_back,
        heads,
        n_ctx,
        7,
    )
    d_one, grad_qkv = reduce_ctx([d_proj, wq, normed_one], ((0, 1, True),), ((2, 0),), n_ctx, 6)
    d_one = d_one.astype(f32)
    row_qkv = lax.psum_scatter(grad_qkv, "fsdp", scatter_dimension=0, tiled=True)

    own_float = x_own.astype(f32)
    scale_one = rms_scale(own_float)
    grad_norm1 = jnp.sum(d_one * own_float * scale_one, 0)
    dh_own = jnp.take(db_all.reshape(pieces, piece, width), own_given, axis=0)
    dh_own = dh_own.reshape(rows, width).astype(f32)
    grad_tokens = (dh_own + norm_back(d_one, own_float, scale_one, gain_one)).astype(bf16)[None]

    norms = lax.psum_scatter(
        jnp.stack([grad_norm1, grad_norm2]), "fsdp", scatter_dimension=1, tiled=True
    )
    norms = jnp.pad(norms, ((0, 6), (0, 0)))

    col_rows = lax.psum_scatter(grad_rows, "fsdp", scatter_dimension=1, tiled=True)
    all_cols = gather_ctx([col_rows], n_ctx, 9)[0]
    owner_rows = all_cols.reshape(n_fsdp, ratio * (ffs + hw), width // n_fsdp)
    swapped = lax.all_to_all(owner_rows, "fsdp", split_axis=0, concat_axis=0, tiled=True)
    row_qkv, all_cols = lax.optimization_barrier((row_qkv, all_cols))
    all_qkv, all_norms = gather_ctx([row_qkv, norms], n_ctx, 8)
    final_gate_up = assemble(all_gate_up, 2)
    final_qkv = assemble(all_qkv, 3)
    final_norms = jnp.sum(all_norms, 0)
    final_down, final_out = assemble_rows(swapped, ratio, ffs)
    return (
        block_out,
        grad_tokens,
        final_norms[0],
        final_qkv,
        final_out,
        final_norms[1],
        final_gate_up,
        final_down,
    )


def solution(mesh):
    in_specs = (
        P("fsdp", "ctx", None),
        P("fsdp", "ctx", None),
        P("fsdp", None),
        P("fsdp", None, None),
        P("fsdp"),
        P("fsdp", None),
        P("fsdp", None),
        P("fsdp"),
        P("fsdp", None),
        P("fsdp", None),
    )
    out_specs = (
        P("fsdp", "ctx", None),
        P("fsdp", "ctx", None),
        P("fsdp"),
        P("fsdp", None),
        P("fsdp", None),
        P("fsdp"),
        P("fsdp", None),
        P("fsdp", None),
    )
    return jax.shard_map(shards, mesh=mesh, in_specs=in_specs, out_specs=out_specs, check_vma=False)
```

```python
import functools
import math

import jax
import jax.numpy as jnp
from jax import lax
from jax.experimental import pallas as pl
from jax.experimental.pallas import tpu as pltpu
from jax.sharding import PartitionSpec as P

MESH = pl.DeviceIdType.MESH
LINE = 4

H = 16
HD = 128

epsilon = 1e-06
rope_base = 10000.0
masked_score = -1e30
f32 = jnp.float32
bf16 = jnp.bfloat16


def greet(a, b, n_a, n_b, f, fsdp=False):
    bar = pltpu.get_barrier_semaphore()
    conds = ((a > 0, a - 1, b), (a < n_a - 1, a + 1, b), (b > 0, a, b - 1), (b < n_b - 1, a, b + 1))
    for cond, aa, bb in conds:

        @pl.when(cond)
        def _():
            pl.semaphore_signal(bar, inc=1, device_id=(aa * n_b + bb, f), device_id_type=MESH)

    low = (a + n_a - 1) // n_a + (b + n_b - 1) // n_b
    high = (2 * n_a - 2 - a) // n_a + (2 * n_b - 2 - b) // n_b
    total = low + high
    if fsdp:
        n_f = lax.axis_size("fsdp")
        for m in range(1, n_f):
            pl.semaphore_signal(
                bar, inc=1, device_id=(a * n_b + b, (f + m) % n_f), device_id_type=MESH
            )
        total = total + n_f - 1
    pl.semaphore_wait(bar, total)


def both(*conds):
    out = True
    for cond in conds:
        if cond is not True:
            out = cond if out is True else jnp.logical_and(out, cond)
    return out


def when(cond):
    return (lambda fn: fn()) if cond is True else pl.when(cond)


def plan(rows, cuts=2):
    unit = rows // 16
    if rows % 16 or unit < 4:
        return ((0, rows, False),)
    swapped = max(1, (unit + 4) // 8)
    rest = unit - swapped
    marks = [rest * i // cuts for i in range(cuts + 1)]
    chunks = [(16 * lo, 16 * (hi - lo), False) for lo, hi in zip(marks, marks[1:])]
    return tuple(chunks) + ((16 * rest, 16 * swapped, True),)


def places(n):
    n_a, n_b = LINE, n // LINE
    c = lax.axis_index("ctx")
    return n_a, n_b, c // n_b, c % n_b, lax.axis_index("fsdp")


def gather_steps(n, x, out, chunk, sems, late=None):
    n_a, n_b, a, b, f = places(n)
    first, count, swapped = chunk
    s1, r1, s2, r2 = sems
    (p1, n1), (p2, n2) = ((b, n_b), (a, n_a)) if swapped else ((a, n_a), (b, n_b))

    def slot(q1, q2):
        return q2 * n_b + q1 if swapped else q1 * n_b + q2

    rows = pl.ds(first, count)
    below1, above1, below2, above2 = p1 > 0, p1 < n1 - 1, p2 > 0, p2 < n2 - 1

    def copy1(k, d):
        q1 = p1 - k if d == 0 else p1 + k
        to = p1 + 1 if d == 0 else p1 - 1
        return pltpu.make_async_remote_copy(
            src_ref=x.at[rows] if k == 0 else out.at[slot(q1, p2), rows],
            dst_ref=out.at[slot(q1, p2), rows],
            send_sem=s1.at[d, k],
            recv_sem=r1.at[d, k],
            device_id=(slot(to, p2), f),
            device_id_type=MESH,
        )

    def copy2(j, q1, m, d):
        q2 = p2 - m if d == 0 else p2 + m
        to = p2 + 1 if d == 0 else p2 - 1
        return pltpu.make_async_remote_copy(
            src_ref=x.at[rows] if j == 0 and m == 0 else out.at[slot(q1, q2), rows],
            dst_ref=out.at[slot(q1, q2), rows],
            send_sem=s2.at[d, m, j],
            recv_sem=r2.at[d, m, j],
            device_id=(slot(p1, to), f),
            device_id_type=MESH,
        )

    shards = [(0, 0, None, p1, True)]
    for k in range(1, n1):
        shards.append((k, k, 0, p1 - k, p1 >= k))
        shards.append((n1 - 1 + k, k, 1, p1 + k, p1 + k < n1))

    def own():
        for d, cond in ((0, above1), (1, below1)):
            when(cond)(lambda d=d: copy1(0, d).start())
        for d, cond in ((0, above2), (1, below2)):
            when(cond)(lambda d=d: copy2(0, p1, 0, d).start())

    def line1(k):
        for j, kk, side, q1, there in shards:
            if kk != k:
                continue

            @when(there)
            def _():
                copy1(k - 1, side).wait_recv()
                if k < n1 - 1:
                    when(above1 if side == 0 else below1)(lambda: copy1(k, side).start())
                for d, cond in ((0, above2), (1, below2)):
                    when(cond)(lambda d=d: copy2(j, q1, 0, d).start())

    def arrive2(m, d, onward, j, q1):
        copy2(j, q1, m - 1, d).wait_recv()
        if m < n2 - 1:
            when(onward)(lambda: copy2(j, q1, m, d).start())

    def arrivals2(m):
        return [
            (both(there2, there), functools.partial(arrive2, m, d, onward, j, q1), m, d, k < 2)
            for j, k, _, q1, there in shards
            for d, there2, onward in ((0, p2 >= m, above2), (1, p2 + m < n2, below2))
        ]

    def line2(m):
        for cond, arrive, _, _, _ in arrivals2(m):
            when(cond)(arrive)

    if late is not None:
        for m in range(1, n2):
            late.extend(arrivals2(m))

    def finish():
        for j, k, side, q1, there in shards:
            for d, onward in ((0, above1), (1, below1)):
                if k < n1 - 1 and side in (None, d):
                    when(both(onward, there))(lambda d=d: copy1(k, d).wait_send())
            for m in range(n2 - 1):
                for d, onward, there2 in ((0, above2, p2 >= m), (1, below2, p2 + m < n2)):
                    when(both(onward, there, True if m == 0 else there2))(
                        lambda d=d, m=m: copy2(j, q1, m, d).wait_send()
                    )

    steps = [own]
    steps += [functools.partial(line1, k) for k in range(1, n1)]
    steps += [functools.partial(line2, m) for m in range(1, n2)]
    return steps, finish


def spread_steps(n, x, out, chunk, sems):
    f = lax.axis_index("fsdp")
    c = lax.axis_index("ctx")
    n_f = lax.axis_size("fsdp")
    n_y = n_f // 2
    y, core = f // 2, f % 2
    owner = c // (n // n_f)
    oy, oc = owner // 2, owner % 2
    first, count = chunk
    rows = pl.ds(first, count)
    up, down, side, come = sems

    def copy(own, sem, to):
        return pltpu.make_async_remote_copy(
            src_ref=x.at[rows] if own else out.at[rows],
            dst_ref=out.at[rows],
            send_sem=sem,
            recv_sem=come,
            device_id=(c, to),
            device_id_type=MESH,
        )

    on = core == oc
    ways = (
        (up, f + 2, jnp.logical_and(on, jnp.logical_and(y >= oy, y < n_y - 1))),
        (down, f - 2, jnp.logical_and(on, jnp.logical_and(y <= oy, y > 0))),
        (side, f + 1 - 2 * core, on),
    )

    def own():
        for sem, to, cond in ways:
            pl.when(jnp.logical_and(cond, f == owner))(lambda sem=sem, to=to: copy(True, sem, to).start())

    def onward():
        @pl.when(f != owner)
        def _():
            copy(False, side, f).wait_recv()
            for sem, to, cond in ways:
                pl.when(cond)(lambda sem=sem, to=to: copy(False, sem, to).start())

    def finish():
        for sem, to, cond in ways:
            pl.when(cond)(lambda sem=sem, to=to: copy(False, sem, to).wait_send())

    return own, onward, finish


def gather_sems(chunks):
    sem = pltpu.SemaphoreType.DMA
    return [sem((chunks, 2, 4)), sem((chunks, 2, 4)), sem((chunks, 2, 4, 7)), sem((chunks, 2, 4, 7))]


def gather_kernel(n, plans, spread, *refs):
    count = len(plans)
    k = count + (1 if spread else 0)
    xs, outs = refs[:k], refs[k : 2 * k]
    held = refs[2 * k : 3 * k]
    local, s1, r1, s2, r2, s3 = refs[3 * k :]
    n_a, n_b, a, b, f = places(n)
    c = a * n_b + b
    greet(a, b, n_a, n_b, f, bool(spread))
    steps, ends, at = [], [], 0
    for x, out, chunks in zip(xs, outs, plans):
        for chunk in chunks:
            sems = (s1.at[at], r1.at[at], s2.at[at], r2.at[at])
            more, end = gather_steps(n, x, out, chunk, sems)
            steps.append(more)
            ends.append(end)
            at += 1
    for i, chunk in enumerate(spread):
        begin, onward, end = spread_steps(n, xs[-1], outs[-1], chunk, [s3.at[i, j] for j in range(4)])
        steps.append([begin] + [lambda: None] * (1 + 2 * i) + [onward])
        ends.append(end)
    mine = f == c // (n // lax.axis_size("fsdp"))
    for t in range(max(map(len, steps))):
        for more in steps:
            if t < len(more):
                more[t]()
        if t < 2:
            for i in range(k):
                out = outs[i].at[c] if i < count else outs[i]

                @when(True if i < count else mine)
                def _():
                    fetch = pltpu.make_async_copy(xs[i], held[i], local.at[i])
                    if t == 0:
                        fetch.start()
                    else:
                        fetch.wait()
                        pltpu.make_async_copy(held[i], out, local.at[i]).start()
    for i in range(k):
        out = outs[i].at[c] if i < count else outs[i]
        when(True if i < count else mine)(pltpu.make_async_copy(held[i], out, local.at[i]).wait)
    for end in ends:
        end()


def gather_ctx(xs, n, cid, cuts=2, spread=None):
    plans = tuple(plan(x.shape[0], cuts) for x in xs)
    shapes = [jax.ShapeDtypeStruct((n,) + x.shape, x.dtype) for x in xs]
    parts = ()
    if spread is not None:
        rows = spread.shape[0]
        half = rows // 32 * 16
        parts = ((0, rows),) if rows % 16 else ((0, half), (half, rows - half))
        xs = xs + [spread]
        shapes = shapes + [jax.ShapeDtypeStruct(spread.shape, spread.dtype)]
    return pl.pallas_call(
        functools.partial(gather_kernel, n, plans, parts),
        out_shape=shapes,
        in_specs=[pl.BlockSpec(memory_space=pl.ANY)] * len(xs),
        out_specs=[pl.BlockSpec(memory_space=pl.ANY)] * len(xs),
        scratch_shapes=[pltpu.VMEM(x.shape, x.dtype) for x in xs]
        + [pltpu.SemaphoreType.DMA((len(xs),))]
        + gather_sems(sum(map(len, plans)))
        + [pltpu.SemaphoreType.DMA((2, 4))],
        compiler_params=pltpu.CompilerParams(
            collective_id=cid, has_side_effects=True, vmem_limit_bytes=60 << 20
        ),
        name=f"gather{cid}",
    )(*xs)


def cast_rows(src, dst):
    rows = src.shape[0]
    if rows % 16:
        dst[...] = src[...].astype(dst.dtype)
        return

    def one(i, carry):
        at = pl.ds(pl.multiple_of(i * 16, 16), 16)
        dst[at, :] = src[at, :].astype(dst.dtype)
        return carry

    lax.fori_loop(0, rows // 16, one, 0)


def first_kernel(n, chunks, ratio, *refs):
    x, wo, wd, g, wq, out, wo_out, wd_out, g_out, wq_out = refs[:10]
    held, wo_wide, wo_low, wd_wide, wd_low, g_held, wq_held, local = refs[10:18]
    s1, r1, s2, r2, gs, gr, ys, yr, cs, cr = refs[18:]
    n_a, n_b, a, b, f = places(n)
    c = a * n_b + b
    n_f = lax.axis_size("fsdp")
    ffs = wd_low.shape[0]
    own = pl.ds(pl.multiple_of((c % ratio) * ffs, 8), ffs)
    loads = [
        pltpu.make_async_copy(src, dst, local.at[i])
        for i, (src, dst) in enumerate(((x, held), (wo, wo_wide), (wd.at[own], wd_wide), (g, g_held), (wq, wq_held)))
    ]
    stores = [
        pltpu.make_async_copy(src, dst, local.at[i])
        for i, (src, dst) in enumerate(
            ((held, out.at[c]), (wo_low, wo_out), (wd_low, wd_out), (g_held, g_out.at[f]), (wq_held, wq_out.at[f]))
        )
    ]
    for copy in loads:
        copy.start()
    greet(a, b, n_a, n_b, f, True)
    steps, ends = [], []
    for i, chunk in enumerate(chunks):
        more, end = gather_steps(n, x, out, chunk, (s1.at[i], r1.at[i], s2.at[i], r2.at[i]))
        steps.append(more)
        ends.append(end)

    def gain(m):
        return pltpu.make_async_remote_copy(
            src_ref=g,
            dst_ref=g_out.at[f],
            send_sem=gs.at[m],
            recv_sem=gr.at[m],
            device_id=(c, (f + m) % n_f),
            device_id_type=MESH,
        )

    def along(m):
        return pltpu.make_async_remote_copy(
            src_ref=wq,
            dst_ref=wq_out.at[f],
            send_sem=ys.at[m],
            recv_sem=yr.at[m],
            device_id=(c, (f + 2 * m) % n_f),
            device_id_type=MESH,
        )

    def across(m):
        at = (f + n_f - 2 * m) % n_f
        return pltpu.make_async_remote_copy(
            src_ref=wq if m == 0 else wq_out.at[at],
            dst_ref=wq_out.at[at],
            send_sem=cs.at[m],
            recv_sem=cr.at[m],
            device_id=(c, f + 1 - 2 * (f % 2)),
            device_id_type=MESH,
        )

    for m in range(1, n_f // 2):
        along(m).start()
    across(0).start()
    for t in range(n_a + n_b - 1):
        for more in steps:
            if t < len(more):
                more[t]()
        if t == 2:
            for m in range(1, n_f // 2):
                along(m).wait_recv()
                across(m).start()
        if t == 0:
            for m in range(1, n_f):
                gain(m).start()
            loads[4].wait()
            stores[4].start()
            loads[0].wait()
            stores[0].start()
            loads[3].wait()
            stores[3].start()
            loads[1].wait()
            cast_rows(wo_wide, wo_low)
            stores[1].start()
        if t == 1:
            loads[2].wait()
            cast_rows(wd_wide, wd_low)
            stores[2].start()
    for copy in stores:
        copy.wait()
    for m in range(1, n_f):
        gain(m).wait()
    for m in range(n_f // 2):
        across(m).wait()
        if m:
            along(m).wait_send()
    for end in ends:
        end()


def gather_first(x, w_out, w_down, gains, wq, n, ratio, ffs, cid):
    n_f = lax.axis_size("fsdp")
    chunks = plan(x.shape[0])
    low = [jax.ShapeDtypeStruct(w_out.shape, bf16), jax.ShapeDtypeStruct((ffs, w_down.shape[1]), bf16)]
    sem = pltpu.SemaphoreType.DMA
    return pl.pallas_call(
        functools.partial(first_kernel, n, chunks, ratio),
        out_shape=[jax.ShapeDtypeStruct((n,) + x.shape, x.dtype)]
        + low
        + [jax.ShapeDtypeStruct((n_f,) + y.shape, y.dtype) for y in (gains, wq)],
        in_specs=[pl.BlockSpec(memory_space=pl.ANY)] * 5,
        out_specs=[pl.BlockSpec(memory_space=pl.ANY)] * 5,
        scratch_shapes=[
            pltpu.VMEM(x.shape, x.dtype),
            pltpu.VMEM(w_out.shape, f32),
            pltpu.VMEM(w_out.shape, bf16),
            pltpu.VMEM((ffs, w_down.shape[1]), f32),
            pltpu.VMEM((ffs, w_down.shape[1]), bf16),
            pltpu.VMEM(gains.shape, gains.dtype),
            pltpu.VMEM(wq.shape, wq.dtype),
            sem((5,)),
        ]
        + gather_sems(len(chunks))
        + [sem((n_f,))] * 6,
        compiler_params=pltpu.CompilerParams(
            collective_id=cid, has_side_effects=True, vmem_limit_bytes=60 << 20
        ),
        name=f"gather{cid}",
    )(x, w_out, w_down, gains, wq)


def attend_gather_kernel(n, chunks, heads, block, *refs):
    x, n_hbm, w_hbm, cos_ref, sin_ref, first_ref, order_ref = refs[:7]
    out, q_ref, k_ref, v_ref, dealt_ref, all_ref = refs[7:13]
    held, n_ref, w_ref, mixed, local, s1, r1, s2, r2, sa, ra = refs[13:]
    n_a, n_b, a, b, f = places(n)
    c = a * n_b + b
    all_rows = n_ref.shape[0]
    rows = all_rows // n
    hw = heads * HD
    loads = [
        pltpu.make_async_copy(src, dst, local.at[i])
        for i, (src, dst) in enumerate(((x, held), (n_hbm, n_ref), (w_hbm, w_ref)))
    ]
    for copy in loads:
        copy.start()
    bar = pltpu.get_barrier_semaphore()
    for m in range(1, n):
        pl.semaphore_signal(bar, inc=1, device_id=((c + m) % n, f), device_id_type=MESH)
    pl.semaphore_wait(bar, n - 1)
    steps, ends = [], []
    for i, chunk in enumerate(chunks):
        more, end = gather_steps(n, x, out, chunk, (s1.at[i], r1.at[i], s2.at[i], r2.at[i]))
        steps.append(more)
        ends.append(end)

    def run(t):
        for more in steps:
            if t < len(more):
                more[t]()

    def exchange(m):
        to = (c + m) % n
        return pltpu.make_async_remote_copy(
            src_ref=dealt_ref.at[to],
            dst_ref=all_ref.at[c],
            send_sem=sa.at[m],
            recv_sem=ra.at[m],
            device_id=(to, f),
            device_id_type=MESH,
        )

    def attend_block(at):
        own = slice(at, at + block)
        proj = dot(n_ref[own, :], w_ref[...], NN)
        cos, sin = cos_ref[own, :], sin_ref[own, :]
        for h in range(heads):
            head = slice(h * HD, (h + 1) * HD)
            for ref, base in ((q_ref, 0), (k_ref, hw)):
                u = proj[:, base + h * HD : base + (h + 1) * HD]
                ref[own, head] = (u * cos + turned(u) * sin).astype(bf16)
        v_ref[own, :] = proj[:, 2 * hw :].astype(bf16)
        for h in range(heads):
            head = slice(h * HD, (h + 1) * HD)
            seen = slice(0, at + block)
            probs = masked_probs(q_ref[own, head], k_ref[seen, head], first_ref[own, :], at)
            mixed[own, head] = dot(probs.astype(bf16), v_ref[seen, head], NN).astype(bf16)

    run(0)
    keep = pltpu.make_async_copy(held, out.at[c], local.at[0])
    loads[0].wait()
    keep.start()
    loads[1].wait()
    loads[2].wait()
    for at in range(0, all_rows, block):
        attend_block(at)
        if at + block == all_rows // 2:
            run(1)
    for m in range(n):
        own = slice(m * rows, (m + 1) * rows)
        given = lax.broadcasted_iota(jnp.int32, (rows, all_rows), 1)
        picks = jnp.where(given == order_ref[own, :], 1.0, 0.0).astype(bf16)
        dealt_ref[m] = dot(picks, mixed[...], NN).astype(bf16)
    for m in range(1, n):
        exchange(m).start()
    mine = pltpu.make_async_copy(dealt_ref.at[c], all_ref.at[c], local.at[1])
    mine.start()
    for t in range(2, n_a + n_b - 1):
        run(t)
    keep.wait()
    mine.wait()
    for m in range(1, n):
        exchange(m).wait()
    for end in ends:
        end()


def attend_gather(x, normed, wq, cos, sin, first, order, heads, n, cid, block=256):
    all_rows = normed.shape[0]
    rows = all_rows // n
    hw = heads * HD
    chunks = plan(x.shape[0])
    one = jax.ShapeDtypeStruct((all_rows, hw), bf16)
    split = jax.ShapeDtypeStruct((n, rows, hw), bf16)
    hbm = pl.BlockSpec(memory_space=pl.ANY)
    vmem = pl.BlockSpec(memory_space=pltpu.VMEM)
    sem = pltpu.SemaphoreType.DMA
    return pl.pallas_call(
        functools.partial(attend_gather_kernel, n, chunks, heads, block),
        out_shape=[jax.ShapeDtypeStruct((n,) + x.shape, x.dtype), one, one, one, split, split],
        in_specs=[hbm] * 3 + [vmem] * 4,
        out_specs=[hbm] + [vmem] * 4 + [hbm],
        scratch_shapes=[
            pltpu.VMEM(x.shape, x.dtype),
            pltpu.VMEM(normed.shape, bf16),
            pltpu.VMEM(wq.shape, bf16),
            pltpu.VMEM((all_rows, hw), bf16),
            sem((3,)),
        ]
        + gather_sems(len(chunks))
        + [sem((n,)), sem((n,))],
        compiler_params=pltpu.CompilerParams(
            collective_id=cid, has_side_effects=True, vmem_limit_bytes=60 << 20
        ),
        name=f"attend{cid}",
    )(x, normed, wq, cos, sin, first, order)


def back_gather_kernel(n, chunks, heads, block, *refs):
    x, db_hbm, wo_hbm, down_hbm, q_ref, k_ref, v_ref, mixed_ref = refs[:8]
    cos_ref, sin_ref, first_ref, order_ref = refs[8:12]
    out, proj_ref, rows_hbm = refs[12:15]
    held, db, wo, down, rows_ref, dealt, given, dk_ref, dv_ref, local, s1, r1, s2, r2 = refs[15:]
    n_a, n_b, a, b, f = places(n)
    c = a * n_b + b
    hw = heads * HD
    all_rows = db.shape[0]
    part = all_rows // n
    ffs = down.shape[0]
    own_rows = pl.ds(pl.multiple_of(c * hw, hw), hw)
    loads = [
        pltpu.make_async_copy(src, dst, local.at[i])
        for i, (src, dst) in enumerate(((x, held), (db_hbm, db), (wo_hbm.at[own_rows], wo), (down_hbm, down)))
    ]
    for copy in loads:
        copy.start()
    greet(a, b, n_a, n_b, f)
    steps, ends = [], []
    for i, chunk in enumerate(chunks):
        more, end = gather_steps(n, x, out, chunk, (s1.at[i], r1.at[i], s2.at[i], r2.at[i]))
        steps.append(more)
        ends.append(end)

    def run(t):
        for more in steps:
            if t < len(more):
                more[t]()

    run(0)
    keep = pltpu.make_async_copy(held, out.at[c], local.at[0])
    loads[0].wait()
    keep.start()
    for copy in loads[1:]:
        copy.wait()
    dealt[...] = dot(db[...], wo[...], NT).astype(bf16)
    for m in range(n):
        own = slice(m * part, (m + 1) * part)
        slots = lax.broadcasted_iota(jnp.int32, (part, all_rows), 1)
        picks = jnp.where(slots == order_ref[own, :], 1.0, 0.0).astype(bf16)
        given[own, :] = dot(picks, dealt[...], NN).astype(bf16)
    rows_ref[:ffs, :] = down[...]
    rows_ref[ffs:, :] = dot(mixed_ref[...], db[...], TN).astype(bf16)
    stored = pltpu.make_async_copy(rows_ref, rows_hbm, local.at[1])
    stored.start()
    attend_back_kernel(
        heads, block, q_ref, k_ref, v_ref, given, cos_ref, sin_ref, first_ref, proj_ref, dk_ref, dv_ref
    )
    for t in range(1, n_a + n_b - 1):
        run(t)
    keep.wait()
    stored.wait()
    for end in ends:
        end()


def back_gather(x, db, wo, down, q, k, v, mixed, cos, sin, first, order, heads, n, cid, block=256):
    all_rows, width = db.shape
    hw = heads * HD
    chunks = plan(x.shape[0])
    hbm = pl.BlockSpec(memory_space=pl.ANY)
    vmem = pl.BlockSpec(memory_space=pltpu.VMEM)
    both_rows = (down.shape[0] + hw, width)
    return pl.pallas_call(
        functools.partial(back_gather_kernel, n, chunks, heads, block),
        out_shape=[
            jax.ShapeDtypeStruct((n,) + x.shape, x.dtype),
            jax.ShapeDtypeStruct((all_rows, 3 * hw), bf16),
            jax.ShapeDtypeStruct(both_rows, bf16),
        ],
        in_specs=[hbm] * 4 + [vmem] * 8,
        out_specs=[hbm, vmem, hbm],
        scratch_shapes=[
            pltpu.VMEM(x.shape, x.dtype),
            pltpu.VMEM(db.shape, bf16),
            pltpu.VMEM((hw, width), bf16),
            pltpu.VMEM(down.shape, bf16),
            pltpu.VMEM(both_rows, bf16),
            pltpu.VMEM((all_rows, hw), bf16),
            pltpu.VMEM((all_rows, hw), bf16),
            pltpu.VMEM((all_rows, HD), f32),
            pltpu.VMEM((all_rows, HD), f32),
            pltpu.SemaphoreType.DMA((4,)),
        ]
        + gather_sems(len(chunks)),
        compiler_params=pltpu.CompilerParams(
            collective_id=cid, has_side_effects=True, vmem_limit_bytes=60 << 20
        ),
        name=f"back{cid}",
    )(x, db, wo, down, q, k, v, mixed, cos, sin, first, order)


def feed_kernel(n, chunks, halves, *refs):
    x, down, w_hbm, g_hbm = refs[:4]
    out, wd_out, act_ref, back_ref = refs[4:8]
    held, down_held, shard, w, g, wd, pre, local, gsem, s1, r1, s2, r2, s3 = refs[8:]
    n_a, n_b, a, b, f = places(n)
    c = a * n_b + b
    rows = x.shape[0]
    pair = 2 * rows
    ffs = wd.shape[0]
    h = a // 2
    mine = f == c // (n // lax.axis_size("fsdp"))
    loads = [
        pltpu.make_async_copy(src, dst, local.at[i])
        for i, (src, dst) in enumerate(((x, held), (w_hbm, w), (down, down_held)))
    ]
    loads += [
        pltpu.make_async_copy(
            g_hbm.at[q * n_b + p], g.at[pl.ds((p * n_a + q) * rows, rows)], gsem.at[q * n_b + p]
        )
        for q in range(n_a)
        for p in range(n_b)
    ]
    for copy in loads:
        copy.start()
    greet(a, b, n_a, n_b, f, True)
    steps, parts, ends = [], [], []
    for i, chunk in enumerate(chunks):
        late = []
        more, end = gather_steps(n, x, out, chunk, (s1.at[i], r1.at[i], s2.at[i], r2.at[i]), late)
        steps.append(more)
        parts.append(late)
        ends.append(end)
    spread = [
        spread_steps(n, down, wd_out, half, [s3.at[i, j] for j in range(4)])
        for i, half in enumerate(halves)
    ]

    def forward(p, half, buf):
        fetches = [
            pltpu.make_async_copy(
                out.at[(2 * half + i) * n_b + p], shard.at[pl.ds(i * rows, rows)], local.at[3 + i]
            )
            for i in (0, 1)
        ]
        for copy in fetches:
            copy.start()
        for copy in fetches:
            copy.wait()
        pre[buf] = dot(shard[...], w[...], NN)

    def backward(p, half, buf):
        gate, up = pre[buf, :, :ffs], pre[buf, :, ffs:]
        sigma = jax.nn.sigmoid(gate)
        gate_act = gate * sigma
        at = pl.multiple_of((p * n_a + 2 * half) * rows, pair)
        d_act = dot(g[pl.ds(at, pair), :], wd[...], NT)
        act = (gate_act * up).astype(bf16)
        d_gate = (d_act * up * sigma * (1.0 + gate * (1.0 - sigma))).astype(bf16)
        d_up = (d_act * gate_act).astype(bf16)
        for i in (0, 1):
            to = pl.ds(pl.multiple_of(((2 * half + i) * n_b + p) * rows, rows), rows)
            own = slice(i * rows, (i + 1) * rows)
            act_ref[to, :] = act[own]
            back_ref[to, :ffs] = d_gate[own]
            back_ref[to, ffs:] = d_up[own]

    for more in steps:
        more[0]()
    for begin, _, _ in spread:
        begin()
    loads[0].wait()
    keep = pltpu.make_async_copy(held, out.at[c], local.at[0])
    keep.start()
    loads[2].wait()
    keep_down = pltpu.make_async_copy(down_held, wd_out, local.at[2])
    pl.when(mine)(keep_down.start)
    loads[1].wait()
    keep.wait()
    for k in range(1, n_a):
        for more in steps:
            more[k]()
        if k == 1:
            forward(b, h, 0)
    forward(b, 1 - h, 1)
    for _, onward, _ in spread:
        onward()
    pl.when(mine)(keep_down.wait)
    fetch = pltpu.make_async_copy(wd_out, wd, local.at[5])
    fetch.start()
    fetch.wait()
    for copy in loads[3:]:
        copy.wait()
    backward(b, h, 0)
    backward(b, 1 - h, 1)
    for m in range(1, n_b):
        for d, p, there in ((0, b - m, b >= m), (1, b + m, b + m < n_b)):
            for half, near in ((h, True), (1 - h, False)):
                for late in zip(*parts):
                    if late[0][2:] == (m, d, near):
                        for cond, arrive, _, _, _ in late:
                            pl.when(cond)(arrive)

                @pl.when(there)
                def _():
                    forward(p, half, 0)
                    backward(p, half, 0)

    for _, _, end in spread:
        end()
    for end in ends:
        end()


def feed_gather(x, down, wgu, g, n, cid):
    rows, width = x.shape
    ffs = down.shape[0]
    half = rows // 2
    chunks = ((0, half, False), (half, half, False))
    cut = ffs // 32 * 16
    halves = ((0, ffs),) if ffs % 16 else ((0, cut), (cut, ffs - cut))
    hbm = pl.BlockSpec(memory_space=pl.ANY)
    vmem = pl.BlockSpec(memory_space=pltpu.VMEM)
    return pl.pallas_call(
        functools.partial(feed_kernel, n, chunks, halves),
        out_shape=[
            jax.ShapeDtypeStruct((n, rows, width), bf16),
            jax.ShapeDtypeStruct((ffs, width), bf16),
            jax.ShapeDtypeStruct((n * rows, ffs), bf16),
            jax.ShapeDtypeStruct((n * rows, 2 * ffs), bf16),
        ],
        in_specs=[hbm] * 4,
        out_specs=[hbm, hbm, vmem, vmem],
        scratch_shapes=[
            pltpu.VMEM((rows, width), bf16),
            pltpu.VMEM((ffs, width), bf16),
            pltpu.VMEM((2 * rows, width), bf16),
            pltpu.VMEM(wgu.shape, bf16),
            pltpu.VMEM((n * rows, width), bf16),
            pltpu.VMEM((ffs, width), bf16),
            pltpu.VMEM((2, 2 * rows, 2 * ffs), f32),
            pltpu.SemaphoreType.DMA((6,)),
            pltpu.SemaphoreType.DMA((n,)),
        ]
        + gather_sems(len(chunks))
        + [pltpu.SemaphoreType.DMA((2, 4))],
        compiler_params=pltpu.CompilerParams(
            collective_id=cid, has_side_effects=True, vmem_limit_bytes=60 << 20
        ),
        name=f"feed{cid}",
    )(x, down, wgu, g)


def order_of(p, n):
    if n == 2:
        return (1 - p, p)
    h = p // 2
    return (3 - 3 * h, 2 - h, 1 - p + 4 * h, p)


def reduce_steps(n, part, chunk, bufs, sems):
    n_a, n_b, a, b, f = places(n)
    first, count, swapped = chunk
    g1, g2 = bufs
    s1, r1, s2, r2 = sems
    (p1, n1), (p2, n2) = ((a, n_a), (b, n_b)) if swapped else ((b, n_b), (a, n_a))

    def slot(q1, q2):
        return q1 * n_b + q2 if swapped else q2 * n_b + q1

    rows = pl.ds(first, count)
    from1 = (p1 > 0, p1 < n1 - 1)
    from2 = (p2 > 0, p2 < n2 - 1)
    targets = order_of(p2, n2)

    def has1(d, k):
        return (p1 + k < n1) if d == 0 else (p1 >= k)

    def add(t, got):
        mine = part.at[t, rows]
        mine[...] = (mine[...].astype(f32) + got[...].astype(f32)).astype(mine.dtype)

    def remote(src, dst, send, recv, to):
        return pltpu.make_async_remote_copy(
            src_ref=src, dst_ref=dst, send_sem=send, recv_sem=recv, device_id=(to, f), device_id_type=MESH
        )

    def side1(d):
        return d if n1 > 2 else 0

    def copy1(j, d, k):
        t = p1 + k if d == 0 else p1 - k
        to = p1 + 1 if d == 0 else p1 - 1
        src = part.at[slot(t, targets[j]), rows]
        return remote(src, g1.at[side1(d), k - 1, j], s1.at[d, k, j], r1.at[d, k - 1, j], slot(to, p2))

    def come1(j, d, k):
        src = part.at[slot(p1, p2), rows]
        return remote(src, g1.at[side1(d), k, j], s1.at[d, k, j], r1.at[d, k, j], slot(p1, p2))

    def copy2(t, d):
        k = t - p2 if d == 0 else p2 - t
        to = p2 + 1 if d == 0 else p2 - 1
        return remote(
            part.at[slot(p1, t), rows], g2.at[d, k - 1], s2.at[d, k], r2.at[d, k - 1], slot(p1, to)
        )

    def come2(d, k):
        src = part.at[slot(p1, p2), rows]
        return remote(src, g2.at[d, k], s2.at[d, k], r2.at[d, k], slot(p1, p2))

    def start(j):
        for d in (0, 1) if j < n2 else ():
            for k in range(n1 - 1, 0, -1):
                when(both(has1(d, k), jnp.logical_not(from1[d])))(
                    lambda d=d, k=k: copy1(j, d, k).start()
                )

    def middle1(j, k):
        for d in (0, 1):

            @when(both(has1(d, k), from1[d]))
            def _():
                come1(j, d, k).wait_recv()
                add(slot(p1 + k if d == 0 else p1 - k, targets[j]), g1.at[side1(d), k, j])
                copy1(j, d, k).start()

    def last1(j):
        for d in (0, 1):

            @when(from1[d])
            def _():
                come1(j, d, 0).wait_recv()
                add(slot(p1, targets[j]), g1.at[side1(d), 0, j])

    def line2(j):
        t = targets[j]
        for d in (0, 1):

            @when((t > p2) if d == 0 else (t < p2))
            def _():
                @when(from2[d])
                def _():
                    k = t - p2 if d == 0 else p2 - t
                    come2(d, k).wait_recv()
                    add(slot(p1, t), g2.at[d, k])

                copy2(t, d).start()

    def last2():
        for d in (0, 1):

            @when(from2[d])
            def _():
                come2(d, 0).wait_recv()
                add(slot(p1, p2), g2.at[d, 0])

    steps = []
    if swapped:
        for k in range(n1 - 2, 0, -1):
            steps.append(lambda k=k: [middle1(j, k) for j in range(n2)])
        steps.append(lambda: [(last1(j), line2(j) if j < n2 - 1 else None) for j in range(n2)])
        steps.append(last2)
    else:

        def item(j):
            for k in range(n1 - 2, 0, -1):
                middle1(j, k)
            last1(j)
            if j < n2 - 1:
                line2(j)

        steps += [functools.partial(item, j) for j in range(n2)] + [last2]

    def finish():
        for j in range(n2):
            for d in (0, 1):
                for k in range(n1 - 1, 0, -1):
                    when(has1(d, k))(lambda j=j, d=d, k=k: copy1(j, d, k).wait_send())
                if j < n2 - 1:
                    t = targets[j]
                    when((t > p2) if d == 0 else (t < p2))(lambda t=t, d=d: copy2(t, d).wait_send())

    return start, steps, finish


def reduce_kernel(n, chunks, jobs, extras, count, *refs):
    n_a, n_b, a, b, f = places(n)
    k, e = len(jobs), len(extras)
    hbm, rest = refs[:count], refs[count:]
    o_refs, p_refs, rest = rest[:k], rest[k : k + e], rest[k + e :]
    held, parts, made, rest = rest[:count], rest[count : count + k], rest[count + k : count + k + e], rest[count + k + e :]
    cuts = len(chunks)
    bufs, rest = rest[: 2 * k * cuts], rest[2 * k * cuts :]
    load, stored, s1, r1, s2, r2 = rest
    rows = o_refs[0].shape[0]
    first = sorted({i for x, w, _ in jobs for i in (x, w)})
    order_in = first + [i for i in range(count) if i not in first]
    loads = [pltpu.make_async_copy(hbm[i], held[i], load.at[i]) for i in range(count)]
    for i in order_in:
        loads[i].start()
    todo = []
    for i in range(k):
        for m, chunk in enumerate(chunks):
            at = i * cuts + m
            sems = (s1.at[at], r1.at[at], s2.at[at], r2.at[at])
            todo.append(reduce_steps(n, parts[i], chunk, bufs[2 * at : 2 * at + 2], sems))

    def term(i, t):
        x, w, nt = jobs[i]
        at = pl.multiple_of(t * rows, rows)
        parts[i][t] = dot(held[x][pl.ds(at, rows), :], held[w][...], NT if nt else NN).astype(bf16)

    tiles, stores = [], []
    for i, (x, y) in enumerate(extras):
        high = held[x].shape[1]
        for lo in range(0, high, 256):
            hi = min(lo + 256, high)

            def tile(i=i, x=x, y=y, lo=lo, hi=hi):
                made[i][lo:hi, :] = dot(held[x][:, lo:hi], held[y][...], TN).astype(bf16)

            tiles.append(tile)
        stores.append((len(tiles), i))

    order = order_of(a, n_a)
    greet(a, b, n_a, n_b, f)
    for i in first:
        loads[i].wait()
    for j in range(n_a):
        for i in range(k):
            for m in range(1, n_b):
                term(i, order[j] * n_b + (b + m) % n_b)
            for start, _, _ in todo[i * cuts : (i + 1) * cuts]:
                start(j)
    for i in order_in[len(first) :]:
        loads[i].wait()
    done = 0
    for j in range(n_a):
        for i in range(k):
            term(i, order[j] * n_b + b)
        upto = len(tiles) * (j + 1) // n_a
        for at in range(done, upto):
            tiles[at]()
            for last, i in stores:
                if last == at + 1:
                    pltpu.make_async_copy(made[i], p_refs[i], stored.at[i]).start()
        done = upto
        for _, steps, _ in todo:
            steps[j]()
    for _, steps, _ in todo:
        steps[n_a]()
    for i in range(k):
        o_refs[i][...] = parts[i][a * n_b + b]
    for _, _, finish in todo:
        finish()
    for i in range(e):
        pltpu.make_async_copy(made[i], p_refs[i], stored.at[i]).wait()


def reduce_ctx(arrays, jobs, extras, n, cid):
    n_a, n_b = LINE, n // LINE
    rows = arrays[jobs[0][0]].shape[0] // n
    half = rows // 2
    chunks = ((0, half, False), (half, half, False))
    widths = [arrays[w].shape[0 if nt else 1] for _, w, nt in jobs]
    bufs = []
    for width in widths:
        for _, count, _ in chunks:
            bufs += [
                pltpu.VMEM((min(2, n_b - 1), n_b - 1, n_a, count, width), bf16),
                pltpu.VMEM((2, n_a - 1, count, width), bf16),
            ]
    made = [(arrays[x].shape[1], arrays[y].shape[1]) for x, y in extras]
    sem = pltpu.SemaphoreType.DMA
    k = len(jobs) * len(chunks)
    return pl.pallas_call(
        functools.partial(reduce_kernel, n, chunks, jobs, extras, len(arrays)),
        out_shape=[jax.ShapeDtypeStruct((rows, width), bf16) for width in widths]
        + [jax.ShapeDtypeStruct(shape, bf16) for shape in made],
        in_specs=[pl.BlockSpec(memory_space=pl.ANY)] * len(arrays),
        out_specs=[pl.BlockSpec(memory_space=pltpu.VMEM)] * len(widths)
        + [pl.BlockSpec(memory_space=pl.ANY)] * len(made),
        scratch_shapes=[pltpu.VMEM(x.shape, x.dtype) for x in arrays]
        + [pltpu.VMEM((n, rows, width), bf16) for width in widths]
        + [pltpu.VMEM(shape, bf16) for shape in made]
        + bufs
        + [sem((len(arrays),)), sem((max(1, len(made)),))]
        + [sem((k, 2, 4, 4)), sem((k, 2, 4, 4)), sem((k, 2, 4)), sem((k, 2, 4))],
        compiler_params=pltpu.CompilerParams(
            collective_id=cid, has_side_effects=True, vmem_limit_bytes=60 << 20
        ),
        name=f"reduce{cid}",
    )(*arrays)


def assemble_rows(parts, ratio, ffs):
    n, rows, w = parts.shape
    each = rows // ratio
    hw = each - ffs

    def body(i_ref, down_ref, out_ref):
        for j in range(ratio):
            down_ref[j * ffs : (j + 1) * ffs, :] = i_ref[0, j * each : j * each + ffs, :].astype(f32)
            out_ref[j * hw : (j + 1) * hw, :] = i_ref[0, j * each + ffs : (j + 1) * each, :].astype(f32)

    return pl.pallas_call(
        body,
        grid=(n,),
        out_shape=[
            jax.ShapeDtypeStruct((ratio * ffs, n * w), f32),
            jax.ShapeDtypeStruct((ratio * hw, n * w), f32),
        ],
        in_specs=[pl.BlockSpec((1, rows, w), lambda i: (i, 0, 0))],
        out_specs=[
            pl.BlockSpec((ratio * ffs, w), lambda i: (0, i)),
            pl.BlockSpec((ratio * hw, w), lambda i: (0, i)),
        ],
        compiler_params=pltpu.CompilerParams(vmem_limit_bytes=60 << 20),
        name="assemble_rows",
    )(parts)


def assemble(parts, n_groups, block=64):
    n, rows, gw = parts.shape
    w = gw // n_groups

    def body(i_ref, o_ref):
        for g in range(n_groups):
            for c in range(n):
                o_ref[:, (g * n + c) * w:(g * n + c + 1) * w] = i_ref[c, :, g * w:(g + 1) * w].astype(jnp.float32)

    return pl.pallas_call(
        body, grid=(rows // block,),
        out_shape=jax.ShapeDtypeStruct((rows, n * gw), jnp.float32),
        in_specs=[pl.BlockSpec((n, block, gw), lambda i: (0, i, 0))],
        out_specs=pl.BlockSpec((block, n * gw), lambda i: (i, 0)),
        compiler_params=pltpu.CompilerParams(vmem_limit_bytes=60 << 20),
        name="assemble")(parts)


def dot(a, b, dims):
    return lax.dot_general(a, b, (dims, ((), ())), preferred_element_type=f32)


NN = ((1,), (0,))
NT = ((1,), (1,))
TN = ((0,), (0,))


def turned(u):
    return pltpu.roll(u, HD // 2, 1)


def masked_probs(q, k, first, at):
    logits = dot(q, k, NT) * (1.0 / math.sqrt(HD))
    keys = lax.broadcasted_iota(jnp.int32, logits.shape, 1)
    queries = lax.broadcasted_iota(jnp.int32, logits.shape, 0) + at
    scaled = jnp.where((keys <= queries) & (keys >= first), logits, masked_score)
    raised = jnp.exp(scaled - jnp.max(scaled, -1, keepdims=True))
    return raised / jnp.sum(raised, -1, keepdims=True)


def attend_back_kernel(
    heads, block, q_ref, k_ref, v_ref, d_ref, cos_ref, sin_ref, first_ref, o_ref, dk_ref, dv_ref
):
    rows = q_ref.shape[0]
    hw = heads * HD

    def back(w, own):
        return (w * cos_ref[own, :] - turned(w) * sin_ref[own, :]).astype(bf16)

    for h in range(heads):
        head = slice(h * HD, (h + 1) * HD)
        for at in reversed(range(0, rows, block)):
            own = slice(at, at + block)
            seen = slice(0, at + block)
            q, k, v, d = q_ref[own, head], k_ref[seen, head], v_ref[seen, head], d_ref[own, head]
            probs = masked_probs(q, k, first_ref[own, :], at)
            d_probs = dot(d, v, NT)
            inner = jnp.sum(probs * d_probs, -1, keepdims=True)
            d_scores = (probs * (d_probs - inner) * (1.0 / math.sqrt(HD))).astype(bf16)
            o_ref[own, head] = back(dot(d_scores, k, NN), own)
            dk = dot(d_scores, q, TN)
            dv = dot(probs.astype(bf16), d, TN)
            if at + block == rows:
                dk_ref[...] = dk
                dv_ref[...] = dv
            else:
                dk_ref[seen, :] += dk
                dv_ref[seen, :] += dv
        every = slice(0, rows)
        o_ref[:, hw + h * HD : hw + (h + 1) * HD] = back(dk_ref[...], every)
        o_ref[:, 2 * hw + h * HD : 2 * hw + (h + 1) * HD] = dv_ref[...].astype(bf16)


def rope_tables(within):
    freq_index = jnp.arange(HD // 2, dtype=f32)
    inverse = rope_base ** (-2.0 * freq_index / HD)
    angles = within.astype(f32)[:, None] * inverse[None, :]
    cos, sin = jnp.cos(angles), jnp.sin(angles)
    return jnp.concatenate([cos, cos], -1), jnp.concatenate([-sin, sin], -1)


def rms_scale(values):
    return lax.rsqrt(jnp.mean(values * values, -1, keepdims=True) + epsilon)


def norm_back(grad_norm, values, scale_rows, gain_float):
    scaled = grad_norm * gain_float[None, :]
    cubed = scale_rows * scale_rows * scale_rows
    return scale_rows * scaled - values * cubed * jnp.mean(scaled * values, -1, keepdims=True)


def shards(
    tokens, cotangent, lengths, deal, norm1_gain, w_qkv, w_out, norm2_gain, w_gate_up, w_down
):
    n_ctx = lax.axis_size("ctx")
    n_fsdp = lax.axis_size("fsdp")
    me = lax.axis_index("ctx")
    mine = lax.axis_index("fsdp")
    rows = tokens.shape[1]
    width = tokens.shape[2]
    piece = rows // n_ctx
    all_rows = rows * n_ctx
    pieces = all_rows // piece
    heads = H // n_ctx
    hw = heads * HD
    kr = w_qkv.shape[0]
    ff = w_gate_up.shape[1] // 2
    ffs = ff // n_ctx
    ff_rows = w_down.shape[0]
    ratio = n_ctx // n_fsdp

    x_own = tokens[0]
    gains = jnp.pad(jnp.stack([norm1_gain, norm2_gain]), ((0, 6), (0, 0)))
    qkv_own = jnp.concatenate(
        [lax.dynamic_slice(w_qkv, (0, i * width + me * hw), (kr, hw)) for i in range(3)], -1
    )
    wg_own = jnp.concatenate(
        [
            lax.dynamic_slice(w_gate_up, (0, me * ffs), (kr, ffs)),
            lax.dynamic_slice(w_gate_up, (0, ff + me * ffs), (kr, ffs)),
        ],
        -1,
    ).astype(bf16)
    first_x, wg_own = lax.optimization_barrier((x_own, wg_own))
    x_all, wo_own, down_own, gains, wq = gather_first(
        first_x, w_out, w_down, gains, qkv_own.astype(bf16), n_ctx, ratio, ffs, 0
    )
    x_all = x_all.reshape(all_rows, width)
    wq = wq.reshape(width, 3 * hw)

    gain_one = gains[:, 0].reshape(width).astype(bf16).astype(f32)
    gain_two = gains[:, 1].reshape(width).astype(bf16).astype(f32)
    wgu = lax.all_gather(wg_own, "fsdp", axis=0, tiled=True)
    wo_own, wgu = lax.optimization_barrier((wo_own, wgu))
    wo = lax.all_gather(wo_own, "fsdp", axis=0, tiled=True)

    deal_table = deal[0]
    device_index = jnp.arange(n_ctx, dtype=jnp.int32)
    marks = (deal_table[:, :, None] == device_index[None, None, :]).astype(jnp.int32)
    source_piece = jnp.sum(marks * device_index[None, :, None], 1)
    dealt_from = (device_index[None, :] * n_ctx + source_piece.T).reshape(pieces)
    given_from = (deal_table * n_ctx + device_index[:, None]).reshape(pieces)
    own_dealt = lax.dynamic_slice(dealt_from, (me * n_ctx,), (n_ctx,))
    own_given = lax.dynamic_slice(given_from, (me * n_ctx,), (n_ctx,))
    places = jnp.arange(all_rows, dtype=jnp.int32)
    doc_lengths = lengths[0]
    ends = jnp.cumsum(doc_lengths)
    starts = ends - doc_lengths
    docs = jnp.sum((places[:, None] >= ends[None, :]).astype(jnp.int32), -1)
    doc_index = jnp.arange(doc_lengths.shape[0], dtype=jnp.int32)
    firsts = jnp.sum(jnp.where(docs[:, None] == doc_index[None, :], starts[None, :], 0), -1)
    within = places - firsts
    first_key = firsts[:, None]
    cosine_table, sine_table = rope_tables(within)

    x_float = x_all.astype(f32)
    normed_one = (x_float * rms_scale(x_float) * gain_one[None, :]).astype(bf16)
    order = (dealt_from[:, None] * piece + jnp.arange(piece, dtype=jnp.int32)).reshape(all_rows, 1)
    g_all, queries, keys, values, mixed_dealt, mixed_own = attend_gather(
        cotangent[0], normed_one, wq, cosine_table, sine_table, first_key, order, heads, n_ctx, 1
    )
    g_all = g_all.reshape(all_rows, width)
    mixed_own = mixed_own.transpose(1, 0, 2).reshape(rows, width)
    mixed_dealt = mixed_dealt.reshape(all_rows, hw)

    x_dealt = jnp.take(x_all.reshape(pieces, piece, width), own_dealt, axis=0)
    hidden = x_dealt.reshape(rows, width).astype(f32) + dot(mixed_own, wo, NN)
    scale_two = rms_scale(hidden)
    normed_two = (hidden * scale_two * gain_two[None, :]).astype(bf16)
    n2_all, wd, activated, d_both = feed_gather(normed_two, down_own, wgu, g_all.reshape(n_ctx, rows, width), n_ctx, 2)
    n2_all = n2_all.reshape(all_rows, width)
    if n_ctx == 8:
        arrays = [activated, wd, d_both, wgu, n2_all, g_all]
        down_rows, d_two, grad_gate_up, grad_down = reduce_ctx(
            arrays, ((0, 1, False), (2, 3, True)), ((4, 2), (0, 5)), n_ctx, 4
        )
    else:
        down_rows, grad_down = reduce_ctx(
            [activated, wd, g_all], ((0, 1, False),), ((0, 2),), n_ctx, 4
        )
        d_two, grad_gate_up = reduce_ctx(
            [d_both, wgu, n2_all], ((0, 1, True),), ((2, 0),), n_ctx, 5
        )
    d_two = d_two.astype(f32)
    block_out = (hidden + down_rows.astype(f32)).astype(bf16)[None]
    row_gate_up = lax.psum_scatter(grad_gate_up, "fsdp", scatter_dimension=0, tiled=True)

    grad_norm2 = jnp.sum(d_two * hidden * scale_two, 0)
    d_hidden = cotangent[0].astype(f32) + norm_back(d_two, hidden, scale_two, gain_two)
    d_branch = d_hidden.astype(bf16)
    db_all = gather_ctx([d_branch], n_ctx, 3)[0].reshape(all_rows, width)

    order_back = (given_from[:, None] * piece + jnp.arange(piece, dtype=jnp.int32)).reshape(
        all_rows, 1
    )
    all_gate_up, d_proj, grad_rows = back_gather(
        row_gate_up,
        db_all,
        wo,
        grad_down,
        queries,
        keys,
        values,
        mixed_dealt,
        cosine_table,
        sine_table,
        first_key,
        order_back,
        heads,
        n_ctx,
        7,
    )
    d_one, grad_qkv = reduce_ctx([d_proj, wq, normed_one], ((0, 1, True),), ((2, 0),), n_ctx, 6)
    d_one = d_one.astype(f32)
    row_qkv = lax.psum_scatter(grad_qkv, "fsdp", scatter_dimension=0, tiled=True)

    own_float = x_own.astype(f32)
    scale_one = rms_scale(own_float)
    grad_norm1 = jnp.sum(d_one * own_float * scale_one, 0)
    dh_own = jnp.take(db_all.reshape(pieces, piece, width), own_given, axis=0)
    dh_own = dh_own.reshape(rows, width).astype(f32)
    grad_tokens = (dh_own + norm_back(d_one, own_float, scale_one, gain_one)).astype(bf16)[None]

    norms = lax.psum_scatter(
        jnp.stack([grad_norm1, grad_norm2]), "fsdp", scatter_dimension=1, tiled=True
    )
    norms = jnp.pad(norms, ((0, 6), (0, 0)))

    col_rows = lax.psum_scatter(grad_rows, "fsdp", scatter_dimension=1, tiled=True)
    all_cols = gather_ctx([col_rows], n_ctx, 9)[0]
    owner_rows = all_cols.reshape(n_fsdp, ratio * (ffs + hw), width // n_fsdp)
    swapped = lax.all_to_all(owner_rows, "fsdp", split_axis=0, concat_axis=0, tiled=True)
    row_qkv, all_cols = lax.optimization_barrier((row_qkv, all_cols))
    all_qkv, all_norms = gather_ctx([row_qkv, norms], n_ctx, 8)
    final_gate_up = assemble(all_gate_up, 2)
    final_qkv = assemble(all_qkv, 3)
    final_norms = jnp.sum(all_norms, 0)
    final_down, final_out = assemble_rows(swapped, ratio, ffs)
    return (
        block_out,
        grad_tokens,
        final_norms[0],
        final_qkv,
        final_out,
        final_norms[1],
        final_gate_up,
        final_down,
    )


def solution(mesh):
    in_specs = (
        P("fsdp", "ctx", None),
        P("fsdp", "ctx", None),
        P("fsdp", None),
        P("fsdp", None, None),
        P("fsdp"),
        P("fsdp", None),
        P("fsdp", None),
        P("fsdp"),
        P("fsdp", None),
        P("fsdp", None),
    )
    out_specs = (
        P("fsdp", "ctx", None),
        P("fsdp", "ctx", None),
        P("fsdp"),
        P("fsdp", None),
        P("fsdp", None),
        P("fsdp"),
        P("fsdp", None),
        P("fsdp", None),
    )
    return jax.shard_map(shards, mesh=mesh, in_specs=in_specs, out_specs=out_specs, check_vma=False)
```
